256 devices in a mesh: enc: 2 (over y_lo), seq: 16 (over x, y_hi, core), tp: 8 (over z).
Axes of the slice: x: 4, y: 4 (y_hi: 2, y_lo: 2; y = y_hi * 2 + y_lo), z: 8, core: 2. Of those that a mesh axis runs over, the one named last changes fastest.
Arguments:
- x_res: bfloat16 [8192, 5120], P('seq', ('enc', 'tp')), may hold values from -6 to 6
- q_proj: bfloat16 [8192, 4096], P('seq', ('enc', 'tp')), may hold values from -40 to 40
- k_proj: bfloat16 [8192, 4096], P('seq', ('enc', 'tp')), may hold values from -40 to 40
- v_proj: bfloat16 [8192, 4096], P('seq', ('enc', 'tp')), may hold values from -6 to 6
- w_out: bfloat16 [4096, 5120], P(None, ('enc', 'tp')), may hold values from -0.09375 to 0.09375
- gate_table: float32 [50, 5120], P(None, ('enc', 'tp')), may hold values from 0.5 to 1.5
- timestep: int32 [1], replicated, may hold values from 0 to 49
- norm_gain: float32 [5120], replicated, may hold values from 0.5 to 1.5
- norm_bias: float32 [5120], replicated, may hold values from -3 to 3
- w_query: bfloat16 [5120, 4096], P(None, ('enc', 'tp')), may hold values from -1 to 1
- context: bfloat16 [512, 5120], P(('enc', 'seq')), may hold values from -6 to 6
- w_key: bfloat16 [5120, 4096], P(None, ('enc', 'tp')), may hold values from -1 to 1
- w_value: bfloat16 [5120, 4096], P(None, ('enc', 'tp')), may hold values from -0.078125 to 0.078125
- gain_cq: float32 [4096], P(('enc', 'tp')), may hold values from 1 to 2.5
- gain_ck: float32 [4096], P(('enc', 'tp')), may hold values from 1 to 2.5
- text_len: int32 [1], replicated, may hold values from 128 to 512
Outputs:
- mixed: bfloat16 [8192, 5120], P('seq', ('enc', 'tp'))
- cross_heads: bfloat16 [8192, 4096], P('seq', ('enc', 'tp'))
The draws below stay inside these ranges and needn't reach their ends.
All inputs are finite; a program needn't handle non-finite values.
Results may differ from the reference program's by a relative error of at most 0.025.
Values may be sent and summed in bfloat16 or wider, within the bound.
No kernel may reach another device: no remote copies, remote signals or barrier semaphores. Data moves between devices by JAX's collectives and lax.ppermute only.
A program may use at most 64 MiB of HBM per device.

```python
import jax
import jax.numpy as jnp
from jax import lax

D = 5120
HEAD_DIM = 128
DT = 5120
TEXT = 512
STEPS = 50
GRID_H = 45
GRID_W = 80
HEADS = 32
ATT = 4096
TOKENS = 8192


THETA = 10000.0


def token_angles(positions):
    frame = (positions // (GRID_H * GRID_W)).astype(jnp.float32)
    row_index = (positions // GRID_W % GRID_H).astype(jnp.float32)
    column = (positions % GRID_W).astype(jnp.float32)
    part_time = HEAD_DIM - 4 * (HEAD_DIM // 6)
    part_space = 2 * (HEAD_DIM // 6)
    freq_time = THETA ** (-jnp.arange(0, part_time, 2).astype(jnp.float32) / part_time)
    freq_space = THETA ** (-jnp.arange(0, part_space, 2).astype(jnp.float32) / part_space)
    return jnp.concatenate([frame[:, None] * freq_time[None, :], row_index[:, None] * freq_space[None, :], column[:, None] * freq_space[None, :]], axis=1)


def paired_keys(key, boost):
    noise = jax.random.normal(jax.random.fold_in(key, 5), (TOKENS, ATT), jnp.float32)
    keys = 2.0 * jnp.clip(noise, -6.0, 6.0)
    index = jnp.arange(TOKENS)
    chosen = index % 113 == 17
    factor = 1.0 + boost * (1.0 + 0.5 * (index // 113 % 3).astype(jnp.float32))
    keys = keys * jnp.where(chosen, factor, 1.0)[:, None]
    return (keys, chosen)


def shared_columns(key):
    leading = jax.random.randint(jax.random.fold_in(key, 61), (), 0, HEADS)
    trailing = (leading + 1 + jax.random.randint(jax.random.fold_in(key, 62), (), 0, HEADS - 1)) % HEADS
    signs = (2 * jax.random.randint(jax.random.fold_in(key, 63), (HEAD_DIM,), 0, 2) - 1).astype(jnp.float32)
    owner = jnp.arange(ATT) // HEAD_DIM
    picked = (owner == leading) | (owner == trailing)
    return jnp.where(picked, jnp.tile(signs, HEADS), 0.0)


def draw_k_proj(key, part):
    strength = 0.0
    keys, chosen = paired_keys(key, strength)
    return keys.astype(jnp.bfloat16)


def draw_q_proj(key, part):
    strength = 0.0
    keys, chosen = paired_keys(key, strength)
    key = jax.random.fold_in(key, 22)
    noise = 2.0 * jnp.clip(jax.random.normal(key, (TOKENS, ATT), jnp.float32), -6.0, 6.0)
    offset = TOKENS // 2
    partner = jnp.roll(keys, -offset, axis=0)
    partner_chosen = jnp.roll(chosen, -offset, axis=0)
    angles = token_angles(jnp.arange(TOKENS, dtype=jnp.int32))
    delta = (jnp.roll(angles, -offset, axis=0) - angles)[:, None, :]
    cosine = jnp.cos(delta)
    sine = jnp.sin(delta)
    pairs = partner.reshape(TOKENS, -1, HEAD_DIM // 2, 2)
    leading = pairs[..., 0]
    trailing = pairs[..., 1]
    turned = jnp.stack([leading * cosine - trailing * sine, leading * sine + trailing * cosine], axis=-1).reshape(TOKENS, ATT)
    result = jnp.where(partner_chosen[:, None], strength * turned + (1.0 - strength) * noise, noise)
    return jnp.clip(result, -40.0, 40.0).astype(jnp.bfloat16)


def draw_w_query(key, part):
    column = shared_columns(key)
    key = jax.random.fold_in(key, 41)
    strength = 0.0
    factor = D ** (-0.5)
    noise = jnp.clip(jax.random.normal(key, (D, ATT), jnp.float32), -6.0, 6.0) * factor
    direction = jnp.clip(jax.random.normal(jax.random.fold_in(key, 1), (D,), jnp.float32), -6.0, 6.0) * factor
    return jnp.clip(noise + strength * direction[:, None] * column[None, :], -1.0, 1.0).astype(jnp.bfloat16)


def draw_w_key(key, part):
    column = shared_columns(key)
    key = jax.random.fold_in(key, 42)
    strength = 0.0
    factor = DT ** (-0.5)
    noise = jnp.clip(jax.random.normal(key, (DT, ATT), jnp.float32), -6.0, 6.0) * factor
    direction = jnp.clip(jax.random.normal(jax.random.fold_in(key, 1), (DT,), jnp.float32), -6.0, 6.0) * factor
    return jnp.clip(noise + strength * direction[:, None] * column[None, :], -1.0, 1.0).astype(jnp.bfloat16)


def shard_levels(stream_key, extent, cuts, low, largest):
    level = 1.0
    for position, blocks in cuts:
        heights = jax.random.uniform(jax.random.fold_in(jax.random.fold_in(stream_key, 6), position), (blocks,), jnp.float32, low / len(cuts), largest / len(cuts))
        level = level * jnp.repeat(jnp.exp(heights), extent[position] // blocks).reshape((-1,) + (1,) * (len(extent) - 1 - position))
    return level


def centred(key, shape, spread, most, split=(), kind=jnp.bfloat16):
    values = jax.random.normal(key, shape, jnp.float32) * spread
    if len(split) > 0:
        values = shard_levels(key, shape, split, -0.22, 0.18) * values
    return jnp.clip(values, min=-most, max=most).astype(kind)


def setup_inputs(seed: int = 0) -> dict:
    seeds = jax.random.split(jax.random.key(seed), 17)
    x_res = centred(seeds[0], (TOKENS, D), 1.0, 6.0, ((0, 16), (1, 16)))
    q_proj = draw_q_proj(jax.random.fold_in(seeds[16], 71), 0)
    k_proj = draw_k_proj(jax.random.fold_in(seeds[16], 71), 0)
    v_proj = centred(seeds[3], (TOKENS, ATT), 1.0, 6.0, ((0, 16), (1, 16)))
    w_out = centred(seeds[4], (ATT, D), ATT ** -0.5, 0.09375, ((1, 16),))
    gate_table = jnp.clip(0.5 + 1.0 * jax.random.uniform(seeds[5], (STEPS, D), jnp.float32) ** shard_levels(seeds[5], (STEPS, D), ((1, 16),), -0.2, 0.2), 0.5, 1.5)
    timestep = jax.random.randint(seeds[6], (1,), 0, STEPS).astype(jnp.int32)
    norm_gain = jnp.clip(jax.random.uniform(seeds[7], (D,), jnp.float32, 0.5, 1.5), 0.5, 1.5)
    norm_bias = centred(seeds[8], (D,), 0.5, 3.0, (), jnp.float32)
    w_query = draw_w_query(jax.random.fold_in(seeds[16], 71), 0)
    context = centred(seeds[10], (TEXT, DT), 1.0, 6.0, ((0, 32),))
    w_key = draw_w_key(jax.random.fold_in(seeds[16], 71), 0)
    w_value = centred(seeds[12], (DT, ATT), DT ** -0.5, 0.078125, ((1, 16),))
    gain_cq = jnp.clip(1.0 + 1.5 * jax.random.uniform(seeds[13], (ATT,), jnp.float32) ** shard_levels(seeds[13], (ATT,), ((0, 16),), -0.2, 0.2), 1.0, 2.5)
    gain_ck = jnp.clip(1.0 + 1.5 * jax.random.uniform(seeds[14], (ATT,), jnp.float32) ** shard_levels(seeds[14], (ATT,), ((0, 16),), -0.2, 0.2), 1.0, 2.5)
    text_len = jax.random.randint(seeds[15], (1,), TEXT // 4, TEXT + 1).astype(jnp.int32)
    return dict(x_res=x_res, q_proj=q_proj, k_proj=k_proj, v_proj=v_proj, w_out=w_out, gate_table=gate_table, timestep=timestep, norm_gain=norm_gain, norm_bias=norm_bias, w_query=w_query, context=context, w_key=w_key, w_value=w_value, gain_cq=gain_cq, gain_ck=gain_ck, text_len=text_len)


EPS = 1e-06
THETA = 10000.0

def rope_angles(positions):
    frame = (positions // (GRID_H * GRID_W)).astype(jnp.float32)
    row = (positions // GRID_W % GRID_H).astype(jnp.float32)
    column = (positions % GRID_W).astype(jnp.float32)
    part_time = HEAD_DIM - 4 * (HEAD_DIM // 6)
    part_space = 2 * (HEAD_DIM // 6)
    freq_time = THETA ** (-jnp.arange(0, part_time, 2).astype(jnp.float32) / part_time)
    freq_space = THETA ** (-jnp.arange(0, part_space, 2).astype(jnp.float32) / part_space)
    return jnp.concatenate([frame[:, None] * freq_time[None, :], row[:, None] * freq_space[None, :], column[:, None] * freq_space[None, :]], axis=1)

def rotate(values, angles):
    count = values.shape[0]
    pairs = values.astype(jnp.float32).reshape(count, -1, HEAD_DIM // 2, 2)
    cosine = jnp.cos(angles)[:, None, :]
    sine = jnp.sin(angles)[:, None, :]
    first = pairs[..., 0]
    second = pairs[..., 1]
    turned = jnp.stack([first * cosine - second * sine, first * sine + second * cosine], axis=-1)
    return turned.reshape(values.shape).astype(jnp.bfloat16)

def reference(x_res, q_proj, k_proj, v_proj, w_out, gate_table, timestep, norm_gain, norm_bias, w_query, context, w_key, w_value, gain_cq, gain_ck, text_len):
    positions = jnp.arange(TOKENS, dtype=jnp.int32)
    angles = rope_angles(positions)
    queries = rotate(q_proj, angles)
    keys = rotate(k_proj, angles)
    scale = HEAD_DIM ** (-0.5)

    def self_head(head):
        begin = head * HEAD_DIM
        q_head = lax.dynamic_slice_in_dim(queries, begin, HEAD_DIM, 1)
        k_head = lax.dynamic_slice_in_dim(keys, begin, HEAD_DIM, 1)
        v_head = lax.dynamic_slice_in_dim(v_proj, begin, HEAD_DIM, 1)
        scores = jnp.dot(q_head, k_head.T, preferred_element_type=jnp.float32) * scale
        high = lax.optimization_barrier(jnp.max(scores, axis=1, keepdims=True))
        weights = jnp.exp(scores - high)
        total = lax.optimization_barrier(jnp.sum(weights, axis=1, keepdims=True))
        summed = jnp.dot(weights.astype(jnp.bfloat16), v_head, preferred_element_type=jnp.float32)
        return (summed / total).astype(jnp.bfloat16)
    heads_all = lax.map(self_head, jnp.arange(HEADS).astype(jnp.int32))
    self_heads = jnp.transpose(heads_all, (1, 0, 2)).reshape(TOKENS, ATT)
    branch = jnp.dot(self_heads, w_out, preferred_element_type=jnp.float32)
    gate = lax.dynamic_slice_in_dim(gate_table, timestep[0].astype(jnp.int32), 1, 0)
    mixed = (x_res.astype(jnp.float32) + gate * branch).astype(jnp.bfloat16)
    stream = mixed.astype(jnp.float32)
    mean = lax.optimization_barrier(jnp.mean(stream, axis=1, keepdims=True))
    meansq = lax.optimization_barrier(jnp.mean(stream * stream, axis=1, keepdims=True))
    normed = ((stream - mean) * lax.rsqrt(meansq - mean * mean + EPS) * norm_gain + norm_bias).astype(jnp.bfloat16)
    query_raw = jnp.dot(normed, w_query, preferred_element_type=jnp.float32)
    key_raw = jnp.dot(context, w_key, preferred_element_type=jnp.float32)
    values_text = jnp.dot(context, w_value, preferred_element_type=jnp.float32).astype(jnp.bfloat16)
    query_text = (query_raw * lax.rsqrt(lax.optimization_barrier(jnp.mean(query_raw * query_raw, axis=1, keepdims=True)) + EPS) * gain_cq).astype(jnp.bfloat16)
    keys_text = (key_raw * lax.rsqrt(lax.optimization_barrier(jnp.mean(key_raw * key_raw, axis=1, keepdims=True)) + EPS) * gain_ck).astype(jnp.bfloat16)
    live = (jnp.arange(TEXT, dtype=jnp.int32) < text_len[0])[None, :]

    def cross_head(head):
        begin = head * HEAD_DIM
        q_head = lax.dynamic_slice_in_dim(query_text, begin, HEAD_DIM, 1)
        k_head = lax.dynamic_slice_in_dim(keys_text, begin, HEAD_DIM, 1)
        v_head = lax.dynamic_slice_in_dim(values_text, begin, HEAD_DIM, 1)
        scores = jnp.dot(q_head, k_head.T, preferred_element_type=jnp.float32) * scale
        high = lax.optimization_barrier(jnp.max(jnp.where(live, scores, -1e+30), axis=1, keepdims=True))
        weights = jnp.exp(jnp.where(live, scores - high, -1e+30))
        total = lax.optimization_barrier(jnp.sum(weights, axis=1, keepdims=True))
        summed = jnp.dot(weights.astype(jnp.bfloat16), v_head, preferred_element_type=jnp.float32)
        return (summed / total).astype(jnp.bfloat16)
    cross_all = lax.map(cross_head, jnp.arange(HEADS).astype(jnp.int32))
    cross_heads = jnp.transpose(cross_all, (1, 0, 2)).reshape(TOKENS, ATT)
    return (mixed, cross_heads)
```

```python
import functools

import jax
import jax.numpy as jnp
import numpy as np
from jax import lax
from jax.experimental import pallas as pl
from jax.experimental.pallas import tpu as pltpu
from jax.sharding import Mesh, PartitionSpec as P

HEAD = 128
GRID_H = 45
GRID_W = 80
EPS = 1e-06
THETA = 10000.0
LOG2E = 1.4426950408889634
SCALE2 = LOG2E * HEAD**-0.5
BF = jnp.bfloat16
F32 = jnp.float32
NT = (((1,), (1,)), ((), ()))
VMEM_LIMIT = 56 * 1024 * 1024
PARAMS = pltpu.CompilerParams(vmem_limit_bytes=VMEM_LIMIT)


def frequencies():
    part_time = HEAD - 4 * (HEAD // 6)
    part_space = 2 * (HEAD // 6)
    time = THETA ** (-np.arange(0, part_time, 2).astype(np.float32) / part_time)
    space = THETA ** (-np.arange(0, part_space, 2).astype(np.float32) / part_space)
    pairs = np.concatenate([time, space, space]).astype(np.float32)
    return np.repeat(pairs, 2)[None, :]


def rope_kernel(place, q_ref, k_ref, v_ref, freq_ref, mine_ref, send_ref):
    rows = q_ref.shape[0]
    core = place[0]
    start = place[1] * 512 + pl.program_id(0) * rows
    shape = (rows, HEAD)
    position = (start + lax.broadcasted_iota(jnp.int32, shape, 0)).astype(F32)
    lane = lax.broadcasted_iota(jnp.int32, shape, 1)
    line = jnp.floor((position + 0.5) * (1.0 / GRID_W))
    column = position - line * GRID_W
    frame = jnp.floor((line + 0.5) * (1.0 / GRID_H))
    row = line - frame * GRID_H
    part_time = HEAD - 4 * (HEAD // 6)
    part_space = 2 * (HEAD // 6)
    axis = jnp.where(lane < part_time, frame, jnp.where(lane < part_time + part_space, row, column))
    angles = axis * freq_ref[...]
    even = lane % 2 == 0
    cosine = jnp.cos(angles)
    sine = jnp.sin(angles)
    sine = jnp.where(even, -sine, sine)
    for index, ref in enumerate((q_ref, k_ref, v_ref)):
        heads = []
        for head in range(2):
            x = ref[:, head * HEAD : (head + 1) * HEAD]
            if index < 2:
                x = x.astype(F32)
                other = jnp.where(even, pltpu.roll(x, HEAD - 1, 1), pltpu.roll(x, 1, 1))
                x = (x * cosine + other * sine).astype(BF)
            heads.append(x)
        first = core == 0
        mine_ref[index] = jnp.where(first, heads[0], heads[1])
        send_ref[index] = jnp.where(first, heads[1], heads[0])


def rope(place, q, k, v):
    rows = 256
    grid_spec = pltpu.PrefetchScalarGridSpec(
        num_scalar_prefetch=1,
        grid=(512 // rows,),
        in_specs=[pl.BlockSpec((rows, 256), lambda i, s: (i, 0))] * 3
        + [pl.BlockSpec((1, HEAD), lambda i, s: (0, 0))],
        out_specs=[pl.BlockSpec((3, rows, HEAD), lambda i, s: (0, i, 0))] * 2,
    )
    return pl.pallas_call(
        rope_kernel,
        grid_spec=grid_spec,
        out_shape=[jax.ShapeDtypeStruct((3, 512, HEAD), BF)] * 2,
        compiler_params=PARAMS,
        name="rope",
    )(place, q, k, v, frequencies())


def attend_kernel(count, first, last, place, *refs):
    q_ref, kvs = refs[0], refs[1 : 1 + count]
    refs = refs[1 + count :]
    if not first:
        acc_in, high_in = refs[:2]
        refs = refs[2:]
    if last:
        out_ref, wide = refs
    else:
        acc_out, high_out, wide = refs
    chunk = 512

    @pl.when(pl.program_id(0) == 0)
    def _():
        base = 0
        for kv in kvs:
            for i in range(kv.shape[0]):
                wide[pl.ds(base, chunk), :HEAD] = kv[i, 1]
                wide[pl.ds(base, chunk), HEAD:] = jnp.ones((chunk, HEAD), BF)
                base += chunk

    sub = 256
    for begin in range(0, q_ref.shape[0], sub):
        rows = pl.ds(begin, sub)
        q = q_ref[rows, :]
        scores = []
        for kv in kvs:
            for i in range(kv.shape[0]):
                scores.append(lax.dot_general(q, kv[i, 0], NT, preferred_element_type=F32))
        high = None
        for s in scores:
            for j in range(0, chunk, HEAD):
                part = s[:, j : j + HEAD]
                high = part if high is None else jnp.maximum(high, part)
        high = jnp.max(high, axis=1, keepdims=True)
        acc = None
        if not first:
            before = high_in[rows, :1]
            high = jnp.maximum(before, high)
            acc = acc_in[rows, :] * jnp.exp2((before - high) * SCALE2)
        shift = high * SCALE2
        for i, s in enumerate(scores):
            p = jnp.exp2(s * SCALE2 - shift).astype(BF)
            update = jnp.dot(p, wide[pl.ds(i * chunk, chunk), :], preferred_element_type=F32)
            acc = update if acc is None else acc + update
        if not last:
            acc_out[rows, :] = acc
            high_out[rows, :] = jnp.broadcast_to(high, (sub, HEAD))
        else:
            total = acc[:, HEAD:]
            block = begin // sub
            out_ref[block, :sub, :] = (acc[:, :HEAD] / total).astype(BF)
            logs = shift + jnp.log(total) * LOG2E
            rank = lax.broadcasted_iota(jnp.int32, (16, HEAD), 0)
            for half in range(sub // HEAD):
                line = jnp.transpose(logs[half * HEAD : (half + 1) * HEAD, :])[:16, :]
                one = line.astype(BF).astype(F32)
                two = (line - one).astype(BF).astype(F32)
                three = line - one - two
                packed = jnp.where(
                    rank == 0, one, jnp.where(rank == 1, two, jnp.where(rank == 2, three, 0.0))
                )
                out_ref[block, pl.ds(sub + 16 * half, 16), :] = packed.astype(BF)


def attend(place, q, kvs, state, last):
    total = q.shape[0]
    keys = sum(kv.shape[0] for kv in kvs) * 512
    rows = 512

    def row(width):
        return pl.BlockSpec((rows, width), lambda i, s: (i, 0))

    operands = [q, *kvs]
    specs = [row(HEAD)] + [pl.BlockSpec(kv.shape, lambda i, s: (0, 0, 0, 0)) for kv in kvs]
    if state is not None:
        operands += list(state)
        specs += [row(256), row(HEAD)]
    if last:
        out_specs = pl.BlockSpec(
            (2, 288, HEAD),
            lambda i, s: (((s[2] + i // 2) % 2) * 2 + (s[0] + i % 2) % 2, 0, 0),
        )
        out_shape = jax.ShapeDtypeStruct((8, 288, HEAD), BF)
    else:
        out_specs = [row(256), row(HEAD)]
        out_shape = [
            jax.ShapeDtypeStruct((total, 256), F32),
            jax.ShapeDtypeStruct((total, HEAD), F32),
        ]
    grid_spec = pltpu.PrefetchScalarGridSpec(
        num_scalar_prefetch=1,
        grid=(total // rows,),
        in_specs=specs,
        out_specs=out_specs,
        scratch_shapes=[pltpu.VMEM((keys, 256), BF)],
    )
    return pl.pallas_call(
        functools.partial(attend_kernel, len(kvs), state is None, last),
        grid_spec=grid_spec,
        out_shape=out_shape,
        compiler_params=PARAMS,
        cost_estimate=pl.CostEstimate(
            flops=8 * total * keys * HEAD, bytes_accessed=8 * 1024 * 1024, transcendentals=total * keys
        ),
        name="attend",
    )(place, *operands)


def merge_kernel(in_ref, out_ref):
    for head in range(4):
        enc, core = head // 2, head % 2
        sources = [half * 4 + core * 2 + enc for half in range(2)]
        for part in range(2):
            logs = []
            for source in sources:
                lines = in_ref[source, pl.ds(256 + 16 * part, 16), :].astype(F32)
                line = lines[0:1, :] + lines[1:2, :] + lines[2:3, :]
                logs.append(jnp.transpose(jnp.broadcast_to(line, (HEAD, HEAD))))
            rows = pl.ds(part * HEAD, HEAD)
            low = in_ref[sources[0], rows, :].astype(F32)
            up = in_ref[sources[1], rows, :].astype(F32)
            value = low / (1.0 + jnp.exp2(logs[1] - logs[0])) + up / (1.0 + jnp.exp2(logs[0] - logs[1]))
            out_ref[rows, head * HEAD : (head + 1) * HEAD] = value.astype(BF)


def merge(parts):
    return pl.pallas_call(
        merge_kernel,
        out_shape=jax.ShapeDtypeStruct((256, 512), BF),
        compiler_params=PARAMS,
        name="merge",
    )(parts)


def ring(value):
    half = value.shape[0] // 2
    up = [(i, (i + 1) % 8) for i in range(8)]
    down = [(i, (i - 1) % 8) for i in range(8)]
    pieces = [(value, 0, 0)]
    right = [value[:half], value[half:]]
    left = [value[:half], value[half:]]
    for step in range(1, 4):
        right = [lax.ppermute(a, "tp", up) for a in right]
        left = [lax.ppermute(a, "tp", down) for a in left]
        for i in range(2):
            pieces.append((right[i], -step, i * half))
            pieces.append((left[i], step, i * half))
    pieces.append((lax.ppermute(right[0], "tp", up), -4, 0))
    pieces.append((lax.ppermute(left[1], "tp", down), 4, half))
    return pieces


def mix_kernel(meta, place, *refs):
    count = len(meta)
    pieces = refs[:count]
    w_own, w_other, x_own, x_other, gate_own, gate_other, own_ref, other_ref, both_ref, heads, acc = refs[count:]
    step = pl.program_id(0)
    z = place[3]

    @pl.when(step == 0)
    def _():
        for ref, (shift, begin) in zip(pieces, meta):
            source = (z + (shift + 8)) % 8
            rows = pl.ds(begin, ref.shape[0])
            for enc in range(2):
                heads[pl.ds(enc * 8 + source, 1), rows, :] = ref[:, enc * 256 : (enc + 1) * 256][None]
        acc[...] = jnp.zeros_like(acc)

    lhs = jnp.concatenate([heads[2 * step], heads[2 * step + 1]], axis=1)
    acc[0] += jnp.dot(lhs, w_own[...], preferred_element_type=F32)
    acc[1] += jnp.dot(lhs, w_other[...], preferred_element_type=F32)

    @pl.when(step == 7)
    def _():
        own = (x_own[...].astype(F32) + gate_own[...] * acc[0]).astype(BF)
        other = (x_other[...].astype(F32) + gate_other[...] * acc[1]).astype(BF)
        own_ref[...] = own
        other_ref[...] = other
        both_ref[:, :320] = own
        both_ref[:, 320:] = other


def mix(place, pieces, w_own, w_other, x_own, x_other, gate_own, gate_other):
    meta = [(shift, begin) for _, shift, begin in pieces]
    arrays = [a for a, _, _ in pieces]
    whole = lambda a: pl.BlockSpec(a.shape, lambda i, s: (0, 0))
    weight = pl.BlockSpec((512, 320), lambda i, s: (i, 0))
    grid_spec = pltpu.PrefetchScalarGridSpec(
        num_scalar_prefetch=1,
        grid=(8,),
        in_specs=[whole(a) for a in arrays]
        + [weight, weight]
        + [whole(a) for a in (x_own, x_other, gate_own, gate_other)],
        out_specs=[
            pl.BlockSpec((256, 320), lambda i, s: (0, 0)),
            pl.BlockSpec((256, 320), lambda i, s: (0, 0)),
            pl.BlockSpec((256, 640), lambda i, s: (0, 0)),
        ],
        scratch_shapes=[pltpu.VMEM((16, 256, 256), BF), pltpu.VMEM((2, 256, 320), F32)],
    )
    return pl.pallas_call(
        functools.partial(mix_kernel, meta),
        grid_spec=grid_spec,
        out_shape=[
            jax.ShapeDtypeStruct((256, 320), BF),
            jax.ShapeDtypeStruct((256, 320), BF),
            jax.ShapeDtypeStruct((256, 640), BF),
        ],
        compiler_params=PARAMS,
        cost_estimate=pl.CostEstimate(flops=4 * 256 * 4096 * 640, bytes_accessed=10 << 20, transcendentals=0),
        name="mix",
    )(place, *arrays, w_own, w_other, x_own, x_other, gate_own, gate_other)


def query_kernel(meta, place, *refs):
    count = len(meta)
    pieces = refs[:count]
    a_own, a_other, b_own, b_other, gain, bias, key_sums, raw_ref, sums_ref, stream, weight, stats, acc = refs[count:]
    step = pl.program_id(0)
    z = place[3]

    @pl.when(step == 0)
    def _():
        for ref, (shift, begin) in zip(pieces, meta):
            source = (z + (shift + 8)) % 8
            rows = pl.ds(begin, ref.shape[0])
            stream[pl.ds(source, 1), rows, :] = ref[...][None]
        total = jnp.zeros((256, HEAD), F32)
        square = jnp.zeros((256, HEAD), F32)
        for source in range(8):
            for j in range(0, 640, HEAD):
                x = stream[source, :, j : j + HEAD].astype(F32)
                total += x
                square += x * x
        mean = jnp.sum(total, axis=1, keepdims=True) * (1.0 / 5120)
        meansq = jnp.sum(square, axis=1, keepdims=True) * (1.0 / 5120)
        stats[0] = jnp.broadcast_to(mean, (256, HEAD))
        stats[1] = jnp.broadcast_to(lax.rsqrt(meansq - mean * mean + EPS), (256, HEAD))
        acc[...] = jnp.zeros_like(acc)

    x = stream[step].astype(F32)
    mean = stats[0, :, :1]
    scale = stats[1, :, :1]
    normed = ((x - mean) * scale * gain[pl.ds(step, 1), :] + bias[pl.ds(step, 1), :]).astype(BF)
    weight[:320, :256] = a_own[...]
    weight[320:, :256] = a_other[...]
    weight[:320, 256:] = b_own[...]
    weight[320:, 256:] = b_other[...]
    acc[...] += jnp.dot(normed, weight[...], preferred_element_type=F32)

    @pl.when(step == 7)
    def _():
        raw = acc[...]
        raw_ref[...] = raw
        square = raw * raw
        part = square[:, :HEAD]
        for j in range(HEAD, 512, HEAD):
            part += square[:, j : j + HEAD]
        sums = jnp.broadcast_to(jnp.sum(part, axis=1, keepdims=True), (256, HEAD))
        rank = lax.broadcasted_iota(jnp.int32, (8, HEAD), 0)
        low = jnp.transpose(sums[:HEAD])[:8]
        up = jnp.transpose(sums[HEAD:])[:8]
        line = jnp.where(rank == 0, low, jnp.where(rank == 1, up, key_sums[...]))
        for i in range(16):
            sums_ref[i] = line


def query(place, pieces, w_own, w_other, gain, bias, key_sums):
    meta = [(shift, begin) for _, shift, begin in pieces]
    arrays = [a for a, _, _ in pieces]
    whole = lambda a: pl.BlockSpec(a.shape, lambda i, s: (0, 0))
    same = pl.BlockSpec((320, 256), lambda i, s: (s[4] * 8 + i, 0))
    cross = pl.BlockSpec((320, 256), lambda i, s: ((1 - s[4]) * 8 + i, 0))
    grid_spec = pltpu.PrefetchScalarGridSpec(
        num_scalar_prefetch=1,
        grid=(8,),
        in_specs=[whole(a) for a in arrays]
        + [same, cross, same, cross]
        + [whole(a) for a in (gain, bias, key_sums)],
        out_specs=[
            pl.BlockSpec((256, 512), lambda i, s: (0, 0)),
            pl.BlockSpec((16, 8, HEAD), lambda i, s: (0, 0, 0)),
        ],
        scratch_shapes=[
            pltpu.VMEM((8, 256, 640), BF),
            pltpu.VMEM((640, 512), BF),
            pltpu.VMEM((2, 256, HEAD), F32),
            pltpu.VMEM((256, 512), F32),
        ],
    )
    return pl.pallas_call(
        functools.partial(query_kernel, meta),
        grid_spec=grid_spec,
        out_shape=[
            jax.ShapeDtypeStruct((256, 512), F32),
            jax.ShapeDtypeStruct((16, 8, HEAD), F32),
        ],
        compiler_params=PARAMS,
        cost_estimate=pl.CostEstimate(flops=2 * 256 * 5120 * 512, bytes_accessed=10 << 20, transcendentals=0),
        name="query",
    )(place, *arrays, w_own, w_own, w_other, w_other, gain, bias, key_sums)


def cross_kernel(place, raw_ref, sums_ref, own_ref, other_ref, own_out, other_out):
    enc, length = place[4], place[5]
    queries = jnp.zeros((8, HEAD), F32)
    keys = jnp.zeros((8, HEAD), F32)
    for i in range(8):
        low, up = sums_ref[i], sums_ref[8 + i]
        queries += jnp.where(enc == 0, low, up)
        keys += low + up
    factor_q = lax.rsqrt(queries * (1.0 / 4096) + EPS)
    factor_k = lax.rsqrt(keys * (1.0 / 4096) + EPS) * SCALE2
    column = jnp.concatenate(
        [jnp.transpose(jnp.broadcast_to(factor_q[i : i + 1], (HEAD, HEAD))) for i in range(2)], axis=0
    )
    line = jnp.concatenate([factor_k[2 + i : 3 + i] for i in range(4)], axis=1)
    live = lax.broadcasted_iota(jnp.int32, (256, 512), 1) < length
    for source, out in ((own_ref, own_out), (other_ref, other_out)):
        for head in range(2):
            base = head * HEAD + (256 if source is other_ref else 0)
            lanes = slice(head * HEAD, (head + 1) * HEAD)
            q = (raw_ref[:, base : base + HEAD] * column).astype(BF)
            s = lax.dot_general(q, source[0, :, lanes], NT, preferred_element_type=F32) * line
            s = jnp.where(live, s, -1e30)
            p = jnp.exp2(s - jnp.max(s, axis=1, keepdims=True))
            total = jnp.sum(p, axis=1, keepdims=True)
            o = jnp.dot(p.astype(BF), source[1, :, lanes], preferred_element_type=F32)
            out[:, lanes] = (o / total).astype(BF)


def cross(place, raw, sums, own, other):
    return pl.pallas_call(
        cross_kernel,
        in_specs=[pl.BlockSpec(memory_space=pltpu.SMEM)] + [pl.BlockSpec(memory_space=pltpu.VMEM)] * 4,
        out_shape=[jax.ShapeDtypeStruct((256, 256), BF)] * 2,
        compiler_params=PARAMS,
        name="cross",
    )(place, raw, sums, own, other)


def on_device(
    x_res,
    q_proj,
    k_proj,
    v_proj,
    w_out,
    gate_table,
    timestep,
    norm_gain,
    norm_bias,
    w_query,
    context,
    w_key,
    w_value,
    gain_cq,
    gain_ck,
    text_len,
):
    e = lax.axis_index("enc")
    c = lax.axis_index("core")
    y = lax.axis_index("yh")
    z = lax.axis_index("tp")
    seq = (lax.axis_index("x") * 2 + y) * 2 + c
    place = jnp.stack([c, seq, y, z, e, text_len[0]]).astype(jnp.int32)
    swap = [(0, 1), (1, 0)]
    x_up = [(i, (i + 1) % 4) for i in range(4)]
    x_down = [(i, (i - 1) % 4) for i in range(4)]

    mine, send = rope(place, q_proj, k_proj, v_proj)
    other = lax.ppermute(send, "core", swap)
    kv = jnp.concatenate([mine[1:], other[1:]], axis=0).reshape(2, 2, 512, HEAD)
    q_own = jnp.concatenate([mine[0], other[0]], axis=0)
    q_far = lax.ppermute(q_own, "yh", swap)
    kv_left = lax.ppermute(kv, "x", x_up)
    kv_right = lax.ppermute(kv, "x", x_down)
    w_out_other = lax.ppermute(w_out, "enc", swap)
    w_query_other = lax.ppermute(w_query, "enc", swap)

    gate = lax.dynamic_slice_in_dim(gate_table, timestep[0], 1, 0)
    one = lax.reduce_precision(gate, 8, 7)
    two = lax.reduce_precision(gate - one, 8, 7)
    gate_rows = jnp.concatenate([one, two, gate - one - two, jnp.zeros((13, 320), F32)], axis=0)
    x_own = lax.dynamic_slice_in_dim(x_res, e * 256, 256, 0)
    x_send = lax.dynamic_slice_in_dim(x_res, (1 - e) * 256, 256, 0)
    x_packed = lax.ppermute(jnp.concatenate([x_send, gate_rows.astype(BF)], axis=0), "enc", swap)
    x_other = x_packed[:256]
    gate_other = jnp.sum(x_packed[256:259].astype(F32), axis=0, keepdims=True)

    q_all = jnp.concatenate([q_own, q_far], axis=0)
    state = attend(place, q_all, [kv], None, False)
    kv_far_a = lax.ppermute(kv_left[:1], "x", x_up)
    kv_far_b = lax.ppermute(kv_right[1:], "x", x_down)
    state = attend(place, q_all, [kv_left, kv_right], state, False)
    parts = attend(place, q_all, [kv_far_a, kv_far_b], state, True)
    parts = lax.all_to_all(parts, ("yh", "core", "enc"), 0, 0, tiled=True)
    heads = merge(parts)

    context, heads = lax.optimization_barrier((context, heads))
    text = lax.all_gather(context, ("enc", "x", "yh", "core"), axis=0, tiled=True)
    key_raw = jnp.dot(text, w_key, preferred_element_type=F32)
    values_text = jnp.dot(text, w_value, preferred_element_type=F32).astype(BF)
    key_sums = jnp.sum(key_raw * key_raw, axis=1).reshape(4, HEAD)
    key_sums = jnp.concatenate([jnp.zeros((2, HEAD), F32), key_sums, jnp.zeros((2, HEAD), F32)], axis=0)
    keys_text = (key_raw * (gain_ck * gain_cq)).astype(BF)
    text_own = jnp.stack([keys_text, values_text])
    text_other = lax.ppermute(text_own, "enc", swap)

    mixed_own, mixed_other, block = mix(
        place, ring(heads), w_out, w_out_other, x_own, x_other, gate, gate_other
    )
    mixed_back = lax.ppermute(mixed_other, "enc", swap)

    order = lambda a: jnp.transpose(
        jnp.where(e == 0, a.reshape(2, 8, 320), a.reshape(2, 8, 320)[::-1]), (1, 0, 2)
    ).reshape(8, 640)
    raw, sums = query(
        place, ring(block), w_query, w_query_other, order(norm_gain), order(norm_bias), key_sums
    )
    sums = lax.all_to_all(sums, ("enc", "tp"), 0, 0, tiled=True)
    cross_own, cross_other = cross(place, raw, sums, text_own, text_other)
    cross_back = lax.ppermute(cross_other, "enc", swap)

    def assemble(own, back):
        return jnp.where(
            e == 0, jnp.concatenate([own, back], axis=0), jnp.concatenate([back, own], axis=0)
        )

    return (assemble(mixed_own, mixed_back), assemble(cross_own, cross_back))


def solution(mesh):
    parts = Mesh(mesh.devices.reshape(2, 4, 2, 2, 8), ("enc", "x", "yh", "core", "tp"))
    seq = ("x", "yh", "core")
    feat = ("enc", "tp")
    placed = (
        P(seq, feat),
        P(seq, feat),
        P(seq, feat),
        P(seq, feat),
        P(None, feat),
        P(None, feat),
        P(),
        P(),
        P(),
        P(None, feat),
        P(("enc", "x", "yh", "core"), None),
        P(None, feat),
        P(None, feat),
        P(feat),
        P(feat),
        P(),
    )
    return jax.shard_map(
        on_device,
        mesh=parts,
        in_specs=placed,
        out_specs=(P(seq, feat), P(seq, feat)),
        check_vma=False,
    )
```

```python
import functools

import jax
import jax.numpy as jnp
import numpy as np
from jax import lax
from jax.experimental import pallas as pl
from jax.experimental.pallas import tpu as pltpu
from jax.sharding import Mesh, PartitionSpec as P

HEAD = 128
GRID_H = 45
GRID_W = 80
EPS = 1e-06
THETA = 10000.0
LOG2E = 1.4426950408889634
SCALE2 = LOG2E * HEAD**-0.5
BF = jnp.bfloat16
F32 = jnp.float32
NT = (((1,), (1,)), ((), ()))
PARAMS = pltpu.CompilerParams(vmem_limit_bytes=24 * 1024 * 1024)
VMEM = pl.BlockSpec(memory_space=pltpu.VMEM)
SMEM = pl.BlockSpec(memory_space=pltpu.SMEM)
PART = 1152


def frequencies():
    part_time = HEAD - 4 * (HEAD // 6)
    part_space = 2 * (HEAD // 6)
    time = THETA ** (-np.arange(0, part_time, 2).astype(np.float32) / part_time)
    space = THETA ** (-np.arange(0, part_space, 2).astype(np.float32) / part_space)
    pairs = np.concatenate([time, space, space]).astype(np.float32)
    return np.repeat(pairs, 2)[None, :]


def rope_kernel(place, q_ref, k_ref, v_ref, freq_ref, mine_ref, send_ref):
    rows = q_ref.shape[0]
    core = place[0]
    start = place[1] * 512
    shape = (rows, HEAD)
    position = (start + lax.broadcasted_iota(jnp.int32, shape, 0)).astype(F32)
    lane = lax.broadcasted_iota(jnp.int32, shape, 1)
    line = jnp.floor((position + 0.5) * (1.0 / GRID_W))
    column = position - line * GRID_W
    frame = jnp.floor((line + 0.5) * (1.0 / GRID_H))
    row = line - frame * GRID_H
    part_time = HEAD - 4 * (HEAD // 6)
    part_space = 2 * (HEAD // 6)
    axis = jnp.where(lane < part_time, frame, jnp.where(lane < part_time + part_space, row, column))
    angles = axis * freq_ref[...]
    even = lane % 2 == 0
    cosine = jnp.cos(angles)
    sine = jnp.sin(angles)
    sine = jnp.where(even, -sine, sine)
    for index, ref in enumerate((q_ref, k_ref, v_ref)):
        heads = []
        for head in range(2):
            x = ref[:, head * HEAD : (head + 1) * HEAD]
            if index < 2:
                x = x.astype(F32)
                other = jnp.where(even, pltpu.roll(x, HEAD - 1, 1), pltpu.roll(x, 1, 1))
                x = (x * cosine + other * sine).astype(BF)
            heads.append(x)
        first = core == 0
        mine_ref[index * 512 : (index + 1) * 512, :] = jnp.where(first, heads[0], heads[1])
        send_ref[index * 512 : (index + 1) * 512, :] = jnp.where(first, heads[1], heads[0])


def rope(place, q, k, v):
    return pl.pallas_call(
        rope_kernel,
        grid_spec=pltpu.PrefetchScalarGridSpec(
            num_scalar_prefetch=1,
            grid=(1,),
            in_specs=[pl.BlockSpec((512, 256), lambda i, s: (0, 0))] * 3
            + [pl.BlockSpec((1, HEAD), lambda i, s: (0, 0))],
            out_specs=[pl.BlockSpec((1536, HEAD), lambda i, s: (0, 0))] * 2,
        ),
        out_shape=[jax.ShapeDtypeStruct((1664, HEAD), BF)] * 2,
        compiler_params=PARAMS,
        name="rope",
    )(place, q, k, v, frequencies())


def text_kernel(text, w_key, w_value, gain, mine_in, send_in, mine_ref, send_ref, acc):
    step = pl.program_id(0)

    @pl.when(step == 0)
    def _():
        acc[...] = jnp.zeros_like(acc)

    x = text[...]
    acc[0] += jnp.dot(x, w_key[...], preferred_element_type=F32)
    acc[1] += jnp.dot(x, w_value[...], preferred_element_type=F32)

    @pl.when(step == pl.num_programs(0) - 1)
    def _():
        values = (acc[0] * gain[...], acc[1])
        for kind in range(2):
            for head in range(2):
                block = values[kind][:, head * HEAD : (head + 1) * HEAD].astype(BF)
                rows = pl.ds((kind * 2 + head) * 32, 32)
                mine_ref[rows, :] = block
                send_ref[rows, :] = block


def text_part(text, w_key, w_value, gain, mine, send):
    depth = 1280
    weight = pl.BlockSpec((depth, 256), lambda i: (i, 0))
    return pl.pallas_call(
        text_kernel,
        grid=(5120 // depth,),
        in_specs=[pl.BlockSpec((32, depth), lambda i: (0, i)), weight, weight]
        + [pl.BlockSpec((1, 256), lambda i: (0, 0))]
        + [pl.BlockSpec(memory_space=pl.ANY)] * 2,
        out_specs=[pl.BlockSpec((HEAD, HEAD), lambda i: (12, 0))] * 2,
        out_shape=[jax.ShapeDtypeStruct((1664, HEAD), BF)] * 2,
        scratch_shapes=[pltpu.VMEM((2, 32, 256), F32)],
        input_output_aliases={4: 0, 5: 1},
        compiler_params=PARAMS,
        name="text_part",
    )(text, w_key, w_value, gain, mine, send)


def text_place_kernel(place, near, far, gain, out_ref, sums_ref):
    core, seq = place[0], place[1]
    x = seq // 4
    y = place[2]
    for group, ref in ((0, near), (1, far)):
        for index in range(8):
            column = (x + (0, 3, 1, 2)[index // 2]) % 4
            device = (column * 2 + (y + group) % 2) * 2 + (core + index % 2) % 2
            for kind in range(2):
                for head in range(2):
                    for enc in range(2):
                        begin = index * HEAD + (kind * 2 + head) * 32 + enc * 16
                        rows = pl.ds(pl.multiple_of(enc * 256 + device * 16, 16), 16)
                        out_ref[kind, rows, head * HEAD : (head + 1) * HEAD] = ref[begin : begin + 16, :]
    keys = out_ref[0].astype(F32) / gain[...]
    square = keys[:, :HEAD] * keys[:, :HEAD] + keys[:, HEAD:] * keys[:, HEAD:]
    line = jnp.sum(jnp.transpose(square), axis=0, keepdims=True)
    rank = lax.broadcasted_iota(jnp.int32, (8, HEAD), 0)
    rows = jnp.zeros((8, HEAD), F32)
    for i in range(4):
        rows = jnp.where(rank == 2 + i, line[:, i * HEAD : (i + 1) * HEAD], rows)
    sums_ref[...] = rows


def text_place(place, near, far, gain):
    return pl.pallas_call(
        text_place_kernel,
        in_specs=[SMEM, VMEM, VMEM, VMEM],
        out_specs=[VMEM, VMEM],
        out_shape=[jax.ShapeDtypeStruct((2, 512, 256), BF), jax.ShapeDtypeStruct((8, HEAD), F32)],
        compiler_params=PARAMS,
        name="text_place",
    )(place, near, far, gain)


def attend_kernel(count, first, last, skip, place, *refs):
    q_ref, kvs = refs[0], refs[1 : 1 + count]
    refs = refs[1 + count :]
    if not first:
        acc_in, high_in = refs[:2]
        refs = refs[2:]
    refs = refs[skip:]
    if last:
        out_ref, wide = refs
    else:
        acc_out, high_out, wide = refs
    chunk = 512
    sub = 256

    @pl.when(pl.program_id(0) == 0)
    def _():
        base = 0
        for kv in kvs:
            for i in range(0, kv.shape[0], PART):
                wide[pl.ds(base, chunk), :HEAD] = kv[i + 512 : i + 1024, :]
                wide[pl.ds(base, chunk), HEAD:] = jnp.ones((chunk, HEAD), BF)
                base += chunk

    def score(begin):
        q = q_ref[pl.ds(begin, sub), :]
        return [
            lax.dot_general(q, kv[i : i + 512, :], NT, preferred_element_type=F32)
            for kv in kvs
            for i in range(0, kv.shape[0], PART)
        ]

    def finish(begin, scores):
        rows = pl.ds(begin, sub)
        high = None
        for s in scores:
            for j in range(0, chunk, HEAD):
                part = s[:, j : j + HEAD]
                high = part if high is None else jnp.maximum(high, part)
        high = jnp.max(high, axis=1, keepdims=True)
        acc = None
        if not first:
            before = high_in[rows, :1]
            high = jnp.maximum(before, high)
            acc = acc_in[rows, :] * jnp.exp2((before - high) * SCALE2)
        shift = high * SCALE2
        for i, s in enumerate(scores):
            p = jnp.exp2(s * SCALE2 - shift).astype(BF)
            update = jnp.dot(p, wide[pl.ds(i * chunk, chunk), :], preferred_element_type=F32)
            acc = update if acc is None else acc + update
        if not last:
            acc_out[rows, :] = acc
            high_out[rows, :] = jnp.broadcast_to(high, (sub, HEAD))
            return
        total = acc[:, HEAD:]
        block = (place[0] + begin // 512) % 2 * 2 + begin // sub % 2
        line = jnp.transpose(shift + jnp.log(total) * LOG2E)[:16, :]
        one = line.astype(BF).astype(F32)
        two = (line - one).astype(BF).astype(F32)
        three = line - one - two
        rank = lax.broadcasted_iota(jnp.int32, (16, sub), 0)
        packed = jnp.where(rank == 0, one, jnp.where(rank == 1, two, jnp.where(rank == 2, three, 0.0)))
        out_ref[pl.ds(block, 1), :HEAD, :] = jnp.transpose(acc[:, :HEAD] / total).astype(BF)[None]
        out_ref[pl.ds(block, 1), HEAD:, :] = packed.astype(BF)[None]

    begins = list(range(0, q_ref.shape[0], sub))
    ahead = score(begins[0])
    for index, begin in enumerate(begins):
        scores = ahead
        if index + 1 < len(begins):
            ahead = score(begins[index + 1])
        finish(begin, scores)


def attend(place, q, kvs, state=None, last=False, into=None, slot=0):
    total = q.shape[0]
    keys = sum(kv.shape[0] for kv in kvs) // PART * 512
    rows = 1024

    def row(width, at=0):
        return pl.BlockSpec((rows, width), lambda i, s: (i + at, 0))

    operands = [q, *kvs]
    specs = [row(HEAD)] + [pl.BlockSpec(kv.shape, lambda i, s: (0, 0)) for kv in kvs]
    if state is not None:
        operands += list(state)
        specs += [row(256), row(HEAD)]
    aliases = {}
    if into is not None:
        aliases = {len(operands) + 1: 0, len(operands) + 2: 1}
        operands += list(into)
        specs += [pl.BlockSpec(memory_space=pl.ANY)] * 2
    if last:
        out_specs = pl.BlockSpec((4, 144, 256), lambda i, s: ((s[2] + i) % 2, 0, 0))
        out_shape = jax.ShapeDtypeStruct((8, 144, 256), BF)
    else:
        out_specs = [row(256, slot), row(HEAD, slot)]
        out_shape = [jax.ShapeDtypeStruct((2048, 256), F32), jax.ShapeDtypeStruct((2048, HEAD), F32)]
    grid_spec = pltpu.PrefetchScalarGridSpec(
        num_scalar_prefetch=1,
        grid=(total // rows,),
        in_specs=specs,
        out_specs=out_specs,
        scratch_shapes=[pltpu.VMEM((keys, 256), BF)],
    )
    return pl.pallas_call(
        functools.partial(attend_kernel, len(kvs), state is None, last, 0 if into is None else 2),
        grid_spec=grid_spec,
        out_shape=out_shape,
        input_output_aliases=aliases,
        compiler_params=PARAMS,
        cost_estimate=pl.CostEstimate(
            flops=4 * total * keys * HEAD, bytes_accessed=4 * 1024 * 1024, transcendentals=total * keys
        ),
        name="attend",
    )(place, *operands)


def merge_kernel(in_ref, low_ref, up_ref):
    for head in range(4):
        enc, core = head // 2, head % 2
        sources = [half * 4 + core * 2 + enc for half in range(2)]
        logs = []
        for source in sources:
            lines = in_ref[source, HEAD:, :].astype(F32)
            logs.append(lines[0:1, :] + lines[1:2, :] + lines[2:3, :])
        first = in_ref[sources[0], :HEAD, :].astype(F32) / (1.0 + jnp.exp2(logs[1] - logs[0]))
        second = in_ref[sources[1], :HEAD, :].astype(F32) / (1.0 + jnp.exp2(logs[0] - logs[1]))
        out = low_ref if enc == 0 else up_ref
        out[core * HEAD : (core + 1) * HEAD, :] = (first + second).astype(BF)


def merge(parts):
    return pl.pallas_call(
        merge_kernel,
        in_specs=[VMEM],
        out_specs=[VMEM] * 2,
        out_shape=[jax.ShapeDtypeStruct((256, 256), BF)] * 2,
        compiler_params=PARAMS,
        name="merge",
    )(parts)


UP = [(i, (i + 1) % 8) for i in range(8)]
DOWN = [(i, (i - 1) % 8) for i in range(8)]


def ring(pair):
    near = [pair]
    right = left = pair
    for step in range(1, 4):
        right = [lax.ppermute(a, "tp", UP) for a in right]
        left = [lax.ppermute(a, "tp", DOWN) for a in left]
        near += [right, left]
    far = [lax.ppermute(right[0], "tp", UP), lax.ppermute(left[1], "tp", DOWN)]
    return near, far


SHIFTS = [0, 7, 1, 6, 2, 5, 3]


def pack_kernel(place, own_x, send_x, gates, own_ref, send_ref):
    lane = lax.broadcasted_iota(jnp.int32, gates.shape, 1)
    gate = jnp.sum(jnp.where(lane == place[6], gates[...], 0.0), axis=1, keepdims=True)
    one = gate.astype(BF).astype(F32)
    two = (gate - one).astype(BF).astype(F32)
    lane = lax.broadcasted_iota(jnp.int32, (320, HEAD), 1)
    terms = jnp.where(lane == 0, one, jnp.where(lane == 1, two, jnp.where(lane == 2, gate - one - two, 0.0)))
    for x, out in ((own_x, own_ref), (send_x, send_ref)):
        out[:, :256] = x[...]
        out[:, 256:] = terms.astype(BF)


def pack(place, x, gates):
    return pl.pallas_call(
        pack_kernel,
        grid_spec=pltpu.PrefetchScalarGridSpec(
            num_scalar_prefetch=1,
            grid=(1,),
            in_specs=[
                pl.BlockSpec((320, 256), lambda i, s: (0, s[4])),
                pl.BlockSpec((320, 256), lambda i, s: (0, 1 - s[4])),
                pl.BlockSpec(gates.shape, lambda i, s: (0, 0)),
            ],
            out_specs=[pl.BlockSpec((320, 384), lambda i, s: (0, 0))] * 2,
        ),
        out_shape=[jax.ShapeDtypeStruct((320, 384), BF)] * 2,
        compiler_params=PARAMS,
        name="pack",
    )(place, x, x, gates)


def mix_add(place, pairs, shifts, w_own, w_one, w_two, acc):
    core, z = place[0], place[3]
    for (low, up), shift in zip(pairs, shifts):
        source = (z + shift) % 8
        first = pl.ds(pl.multiple_of(source * 256, 256), 256)
        second = pl.ds(pl.multiple_of(2048 + source * 256, 256), 256)
        low, up = low[...], up[...]

        def add(w):
            return jnp.dot(w[:, first], low, preferred_element_type=F32) + jnp.dot(
                w[:, second], up, preferred_element_type=F32
            )

        acc[:320] += add(w_own)
        acc[pl.ds(pl.multiple_of(320 + core * 160, 32), 160)] += add(w_one)
        acc[pl.ds(pl.multiple_of(480 - core * 160, 32), 160)] += add(w_two)


def mix_near_kernel(place, *refs):
    pairs = [refs[2 * i : 2 * i + 2] for i in range(7)]
    w_own, w_one, w_two, acc = refs[14:]
    acc[...] = jnp.zeros_like(acc)
    mix_add(place, pairs, SHIFTS, w_own, w_one, w_two, acc)


def mix_near(place, near, weights):
    return pl.pallas_call(
        mix_near_kernel,
        in_specs=[SMEM] + [VMEM] * 17,
        out_specs=VMEM,
        out_shape=jax.ShapeDtypeStruct((640, 256), F32),
        compiler_params=PARAMS,
        cost_estimate=pl.CostEstimate(flops=2 * 256 * 3584 * 640, bytes_accessed=1 << 20, transcendentals=0),
        name="mix_near",
    )(place, *[a for pair in near for a in pair], *weights)


def mix_far_kernel(place, low, up, w_own, w_one, w_two, near, own_x, other_x, own, other, acc):
    acc[...] = near[...]
    mix_add(place, [(low, up)], [4], w_own, w_one, w_two, acc)
    for x, begin, out in ((own_x, 0, own), (other_x, 320, other)):
        gate = jnp.sum(x[:, 256:].astype(F32), axis=1, keepdims=True)
        out[...] = (x[:, :256].astype(F32) + gate * acc[begin : begin + 320]).astype(BF)


def mix_far(place, far, weights, near, own_x, other_x):
    return pl.pallas_call(
        mix_far_kernel,
        in_specs=[SMEM] + [VMEM] * 8,
        out_specs=[VMEM] * 2,
        out_shape=[jax.ShapeDtypeStruct((320, 256), BF)] * 2,
        scratch_shapes=[pltpu.VMEM((640, 256), F32)],
        compiler_params=PARAMS,
        name="mix_far",
    )(place, *far, *weights, near, own_x, other_x)


def stream_kernel(place, *refs):
    pieces = refs[:14]
    gain, bias, out_ref, sums_ref, terms = refs[14:]
    enc = place[4]
    total = jnp.zeros((1, 256), F32)
    square = jnp.zeros((1, 256), F32)
    for i, ref in enumerate(pieces):
        x = ref[...]
        begin = i % 2 * 320
        out_ref[i // 2, :, begin : begin + 320] = jnp.transpose(x)
        x = x.astype(F32)
        total += jnp.sum(x, axis=0, keepdims=True)
        square += jnp.sum(x * x, axis=0, keepdims=True)
    rank = lax.broadcasted_iota(jnp.int32, (8, 256), 0)
    sums_ref[...] = jnp.where(rank == 0, total, jnp.where(rank == 1, square, 0.0))
    for i, ref in enumerate((gain, bias)):
        terms[i, :, :320] = ref[pl.ds(pl.multiple_of(enc * 8, 8), 8), :]
        terms[i, :, 320:] = ref[pl.ds(pl.multiple_of(8 - enc * 8, 8), 8), :]


def stream(place, near, gain, bias):
    return pl.pallas_call(
        stream_kernel,
        in_specs=[SMEM] + [VMEM] * 16,
        out_specs=[VMEM] * 3,
        out_shape=[
            jax.ShapeDtypeStruct((7, 256, 640), BF),
            jax.ShapeDtypeStruct((8, 256), F32),
            jax.ShapeDtypeStruct((2, 8, 640), F32),
        ],
        compiler_params=PARAMS,
        cost_estimate=pl.CostEstimate(flops=1 << 24, bytes_accessed=6 << 20, transcendentals=0),
        name="stream",
    )(place, *[a for pair in near for a in pair], gain, bias)


def query_kernel(
    place, near, far_own, far_other, near_sums, terms, w_own, w_one, w_two, key_sums, raw_ref, sums_ref, last, weight, acc
):
    z, enc = place[3], place[4]
    total = near_sums[0:1]
    square = near_sums[1:2]
    for i, ref in enumerate((far_own, far_other)):
        x = ref[...]
        last[:, i * 320 : (i + 1) * 320] = jnp.transpose(x)
        x = x.astype(F32)
        total += jnp.sum(x, axis=0, keepdims=True)
        square += jnp.sum(x * x, axis=0, keepdims=True)
    mean = total * (1.0 / 5120)
    scale = lax.rsqrt(square * (1.0 / 5120) - mean * mean + EPS)
    mean = jnp.transpose(jnp.broadcast_to(mean, (HEAD, 256)))[:, :1]
    scale = jnp.transpose(jnp.broadcast_to(scale, (HEAD, 256)))[:, :1]
    for step in range(8):
        source = (z + (SHIFTS + [4])[step]) % 8
        x = last[...] if step == 7 else near[step]
        row = pl.ds(source, 1)
        normed = ((x.astype(F32) - mean) * scale * terms[0, row, :] + terms[1, row, :]).astype(BF)
        slot = step % 2
        for i in range(2):
            rows = pl.ds(pl.multiple_of((enc + i) % 2 * 2560 + source * 320, 64), 320)
            to = slice(i * 320, (i + 1) * 320)
            weight[slot, to, :256] = w_own[rows, :]
            weight[slot, to, 256:384] = w_one[rows, :]
            weight[slot, to, 384:] = w_two[rows, :]
        update = jnp.dot(normed, weight[slot], preferred_element_type=F32)
        acc[...] = update if step == 0 else acc[...] + update
    raw = acc[...]
    raw_ref[...] = raw
    square = raw * raw
    part = square[:, :HEAD]
    for j in range(HEAD, 512, HEAD):
        part += square[:, j : j + HEAD]
    line = jnp.sum(jnp.transpose(part), axis=0, keepdims=True)
    rank = lax.broadcasted_iota(jnp.int32, (8, HEAD), 0)
    line = jnp.where(rank == 0, line[:, :HEAD], jnp.where(rank == 1, line[:, HEAD:], key_sums[...]))
    for i in range(16):
        sums_ref[i] = line


def query(place, turned, far, w_own, w_one, w_two, key_sums):
    near, near_sums, terms = turned
    return pl.pallas_call(
        query_kernel,
        in_specs=[SMEM] + [VMEM] * 9,
        out_specs=[VMEM] * 2,
        out_shape=[
            jax.ShapeDtypeStruct((256, 512), F32),
            jax.ShapeDtypeStruct((16, 8, HEAD), F32),
        ],
        scratch_shapes=[
            pltpu.VMEM((256, 640), BF),
            pltpu.VMEM((2, 640, 512), BF),
            pltpu.VMEM((256, 512), F32),
        ],
        compiler_params=PARAMS,
        cost_estimate=pl.CostEstimate(flops=2 * 256 * 5120 * 512, bytes_accessed=1 << 20, transcendentals=0),
        name="query",
    )(place, near, *far, near_sums, terms, w_own, w_one, w_two, key_sums)


def cross_kernel(partner, place, raw_ref, sums_ref, text_ref, out):
    core, enc, length = place[0], place[4], place[5]
    queries = jnp.zeros((8, HEAD), F32)
    keys = jnp.zeros((8, HEAD), F32)
    for i in range(8):
        low, up = sums_ref[i], sums_ref[8 + i]
        queries += jnp.where(enc == 0, low, up)
        keys += low + up
    factor_q = lax.rsqrt(queries * (1.0 / 4096) + EPS)
    factor_k = lax.rsqrt(keys * (1.0 / 4096) + EPS) * SCALE2
    column = jnp.concatenate(
        [jnp.transpose(jnp.broadcast_to(factor_q[i : i + 1], (HEAD, HEAD))) for i in range(2)], axis=0
    )
    line = jnp.concatenate([factor_k[2 + i : 3 + i] for i in range(4)], axis=1)
    live = lax.broadcasted_iota(jnp.int32, (256, 512), 1) < length
    for index in range(2):
        if partner:
            lanes = pl.ds(pl.multiple_of((core + index) % 2 * HEAD, HEAD), HEAD)
        else:
            lanes = slice(index * HEAD, (index + 1) * HEAD)
        begin = index * HEAD + (256 if partner else 0)
        q = (raw_ref[:, begin : begin + HEAD] * column).astype(BF)
        s = lax.dot_general(q, text_ref[0, :, lanes], NT, preferred_element_type=F32) * line
        s = jnp.where(live, s, -1e30)
        p = jnp.exp2(s - jnp.max(s, axis=1, keepdims=True))
        total = jnp.sum(p, axis=1, keepdims=True)
        o = jnp.dot(p.astype(BF), text_ref[1, :, lanes], preferred_element_type=F32)
        out[:, lanes] = (o / total).astype(BF)


def cross(place, raw, sums, text, partner):
    return pl.pallas_call(
        functools.partial(cross_kernel, partner),
        in_specs=[SMEM] + [VMEM] * 3,
        out_specs=VMEM,
        out_shape=jax.ShapeDtypeStruct((256, 256), BF),
        compiler_params=PARAMS,
        name="cross",
    )(place, raw, sums, text)


def on_device(
    x_res,
    q_proj,
    k_proj,
    v_proj,
    w_out,
    gate_table,
    timestep,
    norm_gain,
    norm_bias,
    w_query,
    context,
    w_key,
    w_value,
    gain_cq,
    gain_ck,
    text_len,
):
    e = lax.axis_index("enc")
    c = lax.axis_index("core")
    y = lax.axis_index("yh")
    z = lax.axis_index("tp")
    seq = (lax.axis_index("x") * 2 + y) * 2 + c
    place = jnp.stack([c, seq, y, z, e, text_len[0], timestep[0]]).astype(jnp.int32)
    swap = [(0, 1), (1, 0)]
    x_up = [(i, (i + 1) % 4) for i in range(4)]
    x_down = [(i, (i - 1) % 4) for i in range(4)]

    text = lax.ppermute(context, "enc", swap)
    mine, send = rope(place, q_proj, k_proj, v_proj)
    text = jnp.where(
        e == 0, jnp.concatenate([context, text], axis=0), jnp.concatenate([text, context], axis=0)
    )
    gain = (gain_ck * gain_cq)[None, :]
    mine, send = text_part(text, w_key, w_value, gain, mine, send)
    other = lax.ppermute(send, "core", swap)
    kv = jnp.concatenate([mine[512:], other[512:]], axis=0)
    q_own = jnp.concatenate([mine[:512], other[:512]], axis=0)
    q_far = lax.ppermute(q_own, "yh", swap)
    kv_left = lax.ppermute(kv, "x", x_up)
    kv_right = lax.ppermute(kv, "x", x_down)
    q_all = jnp.concatenate([q_own, q_far], axis=0)
    state = attend(place, q_own, [kv])
    state = attend(place, q_far, [kv], into=state, slot=1)
    kv_far_a = lax.ppermute(kv_left[:PART], "x", x_up)
    kv_far_b = lax.ppermute(kv_right[PART:], "x", x_down)
    state = attend(place, q_all, [kv_left, kv_right], state)
    parts = attend(place, q_all, [kv_far_a, kv_far_b], state, last=True)

    w_mine = w_out.T
    w_send, q_far = lax.optimization_barrier((lax.dynamic_slice_in_dim(w_mine, c * 160, 160, 0), q_far))
    w_one = lax.ppermute(w_send, "enc", swap)
    parts, w_one = lax.optimization_barrier((parts, w_one))
    parts = lax.all_to_all(parts, ("yh", "core", "enc"), 0, 0, tiled=True)
    heads = merge(parts)
    w_two = lax.ppermute(w_one, "core", swap)

    x_own, x_send = pack(place, x_res.T, gate_table.T)
    x_other = lax.ppermute(x_send, "enc", swap)

    text_near = [a[b + 1024 : b + PART] for a in (kv, kv_left, kv_right) for b in (0, PART)]
    text_near = jnp.concatenate(text_near + [kv_far_a[1024:], kv_far_b[1024:]], axis=0)
    text_near, heads = lax.optimization_barrier((text_near, heads))
    text_far = lax.ppermute(text_near, "yh", swap)
    text_own, key_sums = text_place(place, text_near, text_far, gain)
    text_other = lax.ppermute(text_own, "enc", swap)

    q_send = lax.dynamic_slice_in_dim(w_query, c * HEAD, HEAD, 1)
    q_send, heads = lax.optimization_barrier((q_send, heads))
    q_one = lax.ppermute(q_send, "enc", swap)

    weights = (w_mine, w_one, w_two)
    near, far = ring(heads)
    acc = mix_near(place, near, weights)
    mixed = mix_far(place, far, weights, acc, x_own, x_other)

    q_one, mixed = lax.optimization_barrier((q_one, mixed))
    q_two = lax.ppermute(q_one, "core", swap)
    mixed_own, mixed_other = mixed
    near, far = ring(mixed)
    mixed_back = lax.ppermute(mixed_other, "enc", swap)
    turned = stream(place, near, norm_gain.reshape(16, 320), norm_bias.reshape(16, 320))
    raw, sums = query(place, turned, far, w_query, q_one, q_two, key_sums)
    sums = lax.all_to_all(sums, ("enc", "tp"), 0, 0, tiled=True)
    cross_other = cross(place, raw, sums, text_other, True)
    cross_back = lax.ppermute(cross_other, "enc", swap)
    cross_own = cross(place, raw, sums, text_own, False)

    def assemble(own, back, axis):
        return jnp.where(
            e == 0, jnp.concatenate([own, back], axis=axis), jnp.concatenate([back, own], axis=axis)
        )

    return (assemble(mixed_own, mixed_back, 1).T, assemble(cross_own, cross_back, 0))


def solution(mesh):
    parts = Mesh(mesh.devices.reshape(2, 4, 2, 2, 8), ("enc", "x", "yh", "core", "tp"))
    seq = ("x", "yh", "core")
    feat = ("enc", "tp")
    placed = (
        P(seq, feat),
        P(seq, feat),
        P(seq, feat),
        P(seq, feat),
        P(None, feat),
        P(None, feat),
        P(),
        P(),
        P(),
        P(None, feat),
        P(("enc", "x", "yh", "core"), None),
        P(None, feat),
        P(None, feat),
        P(feat),
        P(feat),
        P(),
    )
    return jax.shard_map(
        on_device,
        mesh=parts,
        in_specs=placed,
        out_specs=(P(seq, feat), P(seq, feat)),
        check_vma=False,
    )
```

```python
import functools

import jax
import jax.numpy as jnp
import numpy as np
from jax import lax
from jax.experimental import pallas as pl
from jax.experimental.pallas import tpu as pltpu
from jax.sharding import Mesh, PartitionSpec as P

HEAD = 128
GRID_H = 45
GRID_W = 80
EPS = 1e-06
THETA = 10000.0
LOG2E = 1.4426950408889634
SCALE2 = LOG2E * HEAD**-0.5
BF = jnp.bfloat16
F32 = jnp.float32
NT = (((1,), (1,)), ((), ()))
PARAMS = pltpu.CompilerParams(vmem_limit_bytes=16 * 1024 * 1024)
LARGE = pltpu.CompilerParams(vmem_limit_bytes=60 * 1024 * 1024)
SMALL = pltpu.CompilerParams(vmem_limit_bytes=8 * 1024 * 1024)
VMEM = pl.BlockSpec(memory_space=pltpu.VMEM)
SMEM = pl.BlockSpec(memory_space=pltpu.SMEM)
HBM = pl.BlockSpec(memory_space=pltpu.HBM)
PART = 1152


def frequencies():
    part_time = HEAD - 4 * (HEAD // 6)
    part_space = 2 * (HEAD // 6)
    time = THETA ** (-np.arange(0, part_time, 2).astype(np.float32) / part_time)
    space = THETA ** (-np.arange(0, part_space, 2).astype(np.float32) / part_space)
    pairs = np.concatenate([time, space, space]).astype(np.float32)
    return np.repeat(pairs, 2)[None, :]


def front_kernel(
    place, q_hbm, k_hbm, v_hbm, key_hbm, value_hbm, freq_ref, own, other, gain_k, gain_q,
    mine_ref, text_ref, send_ref, held, weights, sems, weight_sems
):
    copies = [pltpu.make_async_copy(ref, held.at[i], sems.at[i]) for i, ref in enumerate((q_hbm, k_hbm, v_hbm))]
    for copy in copies:
        copy.start()
    depth = weights.shape[2]
    loads = {}
    for i in range(4):
        for kind, ref in enumerate((key_hbm, value_hbm)):
            loads[kind, i] = pltpu.make_async_copy(
                ref.at[pl.ds(i * depth, depth)], weights.at[kind, i], weight_sems.at[kind, i]
            )
            loads[kind, i].start()
    core = place[0]
    shape = (512, HEAD)
    position = (place[1] * 512 + lax.broadcasted_iota(jnp.int32, shape, 0)).astype(F32)
    lane = lax.broadcasted_iota(jnp.int32, shape, 1)
    line = jnp.floor((position + 0.5) * (1.0 / GRID_W))
    column = position - line * GRID_W
    frame = jnp.floor((line + 0.5) * (1.0 / GRID_H))
    row = line - frame * GRID_H
    part_time = HEAD - 4 * (HEAD // 6)
    part_space = 2 * (HEAD // 6)
    axis = jnp.where(lane < part_time, frame, jnp.where(lane < part_time + part_space, row, column))
    angles = axis * freq_ref[...]
    even = lane % 2 == 0
    cosine = jnp.cos(angles)
    sine = jnp.sin(angles)
    sine = jnp.where(even, -sine, sine)
    first = core == 0
    for index in range(3):
        copies[index].wait()
        heads = []
        for head in range(2):
            x = held[index, :, head * HEAD : (head + 1) * HEAD]
            if index < 2:
                x = x.astype(F32)
                partner = jnp.where(even, pltpu.roll(x, HEAD - 1, 1), pltpu.roll(x, 1, 1))
                x = (x * cosine + partner * sine).astype(BF)
            heads.append(x)
        mine_ref[index * 512 : (index + 1) * 512, :] = jnp.where(first, heads[0], heads[1])
        send_ref[index * 512 : (index + 1) * 512, :] = jnp.where(first, heads[1], heads[0])

    first = place[4] == 0
    own, other = own[...], other[...]
    text = jnp.concatenate([jnp.where(first, own, other), jnp.where(first, other, own)], axis=0)
    sums = [jnp.zeros((32, 256), F32)] * 2
    for i in range(4):
        for kind in range(2):
            loads[kind, i].wait()
            sums[kind] += jnp.dot(
                text[:, i * depth : (i + 1) * depth], weights[kind, i], preferred_element_type=F32
            )
    sums[0] = sums[0] * (gain_k[...] * gain_q[...])
    for kind in range(2):
        for head in range(2):
            block = sums[kind][:, head * HEAD : (head + 1) * HEAD].astype(BF)
            begin = (kind * 2 + head) * 32
            text_ref[begin : begin + 32, :] = block
            send_ref[1536 + begin : 1568 + begin, :] = block


def front(place, q, k, v, w_key, w_value, own, other, gain_k, gain_q):
    return pl.pallas_call(
        front_kernel,
        in_specs=[SMEM] + [HBM] * 5 + [VMEM] * 5,
        out_specs=[VMEM] * 3,
        out_shape=[
            jax.ShapeDtypeStruct((1536, HEAD), BF),
            jax.ShapeDtypeStruct((HEAD, HEAD), BF),
            jax.ShapeDtypeStruct((1664, HEAD), BF),
        ],
        scratch_shapes=[
            pltpu.VMEM((3, 512, 256), BF),
            pltpu.VMEM((2, 4, 1280, 256), BF),
            pltpu.SemaphoreType.DMA((3,)),
            pltpu.SemaphoreType.DMA((2, 4)),
        ],
        compiler_params=LARGE,
        name="front",
    )(place, q, k, v, w_key, w_value, frequencies(), own, other, gain_k, gain_q)


def join_kernel(mine, text, other, kv_ref, q_ref, text_ref):
    text_ref[:HEAD, :] = text[...]
    text_ref[HEAD:, :] = other[1536:, :]
    q_ref[:512, :] = mine[:512, :]
    q_ref[512:, :] = other[:512, :]
    kv_ref[:1024, :] = mine[512:, :]
    kv_ref[1024:PART, :] = text[...]
    kv_ref[PART:, :] = other[512:, :]


def join(mine, text, other):
    return pl.pallas_call(
        join_kernel,
        in_specs=[VMEM] * 3,
        out_specs=[VMEM] * 3,
        out_shape=[
            jax.ShapeDtypeStruct((2 * PART, HEAD), BF),
            jax.ShapeDtypeStruct((1024, HEAD), BF),
            jax.ShapeDtypeStruct((2 * HEAD, HEAD), BF),
        ],
        compiler_params=SMALL,
        name="join",
    )(mine, text, other)


def take_kernel(place, ref, out):
    out[...] = ref[...]


def take_half(place, array, axis):
    shape = tuple(n // 2 if i == axis else n for i, n in enumerate(array.shape))
    return pl.pallas_call(
        take_kernel,
        grid_spec=pltpu.PrefetchScalarGridSpec(
            num_scalar_prefetch=1,
            grid=(1,),
            in_specs=[pl.BlockSpec(shape, lambda i, s: (s[0], 0) if axis == 0 else (0, s[0]))],
            out_specs=pl.BlockSpec(shape, lambda i, s: (0, 0)),
        ),
        out_shape=jax.ShapeDtypeStruct(shape, BF),
        compiler_params=SMALL,
        name="take_half",
    )(place, array)


def pick_kernel(place, first, second, out):
    @pl.when(place[0] == 0)
    def _():
        out[...] = first[...]

    @pl.when(place[0] != 0)
    def _():
        out[...] = second[...]


def pick(place, first, second):
    return pl.pallas_call(
        pick_kernel,
        in_specs=[SMEM, VMEM, VMEM],
        out_specs=VMEM,
        out_shape=jax.ShapeDtypeStruct(first.shape, BF),
        compiler_params=SMALL,
        name="pick",
    )(place, first, second)


def text_place_kernel(place, near, far, gain_k, gain_q, out_ref, sums_ref):
    core, seq = place[0], place[1]
    x = seq // 4
    y = place[2]
    for group, ref in ((0, near), (1, far)):
        for index in range(8):
            column = (x + (0, 3, 1, 2)[index // 2]) % 4
            device = (column * 2 + (y + group) % 2) * 2 + (core + index % 2) % 2
            for kind in range(2):
                for head in range(2):
                    for enc in range(2):
                        begin = index * HEAD + (kind * 2 + head) * 32 + enc * 16
                        rows = pl.ds(pl.multiple_of(enc * 256 + device * 16, 16), 16)
                        out_ref[kind, rows, head * HEAD : (head + 1) * HEAD] = ref[begin : begin + 16, :]
    keys = out_ref[0].astype(F32) / (gain_k[...] * gain_q[...])
    square = keys[:, :HEAD] * keys[:, :HEAD] + keys[:, HEAD:] * keys[:, HEAD:]
    line = jnp.sum(jnp.transpose(square), axis=0, keepdims=True)
    rank = lax.broadcasted_iota(jnp.int32, (8, HEAD), 0)
    rows = jnp.zeros((8, HEAD), F32)
    for i in range(4):
        rows = jnp.where(rank == 2 + i, line[:, i * HEAD : (i + 1) * HEAD], rows)
    sums_ref[...] = rows


def text_place(place, near, far, gain_k, gain_q):
    return pl.pallas_call(
        text_place_kernel,
        in_specs=[SMEM] + [VMEM] * 4,
        out_specs=[VMEM, VMEM],
        out_shape=[jax.ShapeDtypeStruct((2, 512, 256), BF), jax.ShapeDtypeStruct((8, HEAD), F32)],
        compiler_params=SMALL,
        name="text_place",
    )(place, near, far, gain_k, gain_q)


def attend_kernel(count, first, last, skip, single, texts, place, *refs):
    if single:
        refs = (refs[0], None) + refs[1:]
    q_low, q_up, kvs = refs[0], refs[1], refs[2 : 2 + count]
    refs = refs[2 + count :]
    if not first:
        acc_in, high_in = refs[:2]
        refs = refs[2:]
    refs = refs[skip:]
    if texts:
        text_in, refs = refs[0], refs[1:]
        text_out = refs[-2]
        refs = refs[:-2] + refs[-1:]
        before = texts * HEAD
        text_out[:before, :] = text_in[...]
        for kv in kvs:
            for i in range(0, kv.shape[0], PART):
                text_out[before : before + HEAD, :] = kv[i + 1024 : i + PART, :]
                before += HEAD
    if last:
        out_ref, wide = refs
    else:
        acc_out, high_out, wide = refs
    chunk = 512
    sub = 256

    @pl.when(pl.program_id(0) == 0)
    def _():
        base = 0
        for kv in kvs:
            for i in range(0, kv.shape[0], PART):
                wide[pl.ds(base, chunk), :HEAD] = kv[i + 512 : i + 1024, :]
                wide[pl.ds(base, chunk), HEAD:] = jnp.ones((chunk, HEAD), BF)
                base += chunk

    def score(begin):
        q = q_low[pl.ds(begin, sub), :]
        if q_up is not None:
            q = jnp.where(pl.program_id(0) == 0, q, q_up[pl.ds(begin, sub), :])
        return [
            lax.dot_general(q, kv[i : i + 512, :], NT, preferred_element_type=F32)
            for kv in kvs
            for i in range(0, kv.shape[0], PART)
        ]

    def finish(begin, scores):
        rows = pl.ds(begin, sub)
        high = None
        for s in scores:
            for j in range(0, chunk, HEAD):
                part = s[:, j : j + HEAD]
                high = part if high is None else jnp.maximum(high, part)
        high = jnp.max(high, axis=1, keepdims=True)
        acc = None
        if not first:
            before = high_in[rows, :1]
            high = jnp.maximum(before, high)
            acc = acc_in[rows, :] * jnp.exp2((before - high) * SCALE2)
        shift = high * SCALE2
        for i, s in enumerate(scores):
            p = jnp.exp2(s * SCALE2 - shift).astype(BF)
            update = jnp.dot(p, wide[pl.ds(i * chunk, chunk), :], preferred_element_type=F32)
            acc = update if acc is None else acc + update
        if not last:
            acc_out[rows, :] = acc
            high_out[rows, :] = jnp.broadcast_to(high, (sub, HEAD))
            return
        total = acc[:, HEAD:]
        block = (place[0] + begin // 512) % 2 * 2 + begin // sub % 2
        line = jnp.transpose(shift + jnp.log(total) * LOG2E)[:16, :]
        one = line.astype(BF).astype(F32)
        two = (line - one).astype(BF).astype(F32)
        three = line - one - two
        rank = lax.broadcasted_iota(jnp.int32, (16, sub), 0)
        packed = jnp.where(rank == 0, one, jnp.where(rank == 1, two, jnp.where(rank == 2, three, 0.0)))
        out_ref[pl.ds(block, 1), :HEAD, :] = jnp.transpose(acc[:, :HEAD] / total).astype(BF)[None]
        out_ref[pl.ds(block, 1), HEAD:, :] = packed.astype(BF)[None]

    begins = list(range(0, q_low.shape[0], sub))
    ahead = score(begins[0])
    for index, begin in enumerate(begins):
        scores = ahead
        if index + 1 < len(begins):
            ahead = score(begins[index + 1])
        finish(begin, scores)


def attend(place, qs, kvs, state=None, last=False, into=None, slot=0, text=None):
    total = len(qs) * 1024
    keys = sum(kv.shape[0] for kv in kvs) // PART * 512
    rows = 1024

    def row(width, at=0):
        return pl.BlockSpec((rows, width), lambda i, s: (i + at, 0))

    operands = [*qs, *kvs]
    specs = [pl.BlockSpec(a.shape, lambda i, s: (0, 0)) for a in operands]
    if state is not None:
        operands += list(state)
        specs += [row(256), row(HEAD)]
    aliases = {}
    if into is not None:
        aliases = {len(operands) + 1: 0, len(operands) + 2: 1}
        operands += list(into)
        specs += [pl.BlockSpec(memory_space=pl.ANY)] * 2
    if last:
        out_specs = [pl.BlockSpec((4, 144, 256), lambda i, s: ((s[2] + i) % 2, 0, 0))]
        out_shape = [jax.ShapeDtypeStruct((8, 144, 256), BF)]
    else:
        out_specs = [row(256, slot), row(HEAD, slot)]
        out_shape = [jax.ShapeDtypeStruct((2048, 256), F32), jax.ShapeDtypeStruct((2048, HEAD), F32)]
    texts = 0
    if text is not None:
        texts = text.shape[0] // HEAD
        operands.append(text)
        specs.append(pl.BlockSpec(text.shape, lambda i, s: (0, 0)))
        shape = (text.shape[0] + keys // 512 * HEAD, HEAD)
        out_specs = out_specs + [pl.BlockSpec(shape, lambda i, s: (0, 0))]
        out_shape = out_shape + [jax.ShapeDtypeStruct(shape, BF)]
    grid_spec = pltpu.PrefetchScalarGridSpec(
        num_scalar_prefetch=1,
        grid=(total // rows,),
        in_specs=specs,
        out_specs=out_specs,
        scratch_shapes=[pltpu.VMEM((keys, 256), BF)],
    )
    return pl.pallas_call(
        functools.partial(attend_kernel, len(kvs), state is None, last, 0 if into is None else 2, len(qs) == 1, texts),
        grid_spec=grid_spec,
        out_shape=out_shape,
        input_output_aliases=aliases,
        compiler_params=PARAMS,
        cost_estimate=pl.CostEstimate(
            flops=4 * total * keys * HEAD, bytes_accessed=4 * 1024 * 1024, transcendentals=total * keys
        ),
        name="attend",
    )(place, *operands)


def merge_kernel(in_ref, low_ref, up_ref):
    for head in range(4):
        enc, core = head // 2, head % 2
        sources = [half * 4 + core * 2 + enc for half in range(2)]
        logs = []
        for source in sources:
            lines = in_ref[source, HEAD:, :].astype(F32)
            logs.append(lines[0:1, :] + lines[1:2, :] + lines[2:3, :])
        first = in_ref[sources[0], :HEAD, :].astype(F32) / (1.0 + jnp.exp2(logs[1] - logs[0]))
        second = in_ref[sources[1], :HEAD, :].astype(F32) / (1.0 + jnp.exp2(logs[0] - logs[1]))
        out = low_ref if enc == 0 else up_ref
        out[core * HEAD : (core + 1) * HEAD, :] = (first + second).astype(BF)


def merge(parts):
    return pl.pallas_call(
        merge_kernel,
        in_specs=[VMEM],
        out_specs=[VMEM] * 2,
        out_shape=[jax.ShapeDtypeStruct((256, 256), BF)] * 2,
        compiler_params=SMALL,
        name="merge",
    )(parts)


UP = [(i, (i + 1) % 8) for i in range(8)]
DOWN = [(i, (i - 1) % 8) for i in range(8)]


def ring(pair, take, due=()):
    right = left = list(pair)
    state = take(None, [pair], [0])
    for step in range(1, 4):
        right = [lax.ppermute(a, "tp", UP) for a in right]
        left = [lax.ppermute(a, "tp", DOWN) for a in left]
        if step == 2:
            left[1], state, due = lax.optimization_barrier((left[1], state, due))
        else:
            left[1], state = lax.optimization_barrier((left[1], state))
        state = take(state, [right, left], [8 - step, step])
    return [lax.ppermute(right[0], "tp", UP), lax.ppermute(left[1], "tp", DOWN)], state, due


SHIFTS = [0, 7, 1, 6, 2, 5, 3, 4]


def pack_kernel(place, own_x, send_x, gates, own_ref, send_ref):
    row = gates[pl.ds(place[6], 1), :]
    diagonal = lax.broadcasted_iota(jnp.int32, (320, 320), 0) == lax.broadcasted_iota(jnp.int32, (320, 320), 1)
    gate = jnp.sum(jnp.where(diagonal, row, 0.0), axis=1, keepdims=True)
    one = gate.astype(BF).astype(F32)
    two = (gate - one).astype(BF).astype(F32)
    lane = lax.broadcasted_iota(jnp.int32, (320, HEAD), 1)
    terms = jnp.where(lane == 0, one, jnp.where(lane == 1, two, jnp.where(lane == 2, gate - one - two, 0.0)))
    for x, out in ((own_x, own_ref), (send_x, send_ref)):
        out[:, :256] = x[...]
        out[:, 256:] = terms.astype(BF)


def pack(place, x, gates):
    return pl.pallas_call(
        pack_kernel,
        grid_spec=pltpu.PrefetchScalarGridSpec(
            num_scalar_prefetch=1,
            grid=(1,),
            in_specs=[
                pl.BlockSpec((320, 256), lambda i, s: (0, s[4])),
                pl.BlockSpec((320, 256), lambda i, s: (0, 1 - s[4])),
                pl.BlockSpec(gates.shape, lambda i, s: (0, 0)),
            ],
            out_specs=[pl.BlockSpec((320, 384), lambda i, s: (0, 0))] * 2,
        ),
        out_shape=[jax.ShapeDtypeStruct((320, 384), BF)] * 2,
        compiler_params=SMALL,
        name="pack",
    )(place, x, x, gates)


def mix_add(place, pairs, shifts, w_own, w_one, w_two, acc):
    core, z = place[0], place[3]
    for (low, up), shift in zip(pairs, shifts):
        source = (z + shift) % 8
        first = pl.ds(pl.multiple_of(source * 256, 256), 256)
        second = pl.ds(pl.multiple_of(2048 + source * 256, 256), 256)
        low, up = low[...], up[...]

        def add(w):
            return jnp.dot(w[:, first], low, preferred_element_type=F32) + jnp.dot(
                w[:, second], up, preferred_element_type=F32
            )

        acc[:320] += add(w_own)
        acc[pl.ds(pl.multiple_of(320 + core * 160, 32), 160)] += add(w_one)
        acc[pl.ds(pl.multiple_of(480 - core * 160, 32), 160)] += add(w_two)


def mix_near_kernel(shifts, place, *refs):
    count = len(shifts)
    pairs = [refs[2 * i : 2 * i + 2] for i in range(count)]
    w_own, w_one, w_two, before, acc = refs[2 * count :]
    acc[...] = before[...]
    mix_add(place, pairs, shifts, w_own, w_one, w_two, acc)


def mix_first_kernel(place, low, up, w_own, w_one, w_two, acc):
    acc[...] = jnp.zeros_like(acc)
    mix_add(place, [(low, up)], [0], w_own, w_one, w_two, acc)


def mix_near(place, weights, state, pairs, shifts):
    operands = [a for pair in pairs for a in pair] + list(weights)
    if state is None:
        kernel = mix_first_kernel
    else:
        kernel = functools.partial(mix_near_kernel, shifts)
        operands.append(state)
    return pl.pallas_call(
        kernel,
        in_specs=[SMEM] + [VMEM] * len(operands),
        out_specs=VMEM,
        out_shape=jax.ShapeDtypeStruct((640, 256), F32),
        compiler_params=SMALL,
        cost_estimate=pl.CostEstimate(
            flops=2 * 256 * 512 * 640 * len(pairs), bytes_accessed=1 << 20, transcendentals=0
        ),
        name="mix_near",
    )(place, *operands)


def mix_far_kernel(place, low, up, w_own, w_one, w_two, near, own_x, other_x, own, other, acc):
    acc[...] = near[...]
    mix_add(place, [(low, up)], [4], w_own, w_one, w_two, acc)
    for x, begin, out in ((own_x, 0, own), (other_x, 320, other)):
        gate = jnp.sum(x[:, 256:].astype(F32), axis=1, keepdims=True)
        out[...] = (x[:, :256].astype(F32) + gate * acc[begin : begin + 320]).astype(BF)


def mix_far(place, far, weights, near, own_x, other_x):
    return pl.pallas_call(
        mix_far_kernel,
        in_specs=[SMEM] + [VMEM] * 8,
        out_specs=[VMEM] * 2,
        out_shape=[jax.ShapeDtypeStruct((320, 256), BF)] * 2,
        scratch_shapes=[pltpu.VMEM((640, 256), F32)],
        compiler_params=SMALL,
        name="mix_far",
    )(place, *far, *weights, near, own_x, other_x)


def stream_kernel(count, place, *refs):
    pieces = refs[: 2 * count]
    refs = refs[2 * count :]
    if count == 1:
        gain, bias, out_ref, sums_ref, terms = refs
        first = place[4] == 0
        for i, ref in enumerate((gain, bias)):
            for j in range(8):
                low = ref[:, j * 320 : (j + 1) * 320]
                up = ref[:, 2560 + j * 320 : 2560 + (j + 1) * 320]
                terms[i, j : j + 1, :320] = jnp.where(first, low, up)
                terms[i, j : j + 1, 320:] = jnp.where(first, up, low)
        total = jnp.zeros((1, 256), F32)
        square = jnp.zeros((1, 256), F32)
    else:
        before, out_ref, sums_ref = refs
        total, square = before[0:1], before[1:2]
    for i, ref in enumerate(pieces):
        x = ref[...]
        begin = i % 2 * 320
        out_ref[i // 2, :, begin : begin + 320] = jnp.transpose(x)
        x = x.astype(F32)
        total += jnp.sum(x, axis=0, keepdims=True)
        square += jnp.sum(x * x, axis=0, keepdims=True)
    rank = lax.broadcasted_iota(jnp.int32, (8, 256), 0)
    sums_ref[...] = jnp.where(rank == 0, total, jnp.where(rank == 1, square, 0.0))


def stream(place, gain, bias, state, pairs, shifts):
    count = len(pairs)
    operands = [a for pair in pairs for a in pair]
    out_shape = [jax.ShapeDtypeStruct((count, 256, 640), BF), jax.ShapeDtypeStruct((8, 256), F32)]
    if state is None:
        operands += [gain, bias]
        out_shape.append(jax.ShapeDtypeStruct((2, 8, 640), F32))
    else:
        operands.append(state[-2])
    outs = pl.pallas_call(
        functools.partial(stream_kernel, count),
        in_specs=[SMEM] + [VMEM] * len(operands),
        out_specs=[VMEM] * len(out_shape),
        out_shape=out_shape,
        compiler_params=SMALL,
        cost_estimate=pl.CostEstimate(flops=1 << 22, bytes_accessed=2 << 20, transcendentals=0),
        name="stream",
    )(place, *operands)
    if state is None:
        return outs
    return [*state[:-2], outs[0], outs[1], state[-1]]


def query_kernel(
    place, near_a, near_b, near_c, near_d, near_sums, terms, far_own, far_other, w_own, w_one, w_two, key_sums, raw_ref, sums_ref, last, weight, acc
):
    z, enc = place[3], place[4]
    total = near_sums[0:1]
    square = near_sums[1:2]
    for i, ref in enumerate((far_own, far_other)):
        x = ref[...]
        last[:, i * 320 : (i + 1) * 320] = jnp.transpose(x)
        x = x.astype(F32)
        total += jnp.sum(x, axis=0, keepdims=True)
        square += jnp.sum(x * x, axis=0, keepdims=True)
    mean = total * (1.0 / 5120)
    scale = lax.rsqrt(square * (1.0 / 5120) - mean * mean + EPS)
    mean = jnp.transpose(jnp.broadcast_to(mean, (HEAD, 256)))[:, :1]
    scale = jnp.transpose(jnp.broadcast_to(scale, (HEAD, 256)))[:, :1]
    blocks = [near_a[0]] + [ref[i] for ref in (near_b, near_c, near_d) for i in range(2)] + [last[...]]
    for step, x in enumerate(blocks):
        source = (z + SHIFTS[step]) % 8
        row = pl.ds(source, 1)
        normed = ((x.astype(F32) - mean) * scale * terms[0, row, :] + terms[1, row, :]).astype(BF)
        slot = step % 2
        for i in range(2):
            rows = pl.ds(pl.multiple_of((enc + i) % 2 * 2560 + source * 320, 64), 320)
            to = slice(i * 320, (i + 1) * 320)
            weight[slot, to, :256] = w_own[rows, :]
            weight[slot, to, 256:384] = w_one[rows, :]
            weight[slot, to, 384:] = w_two[rows, :]
        update = jnp.dot(normed, weight[slot], preferred_element_type=F32)
        acc[...] = update if step == 0 else acc[...] + update
    raw = acc[...]
    raw_ref[...] = raw
    square = raw * raw
    part = square[:, :HEAD]
    for j in range(HEAD, 512, HEAD):
        part += square[:, j : j + HEAD]
    line = jnp.sum(jnp.transpose(part), axis=0, keepdims=True)
    rank = lax.broadcasted_iota(jnp.int32, (8, HEAD), 0)
    line = jnp.where(rank == 0, line[:, :HEAD], jnp.where(rank == 1, line[:, HEAD:], key_sums[...]))
    for i in range(16):
        sums_ref[i] = line


def query(place, turned, far, w_own, w_one, w_two, key_sums):
    return pl.pallas_call(
        query_kernel,
        in_specs=[SMEM] + [VMEM] * 12,
        out_specs=[VMEM] * 2,
        out_shape=[
            jax.ShapeDtypeStruct((256, 512), F32),
            jax.ShapeDtypeStruct((16, 8, HEAD), F32),
        ],
        scratch_shapes=[
            pltpu.VMEM((256, 640), BF),
            pltpu.VMEM((2, 640, 512), BF),
            pltpu.VMEM((256, 512), F32),
        ],
        compiler_params=SMALL,
        cost_estimate=pl.CostEstimate(flops=2 * 256 * 5120 * 512, bytes_accessed=1 << 20, transcendentals=0),
        name="query",
    )(place, *turned, *far, w_own, w_one, w_two, key_sums)


def cross_kernel(partner, place, raw_ref, sums_ref, text_ref, out):
    core, enc, length = place[0], place[4], place[5]
    queries = jnp.zeros((8, HEAD), F32)
    keys = jnp.zeros((8, HEAD), F32)
    for i in range(8):
        low, up = sums_ref[i], sums_ref[8 + i]
        queries += jnp.where(enc == 0, low, up)
        keys += low + up
    factor_q = lax.rsqrt(queries * (1.0 / 4096) + EPS)
    factor_k = lax.rsqrt(keys * (1.0 / 4096) + EPS) * SCALE2
    column = jnp.concatenate(
        [jnp.transpose(jnp.broadcast_to(factor_q[i : i + 1], (HEAD, HEAD))) for i in range(2)], axis=0
    )
    line = jnp.concatenate([factor_k[2 + i : 3 + i] for i in range(4)], axis=1)
    live = lax.broadcasted_iota(jnp.int32, (256, 512), 1) < length
    for index in range(2):
        if partner:
            lanes = pl.ds(pl.multiple_of((core + index) % 2 * HEAD, HEAD), HEAD)
        else:
            lanes = slice(index * HEAD, (index + 1) * HEAD)
        begin = index * HEAD + (256 if partner else 0)
        q = (raw_ref[:, begin : begin + HEAD] * column).astype(BF)
        s = lax.dot_general(q, text_ref[0, :, lanes], NT, preferred_element_type=F32) * line
        s = jnp.where(live, s, -1e30)
        p = jnp.exp2(s - jnp.max(s, axis=1, keepdims=True))
        total = jnp.sum(p, axis=1, keepdims=True)
        o = jnp.dot(p.astype(BF), text_ref[1, :, lanes], preferred_element_type=F32)
        out[:, lanes] = (o / total).astype(BF)


def cross(place, raw, sums, text, partner):
    return pl.pallas_call(
        functools.partial(cross_kernel, partner),
        in_specs=[SMEM] + [VMEM] * 3,
        out_specs=VMEM,
        out_shape=jax.ShapeDtypeStruct((256, 256), BF),
        compiler_params=SMALL,
        name="cross",
    )(place, raw, sums, text)


def on_device(
    x_res,
    q_proj,
    k_proj,
    v_proj,
    w_out,
    gate_table,
    timestep,
    norm_gain,
    norm_bias,
    w_query,
    context,
    w_key,
    w_value,
    gain_cq,
    gain_ck,
    text_len,
):
    e = lax.axis_index("enc")
    c = lax.axis_index("core")
    y = lax.axis_index("yh")
    z = lax.axis_index("tp")
    seq = (lax.axis_index("x") * 2 + y) * 2 + c
    place = jnp.stack([c, seq, y, z, e, text_len[0], timestep[0]]).astype(jnp.int32)
    swap = [(0, 1), (1, 0)]
    x_up = [(i, (i + 1) % 4) for i in range(4)]
    x_down = [(i, (i - 1) % 4) for i in range(4)]

    text = lax.ppermute(context, "enc", swap)
    gain_k, gain_q = gain_ck.reshape(1, 256), gain_cq.reshape(1, 256)
    mine, text, send = front(
        place, q_proj, k_proj, v_proj, w_key, w_value, context, text, gain_k, gain_q
    )
    kv, q_own, text_near = join(mine, text, lax.ppermute(send, "core", swap))
    q_far = lax.ppermute(q_own, "yh", swap)
    kv_left = lax.ppermute(kv, "x", x_up)
    kv_right = lax.ppermute(kv, "x", x_down)
    w_mine = w_out.T
    state = attend(place, [q_own], [kv])
    w_source, x_source, state = lax.optimization_barrier((w_mine, x_res.T, state))
    w_send = take_half(place, w_source, 0)
    x_own, x_send = pack(place, x_source, gate_table)
    q_far, state = lax.optimization_barrier((q_far, state))
    state = attend(place, [q_far], [kv], into=state, slot=1)
    way = [(i * 2 + j, (i + 1 - 2 * j) % 4 * 2 + j) for i in range(4) for j in range(2)]
    kv_far = lax.ppermute(pick(place, kv_left, kv_right), ("x", "core"), way)
    *state, text_near = attend(place, [q_own, q_far], [kv_left, kv_right], state, text=text_near)
    sent, text_near = attend(place, [q_own, q_far], [kv_far], state, last=True, text=text_near)

    w_send, x_send, q_far = lax.optimization_barrier((w_send, x_send, q_far))
    x_other = lax.ppermute(x_send, "enc", swap)
    w_one = lax.ppermute(w_send, "enc", swap)
    sent, x_other = lax.optimization_barrier((sent, x_other))
    parts = lax.all_to_all(sent, ("yh", "core", "enc"), 0, 0, tiled=True)

    q_source, _ = lax.optimization_barrier((w_query, sent))
    q_send = take_half(place, q_source, 1)
    parts, q_send = lax.optimization_barrier((parts, q_send))
    heads = merge(parts)
    heads, w_one = lax.optimization_barrier((heads, w_one))
    w_two = lax.ppermute(w_one, "core", swap)
    text_far = lax.ppermute(text_near, "yh", swap)
    q_one = lax.ppermute(q_send, "enc", swap)

    weights = (w_mine, w_one, w_two)
    far, acc, _ = ring(heads, functools.partial(mix_near, place, weights))
    mixed = mix_far(place, far, weights, acc, x_own, x_other)

    q_one, text_far, mixed = lax.optimization_barrier((q_one, text_far, mixed))
    q_two = lax.ppermute(q_one, "core", swap)
    text_own, key_sums = text_place(place, text_near, text_far, gain_k, gain_q)
    text_other = lax.ppermute(text_own, "enc", swap)
    mixed_own, mixed_other = mixed
    far, turned, text_own = ring(
        mixed, functools.partial(stream, place, norm_gain.reshape(1, 5120), norm_bias.reshape(1, 5120)), text_own
    )
    mixed_back = lax.ppermute(mixed_other, "enc", swap)
    raw, sums = query(place, turned, far, w_query, q_one, q_two, key_sums)
    sums = lax.all_to_all(sums, ("enc", "tp"), 0, 0, tiled=True)
    cross_other = cross(place, raw, sums, text_other, True)
    cross_back = lax.ppermute(cross_other, "enc", swap)
    cross_own = cross(place, raw, sums, text_own, False)

    def assemble(own, back, axis):
        return jnp.where(
            e == 0, jnp.concatenate([own, back], axis=axis), jnp.concatenate([back, own], axis=axis)
        )

    return (assemble(mixed_own, mixed_back, 1).T, assemble(cross_own, cross_back, 0))


def solution(mesh):
    parts = Mesh(mesh.devices.reshape(2, 4, 2, 2, 8), ("enc", "x", "yh", "core", "tp"))
    seq = ("x", "yh", "core")
    feat = ("enc", "tp")
    placed = (
        P(seq, feat),
        P(seq, feat),
        P(seq, feat),
        P(seq, feat),
        P(None, feat),
        P(None, feat),
        P(),
        P(),
        P(),
        P(None, feat),
        P(("enc", "x", "yh", "core"), None),
        P(None, feat),
        P(None, feat),
        P(feat),
        P(feat),
        P(),
    )
    return jax.shard_map(
        on_device,
        mesh=parts,
        in_specs=placed,
        out_specs=(P(seq, feat), P(seq, feat)),
        check_vma=False,
    )
```

```python
import functools

import jax
import jax.numpy as jnp
import numpy as np
from jax import lax
from jax.experimental import pallas as pl
from jax.experimental.pallas import tpu as pltpu
from jax.sharding import Mesh, PartitionSpec as P

HEAD = 128
GRID_H = 45
GRID_W = 80
EPS = 1e-06
THETA = 10000.0
LOG2E = 1.4426950408889634
SCALE2 = LOG2E * HEAD**-0.5
BF = jnp.bfloat16
F32 = jnp.float32
NT = (((1,), (1,)), ((), ()))
PARAMS = pltpu.CompilerParams(vmem_limit_bytes=16 * 1024 * 1024)
LARGE = pltpu.CompilerParams(vmem_limit_bytes=60 * 1024 * 1024)
SMALL = pltpu.CompilerParams(vmem_limit_bytes=8 * 1024 * 1024)
VMEM = pl.BlockSpec(memory_space=pltpu.VMEM)
SMEM = pl.BlockSpec(memory_space=pltpu.SMEM)
HBM = pl.BlockSpec(memory_space=pltpu.HBM)
PART = 1152


def frequencies():
    part_time = HEAD - 4 * (HEAD // 6)
    part_space = 2 * (HEAD // 6)
    time = THETA ** (-np.arange(0, part_time, 2).astype(np.float32) / part_time)
    space = THETA ** (-np.arange(0, part_space, 2).astype(np.float32) / part_space)
    pairs = np.concatenate([time, space, space]).astype(np.float32)
    return np.repeat(pairs, 2)[None, :]


def rope_kernel(place, q_hbm, k_hbm, v_hbm, freq_ref, mine_ref, send_ref, held, sems):
    copies = [pltpu.make_async_copy(ref, held.at[i], sems.at[i]) for i, ref in enumerate((q_hbm, k_hbm, v_hbm))]
    for copy in copies:
        copy.start()
    core = place[0]
    shape = (512, HEAD)
    position = (place[1] * 512 + lax.broadcasted_iota(jnp.int32, shape, 0)).astype(F32)
    lane = lax.broadcasted_iota(jnp.int32, shape, 1)
    line = jnp.floor((position + 0.5) * (1.0 / GRID_W))
    column = position - line * GRID_W
    frame = jnp.floor((line + 0.5) * (1.0 / GRID_H))
    row = line - frame * GRID_H
    part_time = HEAD - 4 * (HEAD // 6)
    part_space = 2 * (HEAD // 6)
    axis = jnp.where(lane < part_time, frame, jnp.where(lane < part_time + part_space, row, column))
    angles = axis * freq_ref[...]
    even = lane % 2 == 0
    cosine = jnp.cos(angles)
    sine = jnp.sin(angles)
    sine = jnp.where(even, -sine, sine)
    first = core == 0
    for index in range(3):
        copies[index].wait()
        heads = []
        for head in range(2):
            x = held[index, :, head * HEAD : (head + 1) * HEAD]
            if index < 2:
                x = x.astype(F32)
                partner = jnp.where(even, pltpu.roll(x, HEAD - 1, 1), pltpu.roll(x, 1, 1))
                x = (x * cosine + partner * sine).astype(BF)
            heads.append(x)
        mine_ref[index * 512 : (index + 1) * 512, :] = jnp.where(first, heads[0], heads[1])
        send_ref[index * 512 : (index + 1) * 512, :] = jnp.where(first, heads[1], heads[0])
    send_ref[1536:, :] = jnp.zeros((HEAD, HEAD), BF)


def rope(place, q, k, v):
    return pl.pallas_call(
        rope_kernel,
        in_specs=[SMEM, HBM, HBM, HBM, VMEM],
        out_specs=[VMEM] * 2,
        out_shape=[jax.ShapeDtypeStruct((1536, HEAD), BF), jax.ShapeDtypeStruct((1664, HEAD), BF)],
        scratch_shapes=[pltpu.VMEM((3, 512, 256), BF), pltpu.SemaphoreType.DMA((3,))],
        compiler_params=LARGE,
        name="rope",
    )(place, q, k, v, frequencies())


def text_kernel(
    place, own, other, key_hbm, value_hbm, gain_k, gain_q, send_in, text_ref, send_ref, weights, block, sems, out_sem
):
    depth = weights.shape[2]
    loads = {}
    for i in range(4):
        for kind, ref in enumerate((key_hbm, value_hbm)):
            loads[kind, i] = pltpu.make_async_copy(
                ref.at[pl.ds(i * depth, depth)], weights.at[kind, i], sems.at[kind, i]
            )
            loads[kind, i].start()
    first = place[4] == 0
    own, other = own[...], other[...]
    text = jnp.concatenate([jnp.where(first, own, other), jnp.where(first, other, own)], axis=0)
    sums = [jnp.zeros((32, 256), F32)] * 2
    for i in range(4):
        for kind in range(2):
            loads[kind, i].wait()
            sums[kind] += jnp.dot(
                text[:, i * depth : (i + 1) * depth], weights[kind, i], preferred_element_type=F32
            )
    sums[0] = sums[0] * (gain_k[...] * gain_q[...])
    for kind in range(2):
        for head in range(2):
            begin = (kind * 2 + head) * 32
            block[begin : begin + 32, :] = sums[kind][:, head * HEAD : (head + 1) * HEAD].astype(BF)
    copy = pltpu.make_async_copy(block, send_ref.at[pl.ds(1536, HEAD)], out_sem)
    copy.start()
    text_ref[...] = block[...]
    copy.wait()


def text_part(place, own, other, w_key, w_value, gain_k, gain_q, send):
    return pl.pallas_call(
        text_kernel,
        in_specs=[SMEM, VMEM, VMEM, HBM, HBM, VMEM, VMEM, HBM],
        out_specs=[VMEM, HBM],
        out_shape=[jax.ShapeDtypeStruct((HEAD, HEAD), BF), jax.ShapeDtypeStruct((1664, HEAD), BF)],
        input_output_aliases={7: 1},
        scratch_shapes=[
            pltpu.VMEM((2, 4, 1280, 256), BF),
            pltpu.VMEM((HEAD, HEAD), BF),
            pltpu.SemaphoreType.DMA((2, 4)),
            pltpu.SemaphoreType.DMA,
        ],
        compiler_params=LARGE,
        name="text_part",
    )(place, own, other, w_key, w_value, gain_k, gain_q, send)


def join_kernel(mine, text, other, kv_ref, q_ref, text_ref):
    text_ref[:HEAD, :] = text[...]
    text_ref[HEAD:, :] = other[1536:, :]
    q_ref[:512, :] = mine[:512, :]
    q_ref[512:, :] = other[:512, :]
    kv_ref[:1024, :] = mine[512:, :]
    kv_ref[1024:PART, :] = text[...]
    kv_ref[PART:, :] = other[512:, :]


def join(mine, text, other):
    return pl.pallas_call(
        join_kernel,
        in_specs=[VMEM] * 3,
        out_specs=[VMEM] * 3,
        out_shape=[
            jax.ShapeDtypeStruct((2 * PART, HEAD), BF),
            jax.ShapeDtypeStruct((1024, HEAD), BF),
            jax.ShapeDtypeStruct((2 * HEAD, HEAD), BF),
        ],
        compiler_params=SMALL,
        name="join",
    )(mine, text, other)


def take_kernel(place, ref, out):
    out[...] = ref[...]


def take_half(place, array, axis):
    shape = tuple(n // 2 if i == axis else n for i, n in enumerate(array.shape))
    return pl.pallas_call(
        take_kernel,
        grid_spec=pltpu.PrefetchScalarGridSpec(
            num_scalar_prefetch=1,
            grid=(1,),
            in_specs=[pl.BlockSpec(shape, lambda i, s: (s[0], 0) if axis == 0 else (0, s[0]))],
            out_specs=pl.BlockSpec(shape, lambda i, s: (0, 0)),
        ),
        out_shape=jax.ShapeDtypeStruct(shape, BF),
        compiler_params=SMALL,
        name="take_half",
    )(place, array)


def pick_kernel(place, first, second, out):
    @pl.when(place[0] == 0)
    def _():
        out[...] = first[...]

    @pl.when(place[0] != 0)
    def _():
        out[...] = second[...]


def pick(place, first, second):
    return pl.pallas_call(
        pick_kernel,
        in_specs=[SMEM, VMEM, VMEM],
        out_specs=VMEM,
        out_shape=jax.ShapeDtypeStruct(first.shape, BF),
        compiler_params=SMALL,
        name="pick",
    )(place, first, second)


def text_place_kernel(place, near, far, gain_k, gain_q, mixed, out_ref, sums_ref):
    out_ref[1024:, :] = mixed[...]
    core, seq = place[0], place[1]
    x = seq // 4
    y = place[2]
    for group, ref in ((0, near), (1, far)):
        for index in range(8):
            column = (x + (0, 3, 1, 2)[index // 2]) % 4
            device = (column * 2 + (y + group) % 2) * 2 + (core + index % 2) % 2
            for kind in range(2):
                for head in range(2):
                    for enc in range(2):
                        begin = index * HEAD + (kind * 2 + head) * 32 + enc * 16
                        rows = pl.ds(pl.multiple_of(kind * 512 + enc * 256 + device * 16, 16), 16)
                        out_ref[rows, head * HEAD : (head + 1) * HEAD] = ref[begin : begin + 16, :]
    keys = out_ref[:512, :].astype(F32) / (gain_k[...] * gain_q[...])
    square = keys[:, :HEAD] * keys[:, :HEAD] + keys[:, HEAD:] * keys[:, HEAD:]
    line = jnp.sum(jnp.transpose(square), axis=0, keepdims=True)
    rank = lax.broadcasted_iota(jnp.int32, (8, HEAD), 0)
    rows = jnp.zeros((8, HEAD), F32)
    for i in range(4):
        rows = jnp.where(rank == 2 + i, line[:, i * HEAD : (i + 1) * HEAD], rows)
    sums_ref[...] = rows


def text_place(place, near, far, gain_k, gain_q, mixed):
    return pl.pallas_call(
        text_place_kernel,
        in_specs=[SMEM] + [VMEM] * 5,
        out_specs=[VMEM, VMEM],
        out_shape=[jax.ShapeDtypeStruct((1344, 256), BF), jax.ShapeDtypeStruct((8, HEAD), F32)],
        compiler_params=SMALL,
        name="text_place",
    )(place, near, far, gain_k, gain_q, mixed)


def attend_kernel(count, first, last, skip, single, texts, place, *refs):
    if single:
        refs = (refs[0], None) + refs[1:]
    q_low, q_up, kvs = refs[0], refs[1], refs[2 : 2 + count]
    refs = refs[2 + count :]
    if not first:
        acc_in, high_in = refs[:2]
        refs = refs[2:]
    refs = refs[skip:]
    if texts:
        text_in, refs = refs[0], refs[1:]
        text_out = refs[-2]
        refs = refs[:-2] + refs[-1:]
        before = texts * HEAD
        text_out[:before, :] = text_in[...]
        for kv in kvs:
            for i in range(0, kv.shape[0], PART):
                text_out[before : before + HEAD, :] = kv[i + 1024 : i + PART, :]
                before += HEAD
    if last:
        out_ref, wide = refs
    else:
        acc_out, high_out, wide = refs
    chunk = 512
    sub = 256

    @pl.when(pl.program_id(0) == 0)
    def _():
        base = 0
        for kv in kvs:
            for i in range(0, kv.shape[0], PART):
                wide[pl.ds(base, chunk), :HEAD] = kv[i + 512 : i + 1024, :]
                wide[pl.ds(base, chunk), HEAD:] = jnp.ones((chunk, HEAD), BF)
                base += chunk

    def score(begin):
        q = q_low[pl.ds(begin, sub), :]
        if q_up is not None:
            q = jnp.where(pl.program_id(0) == 0, q, q_up[pl.ds(begin, sub), :])
        return [
            lax.dot_general(q, kv[i : i + 512, :], NT, preferred_element_type=F32)
            for kv in kvs
            for i in range(0, kv.shape[0], PART)
        ]

    def finish(begin, scores):
        rows = pl.ds(begin, sub)
        high = None
        for s in scores:
            for j in range(0, chunk, HEAD):
                part = s[:, j : j + HEAD]
                high = part if high is None else jnp.maximum(high, part)
        high = jnp.max(high, axis=1, keepdims=True)
        acc = None
        if not first:
            before = high_in[rows, :1]
            high = jnp.maximum(before, high)
            acc = acc_in[rows, :] * jnp.exp2((before - high) * SCALE2)
        shift = high * SCALE2
        for i, s in enumerate(scores):
            p = jnp.exp2(s * SCALE2 - shift).astype(BF)
            update = jnp.dot(p, wide[pl.ds(i * chunk, chunk), :], preferred_element_type=F32)
            acc = update if acc is None else acc + update
        if not last:
            acc_out[rows, :] = acc
            high_out[rows, :] = jnp.broadcast_to(high, (sub, HEAD))
            return
        total = acc[:, HEAD:]
        block = (place[0] + begin // 512) % 2 * 2 + begin // sub % 2
        line = jnp.transpose(shift + jnp.log(total) * LOG2E)[:16, :]
        one = line.astype(BF).astype(F32)
        two = (line - one).astype(BF).astype(F32)
        three = line - one - two
        rank = lax.broadcasted_iota(jnp.int32, (16, sub), 0)
        packed = jnp.where(rank == 0, one, jnp.where(rank == 1, two, jnp.where(rank == 2, three, 0.0)))
        out_ref[pl.ds(block, 1), :HEAD, :] = jnp.transpose(acc[:, :HEAD] / total).astype(BF)[None]
        out_ref[pl.ds(block, 1), HEAD:, :] = packed.astype(BF)[None]

    begins = list(range(0, q_low.shape[0], sub))
    ahead = score(begins[0])
    for index, begin in enumerate(begins):
        scores = ahead
        if index + 1 < len(begins):
            ahead = score(begins[index + 1])
        finish(begin, scores)


def attend(place, qs, kvs, state=None, last=False, into=None, slot=0, text=None):
    total = len(qs) * 1024
    keys = sum(kv.shape[0] for kv in kvs) // PART * 512
    rows = 1024

    def row(width, at=0):
        return pl.BlockSpec((rows, width), lambda i, s: (i + at, 0))

    operands = [*qs, *kvs]
    specs = [pl.BlockSpec(a.shape, lambda i, s: (0, 0)) for a in operands]
    if state is not None:
        operands += list(state)
        specs += [row(256), row(HEAD)]
    aliases = {}
    if into is not None:
        aliases = {len(operands) + 1: 0, len(operands) + 2: 1}
        operands += list(into)
        specs += [pl.BlockSpec(memory_space=pl.ANY)] * 2
    if last:
        out_specs = [pl.BlockSpec((4, 144, 256), lambda i, s: ((s[2] + i) % 2, 0, 0))]
        out_shape = [jax.ShapeDtypeStruct((8, 144, 256), BF)]
    else:
        out_specs = [row(256, slot), row(HEAD, slot)]
        out_shape = [jax.ShapeDtypeStruct((2048, 256), F32), jax.ShapeDtypeStruct((2048, HEAD), F32)]
    texts = 0
    if text is not None:
        texts = text.shape[0] // HEAD
        operands.append(text)
        specs.append(pl.BlockSpec(text.shape, lambda i, s: (0, 0)))
        shape = (text.shape[0] + keys // 512 * HEAD, HEAD)
        out_specs = out_specs + [pl.BlockSpec(shape, lambda i, s: (0, 0))]
        out_shape = out_shape + [jax.ShapeDtypeStruct(shape, BF)]
    grid_spec = pltpu.PrefetchScalarGridSpec(
        num_scalar_prefetch=1,
        grid=(total // rows,),
        in_specs=specs,
        out_specs=out_specs,
        scratch_shapes=[pltpu.VMEM((keys, 256), BF)],
    )
    return pl.pallas_call(
        functools.partial(attend_kernel, len(kvs), state is None, last, 0 if into is None else 2, len(qs) == 1, texts),
        grid_spec=grid_spec,
        out_shape=out_shape,
        input_output_aliases=aliases,
        compiler_params=PARAMS,
        cost_estimate=pl.CostEstimate(
            flops=4 * total * keys * HEAD, bytes_accessed=4 * 1024 * 1024, transcendentals=total * keys
        ),
        name="attend",
    )(place, *operands)


def merge_kernel(in_ref, low_ref, up_ref):
    for head in range(4):
        enc, core = head // 2, head % 2
        sources = [half * 4 + core * 2 + enc for half in range(2)]
        logs = []
        for source in sources:
            lines = in_ref[source, HEAD:, :].astype(F32)
            logs.append(lines[0:1, :] + lines[1:2, :] + lines[2:3, :])
        first = in_ref[sources[0], :HEAD, :].astype(F32) / (1.0 + jnp.exp2(logs[1] - logs[0]))
        second = in_ref[sources[1], :HEAD, :].astype(F32) / (1.0 + jnp.exp2(logs[0] - logs[1]))
        out = low_ref if enc == 0 else up_ref
        out[core * HEAD : (core + 1) * HEAD, :] = (first + second).astype(BF)


def merge(parts):
    return pl.pallas_call(
        merge_kernel,
        in_specs=[VMEM],
        out_specs=[VMEM] * 2,
        out_shape=[jax.ShapeDtypeStruct((256, 256), BF)] * 2,
        compiler_params=SMALL,
        name="merge",
    )(parts)


UP = [(i, (i + 1) % 8) for i in range(8)]
DOWN = [(i, (i - 1) % 8) for i in range(8)]


def ring(pair, take, due=()):
    right = left = list(pair)
    state = take(None, [pair], [0])
    for step in range(1, 4):
        right = [lax.ppermute(a, "tp", UP) for a in right]
        left = [lax.ppermute(a, "tp", DOWN) for a in left]
        if step == 2:
            left[1], state, due = lax.optimization_barrier((left[1], state, due))
        else:
            left[1], state = lax.optimization_barrier((left[1], state))
        state = take(state, [right, left], [8 - step, step])
    return [lax.ppermute(right[0], "tp", UP), lax.ppermute(left[1], "tp", DOWN)], state, due


SHIFTS = [0, 7, 1, 6, 2, 5, 3, 4]


def pack_kernel(place, own_x, send_x, gates, own_ref, send_ref):
    row = gates[pl.ds(place[6], 1), :]
    diagonal = lax.broadcasted_iota(jnp.int32, (320, 320), 0) == lax.broadcasted_iota(jnp.int32, (320, 320), 1)
    gate = jnp.sum(jnp.where(diagonal, row, 0.0), axis=1, keepdims=True)
    one = gate.astype(BF).astype(F32)
    two = (gate - one).astype(BF).astype(F32)
    lane = lax.broadcasted_iota(jnp.int32, (320, HEAD), 1)
    terms = jnp.where(lane == 0, one, jnp.where(lane == 1, two, jnp.where(lane == 2, gate - one - two, 0.0)))
    for x, out in ((own_x, own_ref), (send_x, send_ref)):
        out[:, :256] = x[...]
        out[:, 256:] = terms.astype(BF)


def pack(place, x, gates):
    return pl.pallas_call(
        pack_kernel,
        grid_spec=pltpu.PrefetchScalarGridSpec(
            num_scalar_prefetch=1,
            grid=(1,),
            in_specs=[
                pl.BlockSpec((320, 256), lambda i, s: (0, s[4])),
                pl.BlockSpec((320, 256), lambda i, s: (0, 1 - s[4])),
                pl.BlockSpec(gates.shape, lambda i, s: (0, 0)),
            ],
            out_specs=[pl.BlockSpec((320, 384), lambda i, s: (0, 0))] * 2,
        ),
        out_shape=[jax.ShapeDtypeStruct((320, 384), BF)] * 2,
        compiler_params=SMALL,
        name="pack",
    )(place, x, x, gates)


def mix_add(place, pairs, shifts, w_own, w_one, w_two, acc):
    core, z = place[0], place[3]
    for (low, up), shift in zip(pairs, shifts):
        source = (z + shift) % 8
        first = pl.ds(pl.multiple_of(source * 256, 256), 256)
        second = pl.ds(pl.multiple_of(2048 + source * 256, 256), 256)
        low, up = low[...], up[...]

        def add(w):
            return jnp.dot(w[:, first], low, preferred_element_type=F32) + jnp.dot(
                w[:, second], up, preferred_element_type=F32
            )

        acc[:320] += add(w_own)
        acc[pl.ds(pl.multiple_of(320 + core * 160, 32), 160)] += add(w_one)
        acc[pl.ds(pl.multiple_of(480 - core * 160, 32), 160)] += add(w_two)


def mix_near_kernel(shifts, place, *refs):
    count = len(shifts)
    pairs = [refs[2 * i : 2 * i + 2] for i in range(count)]
    w_own, w_one, w_two, before, acc = refs[2 * count :]
    acc[...] = before[...]
    mix_add(place, pairs, shifts, w_own, w_one, w_two, acc)


def mix_first_kernel(place, low, up, w_own, w_one, w_two, acc):
    acc[...] = jnp.zeros_like(acc)
    mix_add(place, [(low, up)], [0], w_own, w_one, w_two, acc)


def mix_near(place, weights, state, pairs, shifts):
    operands = [a for pair in pairs for a in pair] + list(weights)
    if state is None:
        kernel = mix_first_kernel
    else:
        kernel = functools.partial(mix_near_kernel, shifts)
        operands.append(state)
    return pl.pallas_call(
        kernel,
        in_specs=[SMEM] + [VMEM] * len(operands),
        out_specs=VMEM,
        out_shape=jax.ShapeDtypeStruct((640, 256), F32),
        compiler_params=SMALL,
        cost_estimate=pl.CostEstimate(
            flops=2 * 256 * 512 * 640 * len(pairs), bytes_accessed=1 << 20, transcendentals=0
        ),
        name="mix_near",
    )(place, *operands)


def mix_far_kernel(place, low, up, w_own, w_one, w_two, near, own_x, other_x, own, other, acc):
    acc[...] = near[...]
    mix_add(place, [(low, up)], [4], w_own, w_one, w_two, acc)
    for x, begin, out in ((own_x, 0, own), (other_x, 320, other)):
        gate = jnp.sum(x[:, 256:].astype(F32), axis=1, keepdims=True)
        out[...] = (x[:, :256].astype(F32) + gate * acc[begin : begin + 320]).astype(BF)


def mix_far(place, far, weights, near, own_x, other_x):
    return pl.pallas_call(
        mix_far_kernel,
        in_specs=[SMEM] + [VMEM] * 8,
        out_specs=[VMEM] * 2,
        out_shape=[jax.ShapeDtypeStruct((320, 256), BF)] * 2,
        scratch_shapes=[pltpu.VMEM((640, 256), F32)],
        compiler_params=SMALL,
        name="mix_far",
    )(place, *far, *weights, near, own_x, other_x)


def stream_kernel(count, place, *refs):
    pieces = refs[: 2 * count]
    refs = refs[2 * count :]
    if count == 1:
        gain, bias, out_ref, sums_ref, terms = refs
        first = place[4] == 0
        for i, ref in enumerate((gain, bias)):
            for j in range(8):
                low = ref[:, j * 320 : (j + 1) * 320]
                up = ref[:, 2560 + j * 320 : 2560 + (j + 1) * 320]
                terms[i, j : j + 1, :320] = jnp.where(first, low, up)
                terms[i, j : j + 1, 320:] = jnp.where(first, up, low)
        total = jnp.zeros((1, 256), F32)
        square = jnp.zeros((1, 256), F32)
    else:
        before, out_ref, sums_ref = refs
        total, square = before[0:1], before[1:2]
    for i, ref in enumerate(pieces):
        x = ref[...]
        begin = i % 2 * 320
        out_ref[i // 2, :, begin : begin + 320] = jnp.transpose(x)
        x = x.astype(F32)
        total += jnp.sum(x, axis=0, keepdims=True)
        square += jnp.sum(x * x, axis=0, keepdims=True)
    rank = lax.broadcasted_iota(jnp.int32, (8, 256), 0)
    sums_ref[...] = jnp.where(rank == 0, total, jnp.where(rank == 1, square, 0.0))


def stream(place, gain, bias, state, pairs, shifts):
    count = len(pairs)
    operands = [a for pair in pairs for a in pair]
    out_shape = [jax.ShapeDtypeStruct((count, 256, 640), BF), jax.ShapeDtypeStruct((8, 256), F32)]
    if state is None:
        operands += [gain, bias]
        out_shape.append(jax.ShapeDtypeStruct((2, 8, 640), F32))
    else:
        operands.append(state[-2])
    outs = pl.pallas_call(
        functools.partial(stream_kernel, count),
        in_specs=[SMEM] + [VMEM] * len(operands),
        out_specs=[VMEM] * len(out_shape),
        out_shape=out_shape,
        compiler_params=SMALL,
        cost_estimate=pl.CostEstimate(flops=1 << 22, bytes_accessed=2 << 20, transcendentals=0),
        name="stream",
    )(place, *operands)
    if state is None:
        return outs
    return [*state[:-2], outs[0], outs[1], state[-1]]


def query_kernel(
    place, near_a, near_b, near_c, near_d, near_sums, terms, far_own, far_other, w_own, w_one, w_two, key_sums, raw_ref, sums_ref, last, weight, acc
):
    z, enc = place[3], place[4]
    total = near_sums[0:1]
    square = near_sums[1:2]
    for i, ref in enumerate((far_own, far_other)):
        x = ref[...]
        last[:, i * 320 : (i + 1) * 320] = jnp.transpose(x)
        x = x.astype(F32)
        total += jnp.sum(x, axis=0, keepdims=True)
        square += jnp.sum(x * x, axis=0, keepdims=True)
    mean = total * (1.0 / 5120)
    scale = lax.rsqrt(square * (1.0 / 5120) - mean * mean + EPS)
    mean = jnp.transpose(jnp.broadcast_to(mean, (HEAD, 256)))[:, :1]
    scale = jnp.transpose(jnp.broadcast_to(scale, (HEAD, 256)))[:, :1]
    blocks = [near_a[0]] + [ref[i] for ref in (near_b, near_c, near_d) for i in range(2)] + [last[...]]
    for step, x in enumerate(blocks):
        source = (z + SHIFTS[step]) % 8
        row = pl.ds(source, 1)
        normed = ((x.astype(F32) - mean) * scale * terms[0, row, :] + terms[1, row, :]).astype(BF)
        slot = step % 2
        for i in range(2):
            rows = pl.ds(pl.multiple_of((enc + i) % 2 * 2560 + source * 320, 64), 320)
            to = slice(i * 320, (i + 1) * 320)
            weight[slot, to, :256] = w_own[rows, :]
            weight[slot, to, 256:384] = w_one[rows, :]
            weight[slot, to, 384:] = w_two[rows, :]
        update = jnp.dot(normed, weight[slot], preferred_element_type=F32)
        acc[...] = update if step == 0 else acc[...] + update
    raw = acc[...]
    raw_ref[...] = raw
    square = raw * raw
    part = square[:, :HEAD]
    for j in range(HEAD, 512, HEAD):
        part += square[:, j : j + HEAD]
    line = jnp.sum(jnp.transpose(part), axis=0, keepdims=True)
    rank = lax.broadcasted_iota(jnp.int32, (8, HEAD), 0)
    line = jnp.where(rank == 0, line[:, :HEAD], jnp.where(rank == 1, line[:, HEAD:], key_sums[...]))
    for i in range(16):
        sums_ref[i] = line


def query(place, turned, far, w_own, w_one, w_two, key_sums):
    return pl.pallas_call(
        query_kernel,
        in_specs=[SMEM] + [VMEM] * 12,
        out_specs=[VMEM] * 2,
        out_shape=[
            jax.ShapeDtypeStruct((256, 512), F32),
            jax.ShapeDtypeStruct((16, 8, HEAD), F32),
        ],
        scratch_shapes=[
            pltpu.VMEM((256, 640), BF),
            pltpu.VMEM((2, 640, 512), BF),
            pltpu.VMEM((256, 512), F32),
        ],
        compiler_params=SMALL,
        cost_estimate=pl.CostEstimate(flops=2 * 256 * 5120 * 512, bytes_accessed=1 << 20, transcendentals=0),
        name="query",
    )(place, *turned, *far, w_own, w_one, w_two, key_sums)


def cross_kernel(partner, place, raw_ref, sums_ref, text_ref, out):
    core, enc, length = place[0], place[4], place[5]
    queries = jnp.zeros((8, HEAD), F32)
    keys = jnp.zeros((8, HEAD), F32)
    for i in range(8):
        low, up = sums_ref[i], sums_ref[8 + i]
        queries += jnp.where(enc == 0, low, up)
        keys += low + up
    factor_q = lax.rsqrt(queries * (1.0 / 4096) + EPS)
    factor_k = lax.rsqrt(keys * (1.0 / 4096) + EPS) * SCALE2
    column = jnp.concatenate(
        [jnp.transpose(jnp.broadcast_to(factor_q[i : i + 1], (HEAD, HEAD))) for i in range(2)], axis=0
    )
    line = jnp.concatenate([factor_k[2 + i : 3 + i] for i in range(4)], axis=1)
    live = lax.broadcasted_iota(jnp.int32, (256, 512), 1) < length
    for index in range(2):
        if partner:
            lanes = pl.ds(pl.multiple_of((core + index) % 2 * HEAD, HEAD), HEAD)
        else:
            lanes = slice(index * HEAD, (index + 1) * HEAD)
        begin = index * HEAD + (256 if partner else 0)
        q = (raw_ref[:, begin : begin + HEAD] * column).astype(BF)
        s = lax.dot_general(q, text_ref[:512, lanes], NT, preferred_element_type=F32) * line
        s = jnp.where(live, s, -1e30)
        p = jnp.exp2(s - jnp.max(s, axis=1, keepdims=True))
        total = jnp.sum(p, axis=1, keepdims=True)
        o = jnp.dot(p.astype(BF), text_ref[512:1024, lanes], preferred_element_type=F32)
        out[:, lanes] = (o / total).astype(BF)


def cross(place, raw, sums, text, partner):
    return pl.pallas_call(
        functools.partial(cross_kernel, partner),
        in_specs=[SMEM] + [VMEM] * 3,
        out_specs=VMEM,
        out_shape=jax.ShapeDtypeStruct((256, 256), BF),
        compiler_params=SMALL,
        name="cross",
    )(place, raw, sums, text)


def on_device(
    x_res,
    q_proj,
    k_proj,
    v_proj,
    w_out,
    gate_table,
    timestep,
    norm_gain,
    norm_bias,
    w_query,
    context,
    w_key,
    w_value,
    gain_cq,
    gain_ck,
    text_len,
):
    e = lax.axis_index("enc")
    c = lax.axis_index("core")
    y = lax.axis_index("yh")
    z = lax.axis_index("tp")
    seq = (lax.axis_index("x") * 2 + y) * 2 + c
    place = jnp.stack([c, seq, y, z, e, text_len[0], timestep[0]]).astype(jnp.int32)
    swap = [(0, 1), (1, 0)]
    x_up = [(i, (i + 1) % 4) for i in range(4)]
    x_down = [(i, (i - 1) % 4) for i in range(4)]

    text = lax.ppermute(context, "enc", swap)
    gain_k, gain_q = gain_ck.reshape(1, 256), gain_cq.reshape(1, 256)
    mine, send = rope(place, q_proj, k_proj, v_proj)
    text, send = text_part(place, context, text, w_key, w_value, gain_k, gain_q, send)
    kv, q_own, text_near = join(mine, text, lax.ppermute(send, "core", swap))
    q_far = lax.ppermute(q_own, "yh", swap)
    kv_left = lax.ppermute(kv, "x", x_up)
    kv_right = lax.ppermute(kv, "x", x_down)
    w_mine = w_out.T
    state = attend(place, [q_own], [kv])
    w_source, x_source, state = lax.optimization_barrier((w_mine, x_res.T, state))
    w_send = take_half(place, w_source, 0)
    x_own, x_send = pack(place, x_source, gate_table)
    q_far, state = lax.optimization_barrier((q_far, state))
    state = attend(place, [q_far], [kv], into=state, slot=1)
    way = [(i * 2 + j, (i + 1 - 2 * j) % 4 * 2 + j) for i in range(4) for j in range(2)]
    kv_far = lax.ppermute(pick(place, kv_left, kv_right), ("x", "core"), way)
    *state, text_near = attend(place, [q_own, q_far], [kv_left, kv_right], state, text=text_near)
    sent, text_near = attend(place, [q_own, q_far], [kv_far], state, last=True, text=text_near)

    across = [
        (e * 4 + y * 2 + c, (1 - e) * 4 + (y + c) % 2 * 2 + c) for e in range(2) for y in range(2) for c in range(2)
    ]
    w_send, x_send, q_far = lax.optimization_barrier((w_send, x_send, q_far))
    x_other = lax.ppermute(x_send, "enc", swap)
    w_one = lax.ppermute(w_send, ("enc", "yh", "core"), across)
    parts = lax.all_to_all(sent, ("yh", "core", "enc"), 0, 0, tiled=True)

    q_source, _ = lax.optimization_barrier((w_query, sent))
    q_send = take_half(place, q_source, 1)
    parts, q_send = lax.optimization_barrier((parts, q_send))
    heads = merge(parts)
    heads, w_one = lax.optimization_barrier((heads, w_one))
    w_two = lax.ppermute(w_one, "core", swap)
    text_far = lax.ppermute(text_near, "yh", swap)
    q_one = lax.ppermute(q_send, ("enc", "yh", "core"), across)

    weights = (w_mine, w_one, w_two)
    far, acc, x_other = ring(heads, functools.partial(mix_near, place, weights), x_other)
    mixed = mix_far(place, far, weights, acc, x_own, x_other)

    q_one, text_far, mixed = lax.optimization_barrier((q_one, text_far, mixed))
    q_two = lax.ppermute(q_one, "core", swap)
    mixed_own, mixed_other = mixed
    text_own, key_sums = text_place(place, text_near, text_far, gain_k, gain_q, mixed_other)
    text_other = lax.ppermute(text_own, "enc", swap)
    far, turned, text_own = ring(
        mixed, functools.partial(stream, place, norm_gain.reshape(1, 5120), norm_bias.reshape(1, 5120)), text_own
    )
    raw, sums = query(place, turned, far, w_query, q_one, q_two, key_sums)
    sums = lax.all_to_all(sums, ("enc", "tp"), 0, 0, tiled=True)
    cross_other = cross(place, raw, sums, text_other, True)
    cross_back = lax.ppermute(cross_other, "enc", swap)
    cross_own = cross(place, raw, sums, text_own, False)

    def assemble(own, back, axis):
        return jnp.where(
            e == 0, jnp.concatenate([own, back], axis=axis), jnp.concatenate([back, own], axis=axis)
        )

    return (assemble(mixed_own, text_other[1024:], 1).T, assemble(cross_own, cross_back, 0))


def solution(mesh):
    parts = Mesh(mesh.devices.reshape(2, 4, 2, 2, 8), ("enc", "x", "yh", "core", "tp"))
    seq = ("x", "yh", "core")
    feat = ("enc", "tp")
    placed = (
        P(seq, feat),
        P(seq, feat),
        P(seq, feat),
        P(seq, feat),
        P(None, feat),
        P(None, feat),
        P(),
        P(),
        P(),
        P(None, feat),
        P(("enc", "x", "yh", "core"), None),
        P(None, feat),
        P(None, feat),
        P(feat),
        P(feat),
        P(),
    )
    return jax.shard_map(
        on_device,
        mesh=parts,
        in_specs=placed,
        out_specs=(P(seq, feat), P(seq, feat)),
        check_vma=False,
    )
```

```python
import functools

import jax
import jax.numpy as jnp
import numpy as np
from jax import lax
from jax.experimental import pallas as pl
from jax.experimental.pallas import tpu as pltpu
from jax.sharding import Mesh, PartitionSpec as P

HEAD = 128
GRID_H = 45
GRID_W = 80
EPS = 1e-06
THETA = 10000.0
LOG2E = 1.4426950408889634
SCALE2 = LOG2E * HEAD**-0.5
BF = jnp.bfloat16
F32 = jnp.float32
NT = (((1,), (1,)), ((), ()))
PARAMS = pltpu.CompilerParams(vmem_limit_bytes=16 * 1024 * 1024)
LARGE = pltpu.CompilerParams(vmem_limit_bytes=60 * 1024 * 1024)
SMALL = pltpu.CompilerParams(vmem_limit_bytes=8 * 1024 * 1024)
VMEM = pl.BlockSpec(memory_space=pltpu.VMEM)
SMEM = pl.BlockSpec(memory_space=pltpu.SMEM)
HBM = pl.BlockSpec(memory_space=pltpu.HBM)
PART = 1152


def frequencies():
    part_time = HEAD - 4 * (HEAD // 6)
    part_space = 2 * (HEAD // 6)
    time = THETA ** (-np.arange(0, part_time, 2).astype(np.float32) / part_time)
    space = THETA ** (-np.arange(0, part_space, 2).astype(np.float32) / part_space)
    pairs = np.concatenate([time, space, space]).astype(np.float32)
    return np.repeat(pairs, 2)[None, :]


def rope_kernel(place, q_hbm, k_hbm, v_hbm, freq_ref, mine_ref, send_ref, held, sems):
    copies = [pltpu.make_async_copy(ref, held.at[i], sems.at[i]) for i, ref in enumerate((q_hbm, k_hbm, v_hbm))]
    for copy in copies:
        copy.start()
    core = place[0]
    shape = (512, HEAD)
    position = (place[1] * 512 + lax.broadcasted_iota(jnp.int32, shape, 0)).astype(F32)
    lane = lax.broadcasted_iota(jnp.int32, shape, 1)
    line = jnp.floor((position + 0.5) * (1.0 / GRID_W))
    column = position - line * GRID_W
    frame = jnp.floor((line + 0.5) * (1.0 / GRID_H))
    row = line - frame * GRID_H
    part_time = HEAD - 4 * (HEAD // 6)
    part_space = 2 * (HEAD // 6)
    axis = jnp.where(lane < part_time, frame, jnp.where(lane < part_time + part_space, row, column))
    angles = axis * freq_ref[...]
    even = lane % 2 == 0
    cosine = jnp.cos(angles)
    sine = jnp.sin(angles)
    sine = jnp.where(even, -sine, sine)
    first = core == 0
    for index in range(3):
        copies[index].wait()
        heads = []
        for head in range(2):
            x = held[index, :, head * HEAD : (head + 1) * HEAD]
            if index < 2:
                x = x.astype(F32)
                partner = jnp.where(even, pltpu.roll(x, HEAD - 1, 1), pltpu.roll(x, 1, 1))
                x = (x * cosine + partner * sine).astype(BF)
            heads.append(x)
        mine_ref[index * 512 : (index + 1) * 512, :] = jnp.where(first, heads[0], heads[1])
        send_ref[index * 512 : (index + 1) * 512, :] = jnp.where(first, heads[1], heads[0])
    send_ref[1536:, :] = jnp.zeros((HEAD, HEAD), BF)


def rope(place, q, k, v):
    return pl.pallas_call(
        rope_kernel,
        in_specs=[SMEM, HBM, HBM, HBM, VMEM],
        out_specs=[VMEM] * 2,
        out_shape=[jax.ShapeDtypeStruct((1536, HEAD), BF), jax.ShapeDtypeStruct((1664, HEAD), BF)],
        scratch_shapes=[pltpu.VMEM((3, 512, 256), BF), pltpu.SemaphoreType.DMA((3,))],
        compiler_params=LARGE,
        name="rope",
    )(place, q, k, v, frequencies())


def text_kernel(
    place, own, other, key_hbm, value_hbm, gain_k, gain_q, send_in, text_ref, send_ref, weights, block, sems, out_sem
):
    depth = weights.shape[2]
    loads = {}
    for i in range(4):
        for kind, ref in enumerate((key_hbm, value_hbm)):
            loads[kind, i] = pltpu.make_async_copy(
                ref.at[pl.ds(i * depth, depth)], weights.at[kind, i], sems.at[kind, i]
            )
            loads[kind, i].start()
    first = place[4] == 0
    own, other = own[...], other[...]
    text = jnp.concatenate([jnp.where(first, own, other), jnp.where(first, other, own)], axis=0)
    sums = [jnp.zeros((32, 256), F32)] * 2
    for i in range(4):
        for kind in range(2):
            loads[kind, i].wait()
            sums[kind] += jnp.dot(
                text[:, i * depth : (i + 1) * depth], weights[kind, i], preferred_element_type=F32
            )
    sums[0] = sums[0] * (gain_k[...] * gain_q[...])
    for kind in range(2):
        for head in range(2):
            begin = (kind * 2 + head) * 32
            block[begin : begin + 32, :] = sums[kind][:, head * HEAD : (head + 1) * HEAD].astype(BF)
    copy = pltpu.make_async_copy(block, send_ref.at[pl.ds(1536, HEAD)], out_sem)
    copy.start()
    text_ref[...] = block[...]
    copy.wait()


def text_part(place, own, other, w_key, w_value, gain_k, gain_q, send):
    return pl.pallas_call(
        text_kernel,
        in_specs=[SMEM, VMEM, VMEM, HBM, HBM, VMEM, VMEM, HBM],
        out_specs=[VMEM, HBM],
        out_shape=[jax.ShapeDtypeStruct((HEAD, HEAD), BF), jax.ShapeDtypeStruct((1664, HEAD), BF)],
        input_output_aliases={7: 1},
        scratch_shapes=[
            pltpu.VMEM((2, 4, 1280, 256), BF),
            pltpu.VMEM((HEAD, HEAD), BF),
            pltpu.SemaphoreType.DMA((2, 4)),
            pltpu.SemaphoreType.DMA,
        ],
        compiler_params=LARGE,
        name="text_part",
    )(place, own, other, w_key, w_value, gain_k, gain_q, send)


def join_kernel(mine, text, other, kv_ref, q_ref, text_ref):
    text_ref[:HEAD, :] = text[...]
    text_ref[HEAD:, :] = other[1536:, :]
    q_ref[:512, :] = mine[:512, :]
    q_ref[512:, :] = other[:512, :]
    kv_ref[:1024, :] = mine[512:, :]
    kv_ref[1024:PART, :] = text[...]
    kv_ref[PART:, :] = other[512:, :]


def join(mine, text, other):
    return pl.pallas_call(
        join_kernel,
        in_specs=[VMEM] * 3,
        out_specs=[VMEM] * 3,
        out_shape=[
            jax.ShapeDtypeStruct((2 * PART, HEAD), BF),
            jax.ShapeDtypeStruct((1024, HEAD), BF),
            jax.ShapeDtypeStruct((2 * HEAD, HEAD), BF),
        ],
        compiler_params=SMALL,
        name="join",
    )(mine, text, other)


def take_kernel(place, ref, out):
    out[...] = ref[...]


def take_half(place, array, axis):
    shape = tuple(n // 2 if i == axis else n for i, n in enumerate(array.shape))
    return pl.pallas_call(
        take_kernel,
        grid_spec=pltpu.PrefetchScalarGridSpec(
            num_scalar_prefetch=1,
            grid=(1,),
            in_specs=[pl.BlockSpec(shape, lambda i, s: (s[0], 0) if axis == 0 else (0, s[0]))],
            out_specs=pl.BlockSpec(shape, lambda i, s: (0, 0)),
        ),
        out_shape=jax.ShapeDtypeStruct(shape, BF),
        compiler_params=SMALL,
        name="take_half",
    )(place, array)


def pick_kernel(place, first, second, out):
    @pl.when(place[0] == 0)
    def _():
        out[...] = first[...]

    @pl.when(place[0] != 0)
    def _():
        out[...] = second[...]


def pick(place, first, second):
    return pl.pallas_call(
        pick_kernel,
        in_specs=[SMEM, VMEM, VMEM],
        out_specs=VMEM,
        out_shape=jax.ShapeDtypeStruct(first.shape, BF),
        compiler_params=SMALL,
        name="pick",
    )(place, first, second)


def text_place_kernel(place, near, far, gain_k, gain_q, mixed, out_ref, sums_ref):
    out_ref[1024:, :] = mixed[...]
    core, seq = place[0], place[1]
    x = seq // 4
    y = place[2]
    for group, ref in ((0, near), (1, far)):
        for index in range(8):
            column = (x + (0, 3, 1, 2)[index // 2]) % 4
            device = (column * 2 + (y + group) % 2) * 2 + (core + index % 2) % 2
            for kind in range(2):
                for head in range(2):
                    for enc in range(2):
                        begin = index * HEAD + (kind * 2 + head) * 32 + enc * 16
                        rows = pl.ds(pl.multiple_of(kind * 512 + enc * 256 + device * 16, 16), 16)
                        out_ref[rows, head * HEAD : (head + 1) * HEAD] = ref[begin : begin + 16, :]
    keys = out_ref[:512, :].astype(F32) / (gain_k[...] * gain_q[...])
    square = keys[:, :HEAD] * keys[:, :HEAD] + keys[:, HEAD:] * keys[:, HEAD:]
    line = jnp.sum(jnp.transpose(square), axis=0, keepdims=True)
    rank = lax.broadcasted_iota(jnp.int32, (8, HEAD), 0)
    rows = jnp.zeros((8, HEAD), F32)
    for i in range(4):
        rows = jnp.where(rank == 2 + i, line[:, i * HEAD : (i + 1) * HEAD], rows)
    sums_ref[...] = rows


def text_place(place, near, far, gain_k, gain_q, mixed):
    return pl.pallas_call(
        text_place_kernel,
        in_specs=[SMEM] + [VMEM] * 5,
        out_specs=[VMEM, VMEM],
        out_shape=[jax.ShapeDtypeStruct((1344, 256), BF), jax.ShapeDtypeStruct((8, HEAD), F32)],
        compiler_params=SMALL,
        name="text_place",
    )(place, near, far, gain_k, gain_q, mixed)


def attend_kernel(count, first, last, skip, single, texts, place, *refs):
    if single:
        refs = (refs[0], None) + refs[1:]
    q_low, q_up, kvs = refs[0], refs[1], refs[2 : 2 + count]
    refs = refs[2 + count :]
    if not first:
        acc_in, high_in = refs[:2]
        refs = refs[2:]
    refs = refs[skip:]
    if texts:
        text_in, refs = refs[0], refs[1:]
        text_out = refs[-2]
        refs = refs[:-2] + refs[-1:]
        before = texts * HEAD
        text_out[:before, :] = text_in[...]
        for kv in kvs:
            for i in range(0, kv.shape[0], PART):
                text_out[before : before + HEAD, :] = kv[i + 1024 : i + PART, :]
                before += HEAD
    if last:
        out_ref, wide = refs
    else:
        acc_out, high_out, wide = refs
    chunk = 512
    sub = 256

    @pl.when(pl.program_id(0) == 0)
    def _():
        base = 0
        for kv in kvs:
            for i in range(0, kv.shape[0], PART):
                wide[pl.ds(base, chunk), :HEAD] = kv[i + 512 : i + 1024, :]
                wide[pl.ds(base, chunk), HEAD:] = jnp.ones((chunk, HEAD), BF)
                base += chunk

    def score(begin):
        q = q_low[pl.ds(begin, sub), :]
        if q_up is not None:
            q = jnp.where(pl.program_id(0) == 0, q, q_up[pl.ds(begin, sub), :])
        return [
            lax.dot_general(q, kv[i : i + 512, :], NT, preferred_element_type=F32)
            for kv in kvs
            for i in range(0, kv.shape[0], PART)
        ]

    def finish(begin, scores):
        rows = pl.ds(begin, sub)
        high = None
        for s in scores:
            for j in range(0, chunk, HEAD):
                part = s[:, j : j + HEAD]
                high = part if high is None else jnp.maximum(high, part)
        high = jnp.max(high, axis=1, keepdims=True)
        acc = None
        if not first:
            before = high_in[rows, :1]
            high = jnp.maximum(before, high)
            acc = acc_in[rows, :] * jnp.exp2((before - high) * SCALE2)
        shift = high * SCALE2
        for i, s in enumerate(scores):
            p = jnp.exp2(s * SCALE2 - shift).astype(BF)
            update = jnp.dot(p, wide[pl.ds(i * chunk, chunk), :], preferred_element_type=F32)
            acc = update if acc is None else acc + update
        if not last:
            acc_out[rows, :] = acc
            high_out[rows, :] = jnp.broadcast_to(high, (sub, HEAD))
            return
        total = acc[:, HEAD:]
        block = (place[0] + begin // 512) % 2 * 2 + begin // sub % 2
        line = jnp.transpose(shift + jnp.log(total) * LOG2E)[:16, :]
        one = line.astype(BF).astype(F32)
        two = (line - one).astype(BF).astype(F32)
        three = line - one - two
        rank = lax.broadcasted_iota(jnp.int32, (16, sub), 0)
        packed = jnp.where(rank == 0, one, jnp.where(rank == 1, two, jnp.where(rank == 2, three, 0.0)))
        out_ref[pl.ds(block, 1), :HEAD, :] = jnp.transpose(acc[:, :HEAD] / total).astype(BF)[None]
        out_ref[pl.ds(block, 1), HEAD:, :] = packed.astype(BF)[None]

    begins = list(range(0, q_low.shape[0], sub))
    ahead = score(begins[0])
    for index, begin in enumerate(begins):
        scores = ahead
        if index + 1 < len(begins):
            ahead = score(begins[index + 1])
        finish(begin, scores)


def attend(place, qs, kvs, state=None, last=False, into=None, slot=0, text=None):
    total = len(qs) * 1024
    keys = sum(kv.shape[0] for kv in kvs) // PART * 512
    rows = 1024

    def row(width, at=0):
        return pl.BlockSpec((rows, width), lambda i, s: (i + at, 0))

    operands = [*qs, *kvs]
    specs = [pl.BlockSpec(a.shape, lambda i, s: (0, 0)) for a in operands]
    if state is not None:
        operands += list(state)
        specs += [row(256), row(HEAD)]
    aliases = {}
    if into is not None:
        aliases = {len(operands) + 1: 0, len(operands) + 2: 1}
        operands += list(into)
        specs += [pl.BlockSpec(memory_space=pl.ANY)] * 2
    if last:
        out_specs = [pl.BlockSpec((4, 144, 256), lambda i, s: ((s[2] + i) % 2, 0, 0))]
        out_shape = [jax.ShapeDtypeStruct((8, 144, 256), BF)]
    else:
        out_specs = [row(256, slot), row(HEAD, slot)]
        out_shape = [jax.ShapeDtypeStruct((2048, 256), F32), jax.ShapeDtypeStruct((2048, HEAD), F32)]
    texts = 0
    if text is not None:
        texts = text.shape[0] // HEAD
        operands.append(text)
        specs.append(pl.BlockSpec(text.shape, lambda i, s: (0, 0)))
        shape = (text.shape[0] + keys // 512 * HEAD, HEAD)
        out_specs = out_specs + [pl.BlockSpec(shape, lambda i, s: (0, 0))]
        out_shape = out_shape + [jax.ShapeDtypeStruct(shape, BF)]
    grid_spec = pltpu.PrefetchScalarGridSpec(
        num_scalar_prefetch=1,
        grid=(total // rows,),
        in_specs=specs,
        out_specs=out_specs,
        scratch_shapes=[pltpu.VMEM((keys, 256), BF)],
    )
    return pl.pallas_call(
        functools.partial(attend_kernel, len(kvs), state is None, last, 0 if into is None else 2, len(qs) == 1, texts),
        grid_spec=grid_spec,
        out_shape=out_shape,
        input_output_aliases=aliases,
        compiler_params=PARAMS,
        cost_estimate=pl.CostEstimate(
            flops=4 * total * keys * HEAD, bytes_accessed=4 * 1024 * 1024, transcendentals=total * keys
        ),
        name="attend",
    )(place, *operands)


def merge_kernel(in_ref, low_ref, up_ref):
    for head in range(4):
        enc, core = head // 2, head % 2
        sources = [half * 4 + core * 2 + enc for half in range(2)]
        logs = []
        for source in sources:
            lines = in_ref[source, HEAD:, :].astype(F32)
            logs.append(lines[0:1, :] + lines[1:2, :] + lines[2:3, :])
        first = in_ref[sources[0], :HEAD, :].astype(F32) / (1.0 + jnp.exp2(logs[1] - logs[0]))
        second = in_ref[sources[1], :HEAD, :].astype(F32) / (1.0 + jnp.exp2(logs[0] - logs[1]))
        out = low_ref if enc == 0 else up_ref
        out[core * HEAD : (core + 1) * HEAD, :] = (first + second).astype(BF)


def merge(parts):
    return pl.pallas_call(
        merge_kernel,
        in_specs=[VMEM],
        out_specs=[VMEM] * 2,
        out_shape=[jax.ShapeDtypeStruct((256, 256), BF)] * 2,
        compiler_params=SMALL,
        name="merge",
    )(parts)


UP = [(i, (i + 1) % 8) for i in range(8)]
DOWN = [(i, (i - 1) % 8) for i in range(8)]


def ring(pair, take, due=()):
    right = left = list(pair)
    state = take(None, [pair], [0])
    for step in range(1, 4):
        right = [lax.ppermute(a, "tp", UP) for a in right]
        left = [lax.ppermute(a, "tp", DOWN) for a in left]
        if step == 2:
            left[1], state, due = lax.optimization_barrier((left[1], state, due))
        else:
            left[1], state = lax.optimization_barrier((left[1], state))
        state = take(state, [right, left], [8 - step, step])
    return [lax.ppermute(right[0], "tp", UP), lax.ppermute(left[1], "tp", DOWN)], state, due


SHIFTS = [0, 7, 1, 6, 2, 5, 3, 4]


def pack_kernel(place, own_x, send_x, gates, own_ref, send_ref):
    row = gates[pl.ds(place[6], 1), :]
    diagonal = lax.broadcasted_iota(jnp.int32, (320, 320), 0) == lax.broadcasted_iota(jnp.int32, (320, 320), 1)
    gate = jnp.sum(jnp.where(diagonal, row, 0.0), axis=1, keepdims=True)
    one = gate.astype(BF).astype(F32)
    two = (gate - one).astype(BF).astype(F32)
    lane = lax.broadcasted_iota(jnp.int32, (320, HEAD), 1)
    terms = jnp.where(lane == 0, one, jnp.where(lane == 1, two, jnp.where(lane == 2, gate - one - two, 0.0)))
    for x, out in ((own_x, own_ref), (send_x, send_ref)):
        out[:, :256] = x[...]
        out[:, 256:] = terms.astype(BF)


def pack(place, x, gates):
    return pl.pallas_call(
        pack_kernel,
        grid_spec=pltpu.PrefetchScalarGridSpec(
            num_scalar_prefetch=1,
            grid=(1,),
            in_specs=[
                pl.BlockSpec((320, 256), lambda i, s: (0, s[4])),
                pl.BlockSpec((320, 256), lambda i, s: (0, 1 - s[4])),
                pl.BlockSpec(gates.shape, lambda i, s: (0, 0)),
            ],
            out_specs=[pl.BlockSpec((320, 384), lambda i, s: (0, 0))] * 2,
        ),
        out_shape=[jax.ShapeDtypeStruct((320, 384), BF)] * 2,
        compiler_params=SMALL,
        name="pack",
    )(place, x, x, gates)


def mix_add(place, pairs, shifts, w_own, w_one, w_two, acc):
    core, z = place[0], place[3]
    for (low, up), shift in zip(pairs, shifts):
        source = (z + shift) % 8
        first = pl.ds(pl.multiple_of(source * 256, 256), 256)
        second = pl.ds(pl.multiple_of(2048 + source * 256, 256), 256)
        low, up = low[...], up[...]

        def add(w):
            return jnp.dot(w[:, first], low, preferred_element_type=F32) + jnp.dot(
                w[:, second], up, preferred_element_type=F32
            )

        acc[:320] += add(w_own)
        acc[pl.ds(pl.multiple_of(320 + core * 160, 32), 160)] += add(w_one)
        acc[pl.ds(pl.multiple_of(480 - core * 160, 32), 160)] += add(w_two)


def mix_near_kernel(shifts, place, *refs):
    count = len(shifts)
    pairs = [refs[2 * i : 2 * i + 2] for i in range(count)]
    w_own, w_one, w_two, before, acc = refs[2 * count :]
    acc[...] = before[...]
    mix_add(place, pairs, shifts, w_own, w_one, w_two, acc)


def mix_first_kernel(place, low, up, w_own, w_one, w_two, acc):
    acc[...] = jnp.zeros_like(acc)
    mix_add(place, [(low, up)], [0], w_own, w_one, w_two, acc)


def mix_near(place, weights, state, pairs, shifts):
    operands = [a for pair in pairs for a in pair] + list(weights)
    if state is None:
        kernel = mix_first_kernel
    else:
        kernel = functools.partial(mix_near_kernel, shifts)
        operands.append(state)
    return pl.pallas_call(
        kernel,
        in_specs=[SMEM] + [VMEM] * len(operands),
        out_specs=VMEM,
        out_shape=jax.ShapeDtypeStruct((640, 256), F32),
        compiler_params=SMALL,
        cost_estimate=pl.CostEstimate(
            flops=2 * 256 * 512 * 640 * len(pairs), bytes_accessed=1 << 20, transcendentals=0
        ),
        name="mix_near",
    )(place, *operands)


def mix_far_kernel(place, low, up, w_own, w_one, w_two, near, own_x, other_x, own, other, acc):
    acc[...] = near[...]
    mix_add(place, [(low, up)], [4], w_own, w_one, w_two, acc)
    for x, begin, out in ((own_x, 0, own), (other_x, 320, other)):
        gate = jnp.sum(x[:, 256:].astype(F32), axis=1, keepdims=True)
        out[...] = (x[:, :256].astype(F32) + gate * acc[begin : begin + 320]).astype(BF)


def mix_far(place, far, weights, near, own_x, other_x):
    return pl.pallas_call(
        mix_far_kernel,
        in_specs=[SMEM] + [VMEM] * 8,
        out_specs=[VMEM] * 2,
        out_shape=[jax.ShapeDtypeStruct((320, 256), BF)] * 2,
        scratch_shapes=[pltpu.VMEM((640, 256), F32)],
        compiler_params=SMALL,
        name="mix_far",
    )(place, *far, *weights, near, own_x, other_x)


def stream_kernel(count, place, *refs):
    pieces = refs[: 2 * count]
    refs = refs[2 * count :]
    if count == 1:
        gain, bias, out_ref, sums_ref, terms = refs
        first = place[4] == 0
        for i, ref in enumerate((gain, bias)):
            for j in range(8):
                low = ref[:, j * 320 : (j + 1) * 320]
                up = ref[:, 2560 + j * 320 : 2560 + (j + 1) * 320]
                terms[i, j : j + 1, :320] = jnp.where(first, low, up)
                terms[i, j : j + 1, 320:] = jnp.where(first, up, low)
        total = jnp.zeros((1, 256), F32)
        square = jnp.zeros((1, 256), F32)
    else:
        before, out_ref, sums_ref = refs
        total, square = before[0:1], before[1:2]
    for i, ref in enumerate(pieces):
        x = ref[...]
        begin = i % 2 * 320
        out_ref[i // 2, :, begin : begin + 320] = jnp.transpose(x)
        x = x.astype(F32)
        total += jnp.sum(x, axis=0, keepdims=True)
        square += jnp.sum(x * x, axis=0, keepdims=True)
    rank = lax.broadcasted_iota(jnp.int32, (8, 256), 0)
    sums_ref[...] = jnp.where(rank == 0, total, jnp.where(rank == 1, square, 0.0))


def stream(place, gain, bias, state, pairs, shifts):
    count = len(pairs)
    operands = [a for pair in pairs for a in pair]
    out_shape = [jax.ShapeDtypeStruct((count, 256, 640), BF), jax.ShapeDtypeStruct((8, 256), F32)]
    if state is None:
        operands += [gain, bias]
        out_shape.append(jax.ShapeDtypeStruct((2, 8, 640), F32))
    else:
        operands.append(state[-2])
    outs = pl.pallas_call(
        functools.partial(stream_kernel, count),
        in_specs=[SMEM] + [VMEM] * len(operands),
        out_specs=[VMEM] * len(out_shape),
        out_shape=out_shape,
        compiler_params=SMALL,
        cost_estimate=pl.CostEstimate(flops=1 << 22, bytes_accessed=2 << 20, transcendentals=0),
        name="stream",
    )(place, *operands)
    if state is None:
        return outs
    return [*state[:-2], outs[0], outs[1], state[-1]]


def query_kernel(
    place, near_a, near_b, near_c, near_d, near_sums, terms, far_own, far_other, w_own, w_one, w_two, key_sums, raw_ref, sums_ref, last, weight, acc
):
    z, enc = place[3], place[4]
    total = near_sums[0:1]
    square = near_sums[1:2]
    for i, ref in enumerate((far_own, far_other)):
        x = ref[...]
        last[:, i * 320 : (i + 1) * 320] = jnp.transpose(x)
        x = x.astype(F32)
        total += jnp.sum(x, axis=0, keepdims=True)
        square += jnp.sum(x * x, axis=0, keepdims=True)
    mean = total * (1.0 / 5120)
    scale = lax.rsqrt(square * (1.0 / 5120) - mean * mean + EPS)
    mean = jnp.transpose(jnp.broadcast_to(mean, (HEAD, 256)))[:, :1]
    scale = jnp.transpose(jnp.broadcast_to(scale, (HEAD, 256)))[:, :1]
    blocks = [near_a[0]] + [ref[i] for ref in (near_b, near_c, near_d) for i in range(2)] + [last[...]]
    for step, x in enumerate(blocks):
        source = (z + SHIFTS[step]) % 8
        row = pl.ds(source, 1)
        normed = ((x.astype(F32) - mean) * scale * terms[0, row, :] + terms[1, row, :]).astype(BF)
        slot = step % 2
        for i in range(2):
            rows = pl.ds(pl.multiple_of((enc + i) % 2 * 2560 + source * 320, 64), 320)
            to = slice(i * 320, (i + 1) * 320)
            weight[slot, to, :256] = w_own[rows, :]
            weight[slot, to, 256:384] = w_one[rows, :]
            weight[slot, to, 384:] = w_two[rows, :]
        update = jnp.dot(normed, weight[slot], preferred_element_type=F32)
        acc[...] = update if step == 0 else acc[...] + update
    raw = acc[...]
    raw_ref[...] = raw
    square = raw * raw
    part = square[:, :HEAD]
    for j in range(HEAD, 512, HEAD):
        part += square[:, j : j + HEAD]
    line = jnp.sum(jnp.transpose(part), axis=0, keepdims=True)
    rank = lax.broadcasted_iota(jnp.int32, (8, HEAD), 0)
    line = jnp.where(rank == 0, line[:, :HEAD], jnp.where(rank == 1, line[:, HEAD:], key_sums[...]))
    for i in range(16):
        sums_ref[i] = line


def query(place, turned, far, w_own, w_one, w_two, key_sums):
    return pl.pallas_call(
        query_kernel,
        in_specs=[SMEM] + [VMEM] * 12,
        out_specs=[VMEM] * 2,
        out_shape=[
            jax.ShapeDtypeStruct((256, 512), F32),
            jax.ShapeDtypeStruct((16, 8, HEAD), F32),
        ],
        scratch_shapes=[
            pltpu.VMEM((256, 640), BF),
            pltpu.VMEM((2, 640, 512), BF),
            pltpu.VMEM((256, 512), F32),
        ],
        compiler_params=SMALL,
        cost_estimate=pl.CostEstimate(flops=2 * 256 * 5120 * 512, bytes_accessed=1 << 20, transcendentals=0),
        name="query",
    )(place, *turned, *far, w_own, w_one, w_two, key_sums)


def cross_kernel(partner, place, raw_ref, sums_ref, text_ref, out):
    core, enc, length = place[0], place[4], place[5]
    queries = jnp.zeros((8, HEAD), F32)
    keys = jnp.zeros((8, HEAD), F32)
    for i in range(8):
        low, up = sums_ref[i], sums_ref[8 + i]
        queries += jnp.where(enc == 0, low, up)
        keys += low + up
    factor_q = lax.rsqrt(queries * (1.0 / 4096) + EPS)
    factor_k = lax.rsqrt(keys * (1.0 / 4096) + EPS) * SCALE2
    column = jnp.concatenate(
        [jnp.transpose(jnp.broadcast_to(factor_q[i : i + 1], (HEAD, HEAD))) for i in range(2)], axis=0
    )
    line = jnp.concatenate([factor_k[2 + i : 3 + i] for i in range(4)], axis=1)
    live = lax.broadcasted_iota(jnp.int32, (256, 512), 1) < length
    for index in range(2):
        if partner:
            lanes = pl.ds(pl.multiple_of((core + index) % 2 * HEAD, HEAD), HEAD)
        else:
            lanes = slice(index * HEAD, (index + 1) * HEAD)
        begin = index * HEAD + (256 if partner else 0)
        q = (raw_ref[:, begin : begin + HEAD] * column).astype(BF)
        s = lax.dot_general(q, text_ref[:512, lanes], NT, preferred_element_type=F32) * line
        s = jnp.where(live, s, -1e30)
        p = jnp.exp2(s - jnp.max(s, axis=1, keepdims=True))
        total = jnp.sum(p, axis=1, keepdims=True)
        o = jnp.dot(p.astype(BF), text_ref[512:1024, lanes], preferred_element_type=F32)
        out[:, lanes] = (o / total).astype(BF)


def cross(place, raw, sums, text, partner):
    return pl.pallas_call(
        functools.partial(cross_kernel, partner),
        in_specs=[SMEM] + [VMEM] * 3,
        out_specs=VMEM,
        out_shape=jax.ShapeDtypeStruct((256, 256), BF),
        compiler_params=SMALL,
        name="cross",
    )(place, raw, sums, text)


def on_device(
    x_res,
    q_proj,
    k_proj,
    v_proj,
    w_out,
    gate_table,
    timestep,
    norm_gain,
    norm_bias,
    w_query,
    context,
    w_key,
    w_value,
    gain_cq,
    gain_ck,
    text_len,
):
    e = lax.axis_index("enc")
    c = lax.axis_index("core")
    y = lax.axis_index("yh")
    z = lax.axis_index("tp")
    seq = (lax.axis_index("x") * 2 + y) * 2 + c
    place = jnp.stack([c, seq, y, z, e, text_len[0], timestep[0]]).astype(jnp.int32)
    swap = [(0, 1), (1, 0)]
    x_up = [(i, (i + 1) % 4) for i in range(4)]
    x_down = [(i, (i - 1) % 4) for i in range(4)]

    text = lax.ppermute(context, "enc", swap)
    gain_k, gain_q = gain_ck.reshape(1, 256), gain_cq.reshape(1, 256)
    mine, send = rope(place, q_proj, k_proj, v_proj)
    text, send = text_part(place, context, text, w_key, w_value, gain_k, gain_q, send)
    kv, q_own, text_near = join(mine, text, lax.ppermute(send, "core", swap))
    q_far = lax.ppermute(q_own, "yh", swap)
    kv_left = lax.ppermute(kv, "x", x_up)
    kv_right = lax.ppermute(kv, "x", x_down)
    w_mine = w_out.T
    state = attend(place, [q_own], [kv])
    w_source, x_source, state = lax.optimization_barrier((w_mine, x_res.T, state))
    w_send = take_half(place, w_source, 0)
    x_own, x_send = pack(place, x_source, gate_table)
    q_far, state = lax.optimization_barrier((q_far, state))
    state = attend(place, [q_far], [kv], into=state, slot=1)
    kv_left, kv_right, state = lax.optimization_barrier((kv_left, kv_right, state))
    way = [(i * 2 + j, (i + 1 - 2 * j) % 4 * 2 + j) for i in range(4) for j in range(2)]
    kv_far = lax.ppermute(pick(place, kv_left, kv_right), ("x", "core"), way)
    *state, text_near = attend(place, [q_own, q_far], [kv_left, kv_right], state, text=text_near)
    sent, text_near = attend(place, [q_own, q_far], [kv_far], state, last=True, text=text_near)

    across = [
        (e * 4 + y * 2 + c, (1 - e) * 4 + (y + c) % 2 * 2 + c) for e in range(2) for y in range(2) for c in range(2)
    ]
    w_send, x_send, q_far = lax.optimization_barrier((w_send, x_send, q_far))
    x_other = lax.ppermute(x_send, "enc", swap)
    w_one = lax.ppermute(w_send, ("enc", "yh", "core"), across)
    sent, x_other = lax.optimization_barrier((sent, x_other))
    parts = lax.all_to_all(sent, ("yh", "core", "enc"), 0, 0, tiled=True)

    q_source, _ = lax.optimization_barrier((w_query, sent))
    q_send = take_half(place, q_source, 1)
    parts, q_send = lax.optimization_barrier((parts, q_send))
    heads = merge(parts)
    heads, w_one = lax.optimization_barrier((heads, w_one))
    w_two = lax.ppermute(w_one, "core", swap)
    text_far = lax.ppermute(text_near, "yh", swap)

    weights = (w_mine, w_one, w_two)
    far, acc, text_far = ring(heads, functools.partial(mix_near, place, weights), text_far)
    q_send, text_far = lax.optimization_barrier((q_send, text_far))
    q_one = lax.ppermute(q_send, ("enc", "yh", "core"), across)
    mixed = mix_far(place, far, weights, acc, x_own, x_other)

    q_one, text_far, mixed = lax.optimization_barrier((q_one, text_far, mixed))
    q_two = lax.ppermute(q_one, "core", swap)
    mixed_own, mixed_other = mixed
    text_own, key_sums = text_place(place, text_near, text_far, gain_k, gain_q, mixed_other)
    text_other = lax.ppermute(text_own, "enc", swap)
    far, turned, text_own = ring(
        mixed, functools.partial(stream, place, norm_gain.reshape(1, 5120), norm_bias.reshape(1, 5120)), text_own
    )
    raw, sums = query(place, turned, far, w_query, q_one, q_two, key_sums)
    sums = lax.all_to_all(sums, ("enc", "tp"), 0, 0, tiled=True)
    cross_other = cross(place, raw, sums, text_other, True)
    cross_back = lax.ppermute(cross_other, "enc", swap)
    cross_own = cross(place, raw, sums, text_own, False)

    def assemble(own, back, axis):
        return jnp.where(
            e == 0, jnp.concatenate([own, back], axis=axis), jnp.concatenate([back, own], axis=axis)
        )

    return (assemble(mixed_own, text_other[1024:], 1).T, assemble(cross_own, cross_back, 0))


def solution(mesh):
    parts = Mesh(mesh.devices.reshape(2, 4, 2, 2, 8), ("enc", "x", "yh", "core", "tp"))
    seq = ("x", "yh", "core")
    feat = ("enc", "tp")
    placed = (
        P(seq, feat),
        P(seq, feat),
        P(seq, feat),
        P(seq, feat),
        P(None, feat),
        P(None, feat),
        P(),
        P(),
        P(),
        P(None, feat),
        P(("enc", "x", "yh", "core"), None),
        P(None, feat),
        P(None, feat),
        P(feat),
        P(feat),
        P(),
    )
    return jax.shard_map(
        on_device,
        mesh=parts,
        in_specs=placed,
        out_specs=(P(seq, feat), P(seq, feat)),
        check_vma=False,
    )
```

```python
import functools

import jax
import jax.numpy as jnp
import numpy as np
from jax import lax
from jax.experimental import pallas as pl
from jax.experimental.pallas import tpu as pltpu
from jax.sharding import Mesh, PartitionSpec as P

HEAD = 128
GRID_H = 45
GRID_W = 80
EPS = 1e-06
THETA = 10000.0
LOG2E = 1.4426950408889634
SCALE2 = LOG2E * HEAD**-0.5
BF = jnp.bfloat16
F32 = jnp.float32
NT = (((1,), (1,)), ((), ()))
PARAMS = pltpu.CompilerParams(vmem_limit_bytes=16 * 1024 * 1024)
LARGE = pltpu.CompilerParams(vmem_limit_bytes=60 * 1024 * 1024)
SMALL = pltpu.CompilerParams(vmem_limit_bytes=8 * 1024 * 1024)
VMEM = pl.BlockSpec(memory_space=pltpu.VMEM)
SMEM = pl.BlockSpec(memory_space=pltpu.SMEM)
HBM = pl.BlockSpec(memory_space=pltpu.HBM)
PART = 1152


def frequencies():
    part_time = HEAD - 4 * (HEAD // 6)
    part_space = 2 * (HEAD // 6)
    time = THETA ** (-np.arange(0, part_time, 2).astype(np.float32) / part_time)
    space = THETA ** (-np.arange(0, part_space, 2).astype(np.float32) / part_space)
    pairs = np.concatenate([time, space, space]).astype(np.float32)
    return np.repeat(pairs, 2)[None, :]


def rope_kernel(place, q_hbm, k_hbm, v_hbm, freq_ref, mine_ref, send_ref, held, sems):
    copies = [pltpu.make_async_copy(ref, held.at[i], sems.at[i]) for i, ref in enumerate((q_hbm, k_hbm, v_hbm))]
    for copy in copies:
        copy.start()
    core = place[0]
    shape = (512, HEAD)
    position = (place[1] * 512 + lax.broadcasted_iota(jnp.int32, shape, 0)).astype(F32)
    lane = lax.broadcasted_iota(jnp.int32, shape, 1)
    line = jnp.floor((position + 0.5) * (1.0 / GRID_W))
    column = position - line * GRID_W
    frame = jnp.floor((line + 0.5) * (1.0 / GRID_H))
    row = line - frame * GRID_H
    part_time = HEAD - 4 * (HEAD // 6)
    part_space = 2 * (HEAD // 6)
    axis = jnp.where(lane < part_time, frame, jnp.where(lane < part_time + part_space, row, column))
    angles = axis * freq_ref[...]
    even = lane % 2 == 0
    cosine = jnp.cos(angles)
    sine = jnp.sin(angles)
    sine = jnp.where(even, -sine, sine)
    first = core == 0
    for index in range(3):
        copies[index].wait()
        heads = []
        for head in range(2):
            x = held[index, :, head * HEAD : (head + 1) * HEAD]
            if index < 2:
                x = x.astype(F32)
                partner = jnp.where(even, pltpu.roll(x, HEAD - 1, 1), pltpu.roll(x, 1, 1))
                x = (x * cosine + partner * sine).astype(BF)
            heads.append(x)
        mine_ref[index * 512 : (index + 1) * 512, :] = jnp.where(first, heads[0], heads[1])
        send_ref[index * 512 : (index + 1) * 512, :] = jnp.where(first, heads[1], heads[0])
    send_ref[1536:, :] = jnp.zeros((HEAD, HEAD), BF)


def rope(place, q, k, v):
    return pl.pallas_call(
        rope_kernel,
        in_specs=[SMEM, HBM, HBM, HBM, VMEM],
        out_specs=[VMEM] * 2,
        out_shape=[jax.ShapeDtypeStruct((1536, HEAD), BF), jax.ShapeDtypeStruct((1664, HEAD), BF)],
        scratch_shapes=[pltpu.VMEM((3, 512, 256), BF), pltpu.SemaphoreType.DMA((3,))],
        compiler_params=LARGE,
        name="rope",
    )(place, q, k, v, frequencies())


def text_kernel(
    place, own, other, key_hbm, value_hbm, gain_k, gain_q, send_in, text_ref, send_ref, weights, block, sems, out_sem
):
    depth = weights.shape[2]
    loads = {}
    for i in range(4):
        for kind, ref in enumerate((key_hbm, value_hbm)):
            loads[kind, i] = pltpu.make_async_copy(
                ref.at[pl.ds(i * depth, depth)], weights.at[kind, i], sems.at[kind, i]
            )
            loads[kind, i].start()
    first = place[4] == 0
    own, other = own[...], other[...]
    text = jnp.concatenate([jnp.where(first, own, other), jnp.where(first, other, own)], axis=0)
    sums = [jnp.zeros((32, 256), F32)] * 2
    for i in range(4):
        for kind in range(2):
            loads[kind, i].wait()
            sums[kind] += jnp.dot(
                text[:, i * depth : (i + 1) * depth], weights[kind, i], preferred_element_type=F32
            )
    sums[0] = sums[0] * (gain_k[...] * gain_q[...])
    for kind in range(2):
        for head in range(2):
            begin = (kind * 2 + head) * 32
            block[begin : begin + 32, :] = sums[kind][:, head * HEAD : (head + 1) * HEAD].astype(BF)
    copy = pltpu.make_async_copy(block, send_ref.at[pl.ds(1536, HEAD)], out_sem)
    copy.start()
    text_ref[...] = block[...]
    copy.wait()


def text_part(place, own, other, w_key, w_value, gain_k, gain_q, send):
    return pl.pallas_call(
        text_kernel,
        in_specs=[SMEM, VMEM, VMEM, HBM, HBM, VMEM, VMEM, HBM],
        out_specs=[VMEM, HBM],
        out_shape=[jax.ShapeDtypeStruct((HEAD, HEAD), BF), jax.ShapeDtypeStruct((1664, HEAD), BF)],
        input_output_aliases={7: 1},
        scratch_shapes=[
            pltpu.VMEM((2, 4, 1280, 256), BF),
            pltpu.VMEM((HEAD, HEAD), BF),
            pltpu.SemaphoreType.DMA((2, 4)),
            pltpu.SemaphoreType.DMA,
        ],
        compiler_params=LARGE,
        name="text_part",
    )(place, own, other, w_key, w_value, gain_k, gain_q, send)


def join_kernel(mine, text, other, kv_ref, q_ref, text_ref):
    text_ref[:HEAD, :] = text[...]
    text_ref[HEAD:, :] = other[1536:, :]
    q_ref[:512, :] = mine[:512, :]
    q_ref[512:, :] = other[:512, :]
    kv_ref[:1024, :] = mine[512:, :]
    kv_ref[1024:PART, :] = text[...]
    kv_ref[PART:, :] = other[512:, :]


def join(mine, text, other):
    return pl.pallas_call(
        join_kernel,
        in_specs=[VMEM] * 3,
        out_specs=[VMEM] * 3,
        out_shape=[
            jax.ShapeDtypeStruct((2 * PART, HEAD), BF),
            jax.ShapeDtypeStruct((1024, HEAD), BF),
            jax.ShapeDtypeStruct((2 * HEAD, HEAD), BF),
        ],
        compiler_params=SMALL,
        name="join",
    )(mine, text, other)


def take_kernel(place, ref, out):
    out[...] = ref[...]


def take_half(place, array, axis):
    shape = tuple(n // 2 if i == axis else n for i, n in enumerate(array.shape))
    return pl.pallas_call(
        take_kernel,
        grid_spec=pltpu.PrefetchScalarGridSpec(
            num_scalar_prefetch=1,
            grid=(1,),
            in_specs=[pl.BlockSpec(shape, lambda i, s: (s[0], 0) if axis == 0 else (0, s[0]))],
            out_specs=pl.BlockSpec(shape, lambda i, s: (0, 0)),
        ),
        out_shape=jax.ShapeDtypeStruct(shape, BF),
        compiler_params=SMALL,
        name="take_half",
    )(place, array)


def pick_kernel(place, first, second, out):
    @pl.when(place[0] == 0)
    def _():
        out[...] = first[...]

    @pl.when(place[0] != 0)
    def _():
        out[...] = second[...]


def pick(place, first, second):
    return pl.pallas_call(
        pick_kernel,
        in_specs=[SMEM, VMEM, VMEM],
        out_specs=VMEM,
        out_shape=jax.ShapeDtypeStruct(first.shape, BF),
        compiler_params=SMALL,
        name="pick",
    )(place, first, second)


def text_place_kernel(place, near, far, gain_k, gain_q, mixed, out_ref, sums_ref):
    out_ref[1024:, :] = mixed[...]
    core, seq = place[0], place[1]
    x = seq // 4
    y = place[2]
    for group, ref in ((0, near), (1, far)):
        for index in range(8):
            column = (x + (0, 3, 1, 2)[index // 2]) % 4
            device = (column * 2 + (y + group) % 2) * 2 + (core + index % 2) % 2
            for kind in range(2):
                for head in range(2):
                    for enc in range(2):
                        begin = index * HEAD + (kind * 2 + head) * 32 + enc * 16
                        rows = pl.ds(pl.multiple_of(kind * 512 + enc * 256 + device * 16, 16), 16)
                        out_ref[rows, head * HEAD : (head + 1) * HEAD] = ref[begin : begin + 16, :]
    keys = out_ref[:512, :].astype(F32) / (gain_k[...] * gain_q[...])
    square = keys[:, :HEAD] * keys[:, :HEAD] + keys[:, HEAD:] * keys[:, HEAD:]
    line = jnp.sum(jnp.transpose(square), axis=0, keepdims=True)
    rank = lax.broadcasted_iota(jnp.int32, (8, HEAD), 0)
    rows = jnp.zeros((8, HEAD), F32)
    for i in range(4):
        rows = jnp.where(rank == 2 + i, line[:, i * HEAD : (i + 1) * HEAD], rows)
    sums_ref[...] = rows


def text_place(place, near, far, gain_k, gain_q, mixed):
    return pl.pallas_call(
        text_place_kernel,
        in_specs=[SMEM] + [VMEM] * 5,
        out_specs=[VMEM, VMEM],
        out_shape=[jax.ShapeDtypeStruct((1344, 256), BF), jax.ShapeDtypeStruct((8, HEAD), F32)],
        compiler_params=SMALL,
        name="text_place",
    )(place, near, far, gain_k, gain_q, mixed)


def attend_kernel(count, first, last, skip, single, texts, place, *refs):
    if single:
        refs = (refs[0], None) + refs[1:]
    q_low, q_up, kvs = refs[0], refs[1], refs[2 : 2 + count]
    refs = refs[2 + count :]
    if not first:
        acc_in, high_in = refs[:2]
        refs = refs[2:]
    refs = refs[skip:]
    if texts:
        text_in, refs = refs[0], refs[1:]
        text_out = refs[-2]
        refs = refs[:-2] + refs[-1:]
        before = texts * HEAD
        text_out[:before, :] = text_in[...]
        for kv in kvs:
            for i in range(0, kv.shape[0], PART):
                text_out[before : before + HEAD, :] = kv[i + 1024 : i + PART, :]
                before += HEAD
    if last:
        out_ref, wide = refs
    else:
        acc_out, high_out, wide = refs
    chunk = 512
    sub = 256

    @pl.when(pl.program_id(0) == 0)
    def _():
        base = 0
        for kv in kvs:
            for i in range(0, kv.shape[0], PART):
                wide[pl.ds(base, chunk), :HEAD] = kv[i + 512 : i + 1024, :]
                wide[pl.ds(base, chunk), HEAD:] = jnp.ones((chunk, HEAD), BF)
                base += chunk

    def score(begin):
        q = q_low[pl.ds(begin, sub), :]
        if q_up is not None:
            q = jnp.where(pl.program_id(0) == 0, q, q_up[pl.ds(begin, sub), :])
        return [
            lax.dot_general(q, kv[i : i + 512, :], NT, preferred_element_type=F32)
            for kv in kvs
            for i in range(0, kv.shape[0], PART)
        ]

    def finish(begin, scores):
        rows = pl.ds(begin, sub)
        high = None
        for s in scores:
            for j in range(0, chunk, HEAD):
                part = s[:, j : j + HEAD]
                high = part if high is None else jnp.maximum(high, part)
        high = jnp.max(high, axis=1, keepdims=True)
        acc = None
        if not first:
            before = high_in[rows, :1]
            high = jnp.maximum(before, high)
            acc = acc_in[rows, :] * jnp.exp2((before - high) * SCALE2)
        shift = high * SCALE2
        for i, s in enumerate(scores):
            p = jnp.exp2(s * SCALE2 - shift).astype(BF)
            update = jnp.dot(p, wide[pl.ds(i * chunk, chunk), :], preferred_element_type=F32)
            acc = update if acc is None else acc + update
        if not last:
            acc_out[rows, :] = acc
            high_out[rows, :] = jnp.broadcast_to(high, (sub, HEAD))
            return
        total = acc[:, HEAD:]
        block = (place[0] + begin // 512) % 2 * 2 + begin // sub % 2
        line = jnp.transpose(shift + jnp.log(total) * LOG2E)[:16, :]
        one = line.astype(BF).astype(F32)
        two = (line - one).astype(BF).astype(F32)
        three = line - one - two
        rank = lax.broadcasted_iota(jnp.int32, (16, sub), 0)
        packed = jnp.where(rank == 0, one, jnp.where(rank == 1, two, jnp.where(rank == 2, three, 0.0)))
        out_ref[pl.ds(block, 1), :HEAD, :] = jnp.transpose(acc[:, :HEAD] / total).astype(BF)[None]
        out_ref[pl.ds(block, 1), HEAD:, :] = packed.astype(BF)[None]

    begins = list(range(0, q_low.shape[0], sub))
    ahead = score(begins[0])
    for index, begin in enumerate(begins):
        scores = ahead
        if index + 1 < len(begins):
            ahead = score(begins[index + 1])
        finish(begin, scores)


def attend(place, qs, kvs, state=None, last=False, into=None, slot=0, text=None):
    total = len(qs) * 1024
    keys = sum(kv.shape[0] for kv in kvs) // PART * 512
    rows = 1024

    def row(width, at=0):
        return pl.BlockSpec((rows, width), lambda i, s: (i + at, 0))

    operands = [*qs, *kvs]
    specs = [pl.BlockSpec(a.shape, lambda i, s: (0, 0)) for a in operands]
    if state is not None:
        operands += list(state)
        specs += [row(256), row(HEAD)]
    aliases = {}
    if into is not None:
        aliases = {len(operands) + 1: 0, len(operands) + 2: 1}
        operands += list(into)
        specs += [pl.BlockSpec(memory_space=pl.ANY)] * 2
    if last:
        out_specs = [pl.BlockSpec((4, 144, 256), lambda i, s: ((s[2] + i) % 2, 0, 0))]
        out_shape = [jax.ShapeDtypeStruct((8, 144, 256), BF)]
    else:
        out_specs = [row(256, slot), row(HEAD, slot)]
        out_shape = [jax.ShapeDtypeStruct((2048, 256), F32), jax.ShapeDtypeStruct((2048, HEAD), F32)]
    texts = 0
    if text is not None:
        texts = text.shape[0] // HEAD
        operands.append(text)
        specs.append(pl.BlockSpec(text.shape, lambda i, s: (0, 0)))
        shape = (text.shape[0] + keys // 512 * HEAD, HEAD)
        out_specs = out_specs + [pl.BlockSpec(shape, lambda i, s: (0, 0))]
        out_shape = out_shape + [jax.ShapeDtypeStruct(shape, BF)]
    grid_spec = pltpu.PrefetchScalarGridSpec(
        num_scalar_prefetch=1,
        grid=(total // rows,),
        in_specs=specs,
        out_specs=out_specs,
        scratch_shapes=[pltpu.VMEM((keys, 256), BF)],
    )
    return pl.pallas_call(
        functools.partial(attend_kernel, len(kvs), state is None, last, 0 if into is None else 2, len(qs) == 1, texts),
        grid_spec=grid_spec,
        out_shape=out_shape,
        input_output_aliases=aliases,
        compiler_params=PARAMS,
        cost_estimate=pl.CostEstimate(
            flops=4 * total * keys * HEAD, bytes_accessed=4 * 1024 * 1024, transcendentals=total * keys
        ),
        name="attend",
    )(place, *operands)


def merge_kernel(in_ref, low_ref, up_ref):
    for head in range(4):
        enc, core = head // 2, head % 2
        sources = [half * 4 + core * 2 + enc for half in range(2)]
        logs = []
        for source in sources:
            lines = in_ref[source, HEAD:, :].astype(F32)
            logs.append(lines[0:1, :] + lines[1:2, :] + lines[2:3, :])
        first = in_ref[sources[0], :HEAD, :].astype(F32) / (1.0 + jnp.exp2(logs[1] - logs[0]))
        second = in_ref[sources[1], :HEAD, :].astype(F32) / (1.0 + jnp.exp2(logs[0] - logs[1]))
        out = low_ref if enc == 0 else up_ref
        out[core * HEAD : (core + 1) * HEAD, :] = (first + second).astype(BF)


def merge(parts):
    return pl.pallas_call(
        merge_kernel,
        in_specs=[VMEM],
        out_specs=[VMEM] * 2,
        out_shape=[jax.ShapeDtypeStruct((256, 256), BF)] * 2,
        compiler_params=SMALL,
        name="merge",
    )(parts)


UP = [(i, (i + 1) % 8) for i in range(8)]
DOWN = [(i, (i - 1) % 8) for i in range(8)]


def ring(pair, take, due=()):
    right = left = list(pair)
    state = take(None, [pair], [0])
    for step in range(1, 4):
        right = [lax.ppermute(a, "tp", UP) for a in right]
        left = [lax.ppermute(a, "tp", DOWN) for a in left]
        if step == 2:
            left[1], state, due = lax.optimization_barrier((left[1], state, due))
        else:
            left[1], state = lax.optimization_barrier((left[1], state))
        state = take(state, [right, left], [8 - step, step])
    return [lax.ppermute(right[0], "tp", UP), lax.ppermute(left[1], "tp", DOWN)], state, due


SHIFTS = [0, 7, 1, 6, 2, 5, 3, 4]


def pack_kernel(place, own_x, send_x, gates, own_ref, send_ref):
    row = gates[pl.ds(place[6], 1), :]
    diagonal = lax.broadcasted_iota(jnp.int32, (320, 320), 0) == lax.broadcasted_iota(jnp.int32, (320, 320), 1)
    gate = jnp.sum(jnp.where(diagonal, row, 0.0), axis=1, keepdims=True)
    one = gate.astype(BF).astype(F32)
    two = (gate - one).astype(BF).astype(F32)
    lane = lax.broadcasted_iota(jnp.int32, (320, HEAD), 1)
    terms = jnp.where(lane == 0, one, jnp.where(lane == 1, two, jnp.where(lane == 2, gate - one - two, 0.0)))
    for x, out in ((own_x, own_ref), (send_x, send_ref)):
        out[:, :256] = x[...]
        out[:, 256:] = terms.astype(BF)


def pack(place, x, gates):
    return pl.pallas_call(
        pack_kernel,
        grid_spec=pltpu.PrefetchScalarGridSpec(
            num_scalar_prefetch=1,
            grid=(1,),
            in_specs=[
                pl.BlockSpec((320, 256), lambda i, s: (0, s[4])),
                pl.BlockSpec((320, 256), lambda i, s: (0, 1 - s[4])),
                pl.BlockSpec(gates.shape, lambda i, s: (0, 0)),
            ],
            out_specs=[pl.BlockSpec((320, 384), lambda i, s: (0, 0))] * 2,
        ),
        out_shape=[jax.ShapeDtypeStruct((320, 384), BF)] * 2,
        compiler_params=SMALL,
        name="pack",
    )(place, x, x, gates)


def mix_add(place, pairs, shifts, w_own, w_one, w_two, acc):
    core, z = place[0], place[3]
    for (low, up), shift in zip(pairs, shifts):
        source = (z + shift) % 8
        first = pl.ds(pl.multiple_of(source * 256, 256), 256)
        second = pl.ds(pl.multiple_of(2048 + source * 256, 256), 256)
        low, up = low[...], up[...]

        def add(w):
            return jnp.dot(w[:, first], low, preferred_element_type=F32) + jnp.dot(
                w[:, second], up, preferred_element_type=F32
            )

        acc[:320] += add(w_own)
        acc[pl.ds(pl.multiple_of(320 + core * 160, 32), 160)] += add(w_one)
        acc[pl.ds(pl.multiple_of(480 - core * 160, 32), 160)] += add(w_two)


def mix_near_kernel(shifts, place, *refs):
    count = len(shifts)
    pairs = [refs[2 * i : 2 * i + 2] for i in range(count)]
    w_own, w_one, w_two, before, acc = refs[2 * count :]
    acc[...] = before[...]
    mix_add(place, pairs, shifts, w_own, w_one, w_two, acc)


def mix_first_kernel(place, low, up, w_own, w_one, w_two, acc):
    acc[...] = jnp.zeros_like(acc)
    mix_add(place, [(low, up)], [0], w_own, w_one, w_two, acc)


def mix_near(place, weights, state, pairs, shifts):
    operands = [a for pair in pairs for a in pair] + list(weights)
    if state is None:
        kernel = mix_first_kernel
    else:
        kernel = functools.partial(mix_near_kernel, shifts)
        operands.append(state)
    return pl.pallas_call(
        kernel,
        in_specs=[SMEM] + [VMEM] * len(operands),
        out_specs=VMEM,
        out_shape=jax.ShapeDtypeStruct((640, 256), F32),
        compiler_params=SMALL,
        cost_estimate=pl.CostEstimate(
            flops=2 * 256 * 512 * 640 * len(pairs), bytes_accessed=1 << 20, transcendentals=0
        ),
        name="mix_near",
    )(place, *operands)


def mix_far_kernel(place, low, up, w_own, w_one, w_two, near, own_x, other_x, own, other, acc):
    acc[...] = near[...]
    mix_add(place, [(low, up)], [4], w_own, w_one, w_two, acc)
    for x, begin, out in ((own_x, 0, own), (other_x, 320, other)):
        gate = jnp.sum(x[:, 256:].astype(F32), axis=1, keepdims=True)
        out[...] = (x[:, :256].astype(F32) + gate * acc[begin : begin + 320]).astype(BF)


def mix_far(place, far, weights, near, own_x, other_x):
    return pl.pallas_call(
        mix_far_kernel,
        in_specs=[SMEM] + [VMEM] * 8,
        out_specs=[VMEM] * 2,
        out_shape=[jax.ShapeDtypeStruct((320, 256), BF)] * 2,
        scratch_shapes=[pltpu.VMEM((640, 256), F32)],
        compiler_params=SMALL,
        name="mix_far",
    )(place, *far, *weights, near, own_x, other_x)


def stream_kernel(count, place, *refs):
    pieces = refs[: 2 * count]
    refs = refs[2 * count :]
    if count == 1:
        gain, bias, out_ref, sums_ref, terms = refs
        first = place[4] == 0
        for i, ref in enumerate((gain, bias)):
            for j in range(8):
                low = ref[:, j * 320 : (j + 1) * 320]
                up = ref[:, 2560 + j * 320 : 2560 + (j + 1) * 320]
                terms[i, j : j + 1, :320] = jnp.where(first, low, up)
                terms[i, j : j + 1, 320:] = jnp.where(first, up, low)
        total = jnp.zeros((1, 256), F32)
        square = jnp.zeros((1, 256), F32)
    else:
        before, out_ref, sums_ref = refs
        total, square = before[0:1], before[1:2]
    for i, ref in enumerate(pieces):
        x = ref[...]
        begin = i % 2 * 320
        out_ref[i // 2, :, begin : begin + 320] = jnp.transpose(x)
        x = x.astype(F32)
        total += jnp.sum(x, axis=0, keepdims=True)
        square += jnp.sum(x * x, axis=0, keepdims=True)
    rank = lax.broadcasted_iota(jnp.int32, (8, 256), 0)
    sums_ref[...] = jnp.where(rank == 0, total, jnp.where(rank == 1, square, 0.0))


def stream(place, gain, bias, state, pairs, shifts):
    count = len(pairs)
    operands = [a for pair in pairs for a in pair]
    out_shape = [jax.ShapeDtypeStruct((count, 256, 640), BF), jax.ShapeDtypeStruct((8, 256), F32)]
    if state is None:
        operands += [gain, bias]
        out_shape.append(jax.ShapeDtypeStruct((2, 8, 640), F32))
    else:
        operands.append(state[-2])
    outs = pl.pallas_call(
        functools.partial(stream_kernel, count),
        in_specs=[SMEM] + [VMEM] * len(operands),
        out_specs=[VMEM] * len(out_shape),
        out_shape=out_shape,
        compiler_params=SMALL,
        cost_estimate=pl.CostEstimate(flops=1 << 22, bytes_accessed=2 << 20, transcendentals=0),
        name="stream",
    )(place, *operands)
    if state is None:
        return outs
    return [*state[:-2], outs[0], outs[1], state[-1]]


def query_kernel(
    place, near_a, near_b, near_c, near_d, near_sums, terms, far_own, far_other, w_own, w_one, w_two, key_sums, raw_ref, sums_ref, last, weight, acc
):
    z, enc = place[3], place[4]
    total = near_sums[0:1]
    square = near_sums[1:2]
    for i, ref in enumerate((far_own, far_other)):
        x = ref[...]
        last[:, i * 320 : (i + 1) * 320] = jnp.transpose(x)
        x = x.astype(F32)
        total += jnp.sum(x, axis=0, keepdims=True)
        square += jnp.sum(x * x, axis=0, keepdims=True)
    mean = total * (1.0 / 5120)
    scale = lax.rsqrt(square * (1.0 / 5120) - mean * mean + EPS)
    mean = jnp.transpose(jnp.broadcast_to(mean, (HEAD, 256)))[:, :1]
    scale = jnp.transpose(jnp.broadcast_to(scale, (HEAD, 256)))[:, :1]
    blocks = [near_a[0]] + [ref[i] for ref in (near_b, near_c, near_d) for i in range(2)] + [last[...]]
    for step, x in enumerate(blocks):
        source = (z + SHIFTS[step]) % 8
        row = pl.ds(source, 1)
        normed = ((x.astype(F32) - mean) * scale * terms[0, row, :] + terms[1, row, :]).astype(BF)
        slot = step % 2
        for i in range(2):
            rows = pl.ds(pl.multiple_of((enc + i) % 2 * 2560 + source * 320, 64), 320)
            to = slice(i * 320, (i + 1) * 320)
            weight[slot, to, :256] = w_own[rows, :]
            weight[slot, to, 256:384] = w_one[rows, :]
            weight[slot, to, 384:] = w_two[rows, :]
        update = jnp.dot(normed, weight[slot], preferred_element_type=F32)
        acc[...] = update if step == 0 else acc[...] + update
    raw = acc[...]
    raw_ref[...] = raw
    square = raw * raw
    part = square[:, :HEAD]
    for j in range(HEAD, 512, HEAD):
        part += square[:, j : j + HEAD]
    line = jnp.sum(jnp.transpose(part), axis=0, keepdims=True)
    rank = lax.broadcasted_iota(jnp.int32, (8, HEAD), 0)
    line = jnp.where(rank == 0, line[:, :HEAD], jnp.where(rank == 1, line[:, HEAD:], key_sums[...]))
    for i in range(16):
        sums_ref[i] = line


def query(place, turned, far, w_own, w_one, w_two, key_sums):
    return pl.pallas_call(
        query_kernel,
        in_specs=[SMEM] + [VMEM] * 12,
        out_specs=[VMEM] * 2,
        out_shape=[
            jax.ShapeDtypeStruct((256, 512), F32),
            jax.ShapeDtypeStruct((16, 8, HEAD), F32),
        ],
        scratch_shapes=[
            pltpu.VMEM((256, 640), BF),
            pltpu.VMEM((2, 640, 512), BF),
            pltpu.VMEM((256, 512), F32),
        ],
        compiler_params=SMALL,
        cost_estimate=pl.CostEstimate(flops=2 * 256 * 5120 * 512, bytes_accessed=1 << 20, transcendentals=0),
        name="query",
    )(place, *turned, *far, w_own, w_one, w_two, key_sums)


def cross_kernel(partner, place, raw_ref, sums_ref, text_ref, out):
    core, enc, length = place[0], place[4], place[5]
    queries = jnp.zeros((8, HEAD), F32)
    keys = jnp.zeros((8, HEAD), F32)
    for i in range(8):
        low, up = sums_ref[i], sums_ref[8 + i]
        queries += jnp.where(enc == 0, low, up)
        keys += low + up
    factor_q = lax.rsqrt(queries * (1.0 / 4096) + EPS)
    factor_k = lax.rsqrt(keys * (1.0 / 4096) + EPS) * SCALE2
    column = jnp.concatenate(
        [jnp.transpose(jnp.broadcast_to(factor_q[i : i + 1], (HEAD, HEAD))) for i in range(2)], axis=0
    )
    line = jnp.concatenate([factor_k[2 + i : 3 + i] for i in range(4)], axis=1)
    live = lax.broadcasted_iota(jnp.int32, (256, 512), 1) < length
    for index in range(2):
        if partner:
            lanes = pl.ds(pl.multiple_of((core + index) % 2 * HEAD, HEAD), HEAD)
        else:
            lanes = slice(index * HEAD, (index + 1) * HEAD)
        begin = index * HEAD + (256 if partner else 0)
        q = (raw_ref[:, begin : begin + HEAD] * column).astype(BF)
        s = lax.dot_general(q, text_ref[:512, lanes], NT, preferred_element_type=F32) * line
        s = jnp.where(live, s, -1e30)
        p = jnp.exp2(s - jnp.max(s, axis=1, keepdims=True))
        total = jnp.sum(p, axis=1, keepdims=True)
        o = jnp.dot(p.astype(BF), text_ref[512:1024, lanes], preferred_element_type=F32)
        out[:, lanes] = (o / total).astype(BF)


def cross(place, raw, sums, text, partner):
    return pl.pallas_call(
        functools.partial(cross_kernel, partner),
        in_specs=[SMEM] + [VMEM] * 3,
        out_specs=VMEM,
        out_shape=jax.ShapeDtypeStruct((256, 256), BF),
        compiler_params=SMALL,
        name="cross",
    )(place, raw, sums, text)


def on_device(
    x_res,
    q_proj,
    k_proj,
    v_proj,
    w_out,
    gate_table,
    timestep,
    norm_gain,
    norm_bias,
    w_query,
    context,
    w_key,
    w_value,
    gain_cq,
    gain_ck,
    text_len,
):
    e = lax.axis_index("enc")
    c = lax.axis_index("core")
    y = lax.axis_index("yh")
    z = lax.axis_index("tp")
    seq = (lax.axis_index("x") * 2 + y) * 2 + c
    place = jnp.stack([c, seq, y, z, e, text_len[0], timestep[0]]).astype(jnp.int32)
    swap = [(0, 1), (1, 0)]
    x_up = [(i, (i + 1) % 4) for i in range(4)]
    x_down = [(i, (i - 1) % 4) for i in range(4)]

    text = lax.ppermute(context, "enc", swap)
    gain_k, gain_q = gain_ck.reshape(1, 256), gain_cq.reshape(1, 256)
    mine, send = rope(place, q_proj, k_proj, v_proj)
    text, send = text_part(place, context, text, w_key, w_value, gain_k, gain_q, send)
    kv, q_own, text_near = join(mine, text, lax.ppermute(send, "core", swap))
    q_far = lax.ppermute(q_own, "yh", swap)
    kv_left = lax.ppermute(kv, "x", x_up)
    kv_right = lax.ppermute(kv, "x", x_down)
    w_mine = w_out.T
    state = attend(place, [q_own], [kv])
    w_source, x_source, state = lax.optimization_barrier((w_mine, x_res.T, state))
    w_send = take_half(place, w_source, 0)
    x_own, x_send = pack(place, x_source, gate_table)
    q_far, state = lax.optimization_barrier((q_far, state))
    state = attend(place, [q_far], [kv], into=state, slot=1)
    way = [(i * 2 + j, (i + 1 - 2 * j) % 4 * 2 + j) for i in range(4) for j in range(2)]
    kv_far = lax.ppermute(pick(place, kv_left, kv_right), ("x", "core"), way)
    *state, text_near = attend(place, [q_own, q_far], [kv_left, kv_right], state, text=text_near)
    sent, text_near = attend(place, [q_own, q_far], [kv_far], state, last=True, text=text_near)

    across = [
        (e * 4 + y * 2 + c, (1 - e) * 4 + (y + c) % 2 * 2 + c) for e in range(2) for y in range(2) for c in range(2)
    ]
    w_send, x_send, q_far = lax.optimization_barrier((w_send, x_send, q_far))
    x_other = lax.ppermute(x_send, "enc", swap)
    w_one = lax.ppermute(w_send, ("enc", "yh", "core"), across)
    parts = lax.all_to_all(sent, ("yh", "core", "enc"), 0, 0, tiled=True)

    q_source, _ = lax.optimization_barrier((w_query, sent))
    q_send = take_half(place, q_source, 1)
    parts, q_send = lax.optimization_barrier((parts, q_send))
    heads = merge(parts)
    heads, w_one, x_other = lax.optimization_barrier((heads, w_one, x_other))
    w_two = lax.ppermute(w_one, "core", swap)
    text_far = lax.ppermute(text_near, "yh", swap)
    q_one = lax.ppermute(q_send, ("enc", "yh", "core"), across)

    weights = (w_mine, w_one, w_two)
    far, acc, _ = ring(heads, functools.partial(mix_near, place, weights))
    mixed = mix_far(place, far, weights, acc, x_own, x_other)

    q_one, text_far, mixed = lax.optimization_barrier((q_one, text_far, mixed))
    q_two = lax.ppermute(q_one, "core", swap)
    mixed_own, mixed_other = mixed
    text_own, key_sums = text_place(place, text_near, text_far, gain_k, gain_q, mixed_other)
    text_other = lax.ppermute(text_own, "enc", swap)
    far, turned, text_own = ring(
        mixed, functools.partial(stream, place, norm_gain.reshape(1, 5120), norm_bias.reshape(1, 5120)), text_own
    )
    raw, sums = query(place, turned, far, w_query, q_one, q_two, key_sums)
    sums = lax.all_to_all(sums, ("enc", "tp"), 0, 0, tiled=True)
    cross_other = cross(place, raw, sums, text_other, True)
    cross_back = lax.ppermute(cross_other, "enc", swap)
    cross_own = cross(place, raw, sums, text_own, False)

    def assemble(own, back, axis):
        return jnp.where(
            e == 0, jnp.concatenate([own, back], axis=axis), jnp.concatenate([back, own], axis=axis)
        )

    return (assemble(mixed_own, text_other[1024:], 1).T, assemble(cross_own, cross_back, 0))


def solution(mesh):
    parts = Mesh(mesh.devices.reshape(2, 4, 2, 2, 8), ("enc", "x", "yh", "core", "tp"))
    seq = ("x", "yh", "core")
    feat = ("enc", "tp")
    placed = (
        P(seq, feat),
        P(seq, feat),
        P(seq, feat),
        P(seq, feat),
        P(None, feat),
        P(None, feat),
        P(),
        P(),
        P(),
        P(None, feat),
        P(("enc", "x", "yh", "core"), None),
        P(None, feat),
        P(None, feat),
        P(feat),
        P(feat),
        P(),
    )
    return jax.shard_map(
        on_device,
        mesh=parts,
        in_specs=placed,
        out_specs=(P(seq, feat), P(seq, feat)),
        check_vma=False,
    )
```
